128 devices in a mesh: seq: 16 (over z_hi, y, core), tp: 8 (over z_lo, x).
Axes of the slice: x: 4, y: 4, z: 4 (z_hi: 2, z_lo: 2; z = z_hi * 2 + z_lo), core: 2. Of those that a mesh axis runs over, the one named last changes fastest.
Arguments:
- inputs: bfloat16 [2048, 4096], P('seq', 'tp'), may hold values from -6 to 6
- target: bfloat16 [2048, 4096], P('seq', 'tp'), may hold values from -6 to 6
- feature_slots: int32 [2048, 16, 8], P(None, 'seq'), may hold values from -1 to 4095, as said below
- w_enc: bfloat16 [65536, 4096], P('seq', 'tp'), may hold values from -0.09375 to 0.09375
- b_enc: float32 [65536], P('seq'), may hold values from -1 to 1
- w_dec: bfloat16 [65536, 4096], P('seq', 'tp'), may hold values from -0.75 to 0.75
- b_dec: float32 [4096], P('tp'), may hold values from -3 to 3
- w_skip: bfloat16 [4096, 4096], P('seq', 'tp'), may hold values from -0.09375 to 0.09375
Outputs:
- reconstruction: bfloat16 [2048, 4096], P('seq', 'tp')
- grad_enc: bfloat16 [65536, 4096], P('seq', 'tp')
- grad_dec: bfloat16 [65536, 4096], P('seq', 'tp')
- grad_benc: float32 [65536], P('seq')
- grad_bdec: float32 [4096], P('tp')
- grad_skip: bfloat16 [4096, 4096], P('seq', 'tp')
The draws below stay inside these ranges and needn't reach their ends.
Inputs may be any that keep to these rules, and one draw needn't show every extreme that they name: feature_slots[t, o, j] is a feature number inside block o of 4096 features, or -1 for an empty slot; each token has exactly 64 live slots naming distinct features, at most 8 in one block, and every token fills all 8 slots of at least one block.
All inputs are finite; a program needn't handle non-finite values.
Results may differ from the reference program's by a relative error of at most 0.0059.
Values may be sent and summed in bfloat16 or wider, within the bound.
A program may use at most 128 MiB of HBM per device.

```python
import jax
import jax.numpy as jnp
from jax import lax

D = 4096
F = 65536
K = 64
SLOT = 8
TOKENS = 2048
N_SEQ = 16


def draw_feature_slots(key, part):
    key_score, key_base, key_stride = jax.random.split(jax.random.fold_in(key, 11), 3)
    slot_width = N_SEQ * SLOT
    position = jnp.arange(slot_width, dtype=jnp.int32)
    owner_of = position // SLOT
    favored = jnp.arange(TOKENS, dtype=jnp.int32) % N_SEQ
    score = jax.random.randint(key_score, (TOKENS, slot_width), 0, 1024)
    score = jnp.where(owner_of[None, :] == favored[:, None], score + 2048, score)
    keyed = score * slot_width + position[None, :]
    order = jnp.argsort(-keyed, axis=1)
    rank = jnp.argsort(order, axis=1)
    live = (rank < K).reshape(TOKENS, N_SEQ, SLOT)
    block_feats = F // N_SEQ
    base = jax.random.randint(key_base, (TOKENS, N_SEQ, 1), 0, block_feats)
    stride = jax.random.randint(key_stride, (TOKENS, N_SEQ, 1), 1, block_feats // SLOT + 1)
    local = (base + jnp.arange(SLOT, dtype=jnp.int32)[None, None, :] * stride) % block_feats
    return jnp.where(live, local, -1).astype(jnp.int32)


def levels(key, shape, cuts, least, top_value):
    loudness, own = 1.0, jax.random.fold_in(key, 6)
    for dim, parts in cuts:
        steps = jnp.exp(jax.random.uniform(jax.random.fold_in(own, dim), (parts,), jnp.float32, least / len(cuts), top_value / len(cuts)))
        loudness = loudness * jnp.repeat(steps, shape[dim] // parts).reshape([-1 if axis == dim else 1 for axis in range(len(shape))])
    return loudness


def normal_values(key, extent, width, bound, cuts=(), kind=jnp.bfloat16):
    drawn = width * jax.random.normal(key, extent, jnp.float32)
    if cuts:
        drawn = drawn * levels(key, extent, cuts, -0.22, 0.18)
    return jnp.clip(drawn, -bound, bound).astype(kind)


def setup_inputs(seed: int = 0) -> dict:
    keys = jax.random.split(jax.random.key(seed), 9)
    inputs = normal_values(keys[0], (TOKENS, D), 1.0, 6.0, ((0, 16), (1, 8)))
    target = normal_values(keys[1], (TOKENS, D), 1.0, 6.0, ((0, 16), (1, 8)))
    feature_slots = draw_feature_slots(jax.random.fold_in(keys[8], 71), 0)
    w_enc = normal_values(keys[3], (F, D), D ** -0.5, 0.09375, ((0, 16), (1, 8)))
    b_enc = jnp.clip(jax.random.uniform(keys[4], (F,), jnp.float32, -1.0, 1.0) * levels(keys[4], (F,), ((0, 16),), -0.4, 0.0), -1.0, 1.0)
    w_dec = normal_values(keys[5], (F, D), K ** -0.5, 0.75, ((0, 16), (1, 8)))
    b_dec = normal_values(keys[6], (D,), 0.5, 3.0, ((0, 8),), jnp.float32)
    w_skip = normal_values(keys[7], (D, D), D ** -0.5, 0.09375, ((0, 16), (1, 8)))
    return dict(inputs=inputs, target=target, feature_slots=feature_slots, w_enc=w_enc, b_enc=b_enc, w_dec=w_dec, b_dec=b_dec, w_skip=w_skip)


def reference(inputs, target, feature_slots, w_enc, b_enc, w_dec, b_dec, w_skip):
    owners = jnp.arange(N_SEQ, dtype=jnp.int32)[None, :, None] * (F // N_SEQ)
    live_mask = feature_slots >= 0
    global_ids = jnp.where(live_mask, feature_slots + owners, 0).astype(jnp.int32).reshape(TOKENS, N_SEQ * SLOT)
    live_float = live_mask.reshape(TOKENS, N_SEQ * SLOT).astype(jnp.float32)
    block_total = TOKENS // 32
    tok_blocks = inputs.reshape(block_total, 32, D)
    id_blocks = global_ids.reshape(block_total, 32, N_SEQ * SLOT)
    start_carry = jnp.zeros((), jnp.float32)

    def encode(carry, item):
        tok_rows, id_rows = item
        weights = w_enc[id_rows].astype(jnp.float32)
        return carry, jnp.einsum("bd,bsd->bs", tok_rows.astype(jnp.float32), weights)

    pre_sum = lax.scan(encode, start_carry, (tok_blocks, id_blocks))[1].reshape(TOKENS, N_SEQ * SLOT)
    preact = pre_sum + b_enc[global_ids]
    active = (jnp.maximum(preact, 0.0) * live_float).astype(jnp.bfloat16)
    act_blocks = active.reshape(block_total, 32, N_SEQ * SLOT)

    def decode(carry, item):
        act_rows, id_rows = item
        weights = w_dec[id_rows].astype(jnp.float32)
        return carry, jnp.einsum("bs,bsd->bd", act_rows.astype(jnp.float32), weights)

    decoded = lax.scan(decode, start_carry, (act_blocks, id_blocks))[1].reshape(TOKENS, D)
    skip_out = jnp.dot(inputs, w_skip, preferred_element_type=jnp.float32)
    predicted = decoded + skip_out + b_dec
    reconstruction = predicted.astype(jnp.bfloat16)
    residual = (predicted - target.astype(jnp.float32)).astype(jnp.bfloat16)
    res_blocks = residual.reshape(block_total, 32, D)

    def backward(carry, item):
        res_rows, id_rows = item
        weights = w_dec[id_rows].astype(jnp.float32)
        return carry, jnp.einsum("bd,bsd->bs", res_rows.astype(jnp.float32), weights)

    back_sum = lax.scan(backward, start_carry, (res_blocks, id_blocks))[1].reshape(TOKENS, N_SEQ * SLOT)
    slope = back_sum * (preact > 0.0).astype(jnp.float32) * live_float
    grad_benc = jnp.zeros((F,), jnp.float32).at[global_ids.reshape(-1)].add(slope.reshape(-1))
    slope_blocks = slope.astype(jnp.bfloat16).reshape(block_total, 32, N_SEQ * SLOT)

    def accumulate(carry, item):
        enc_total, dec_total = carry
        tok_rows, res_rows, id_rows, slope_rows, act_rows = item
        flat_ids = id_rows.reshape(-1)
        enc_terms = slope_rows.astype(jnp.float32)[:, :, None] * tok_rows.astype(jnp.float32)[:, None, :]
        dec_terms = act_rows.astype(jnp.float32)[:, :, None] * res_rows.astype(jnp.float32)[:, None, :]
        enc_total = enc_total.at[flat_ids].add(enc_terms.reshape(-1, D))
        dec_total = dec_total.at[flat_ids].add(dec_terms.reshape(-1, D))
        return (enc_total, dec_total), start_carry

    zero_grads = jnp.zeros((F, D), jnp.float32)
    totals = lax.scan(accumulate, (zero_grads, zero_grads), (tok_blocks, res_blocks, id_blocks, slope_blocks, act_blocks))[0]
    grad_bdec = jnp.sum(residual.astype(jnp.float32), axis=0)
    grad_skip = jnp.dot(inputs.T, residual, preferred_element_type=jnp.float32).astype(jnp.bfloat16)
    return (reconstruction, totals[0].astype(jnp.bfloat16), totals[1].astype(jnp.bfloat16), grad_benc, grad_bdec, grad_skip)
```

```python
import functools

import jax
import jax.numpy as jnp
from jax import lax
from jax.experimental import pallas as pl
from jax.experimental.pallas import tpu as pltpu
from jax.sharding import PartitionSpec as P

MESH = pl.DeviceIdType.MESH
BF16 = jnp.bfloat16
F32 = jnp.float32
VMEM_LIMIT = 56 << 20

N_SEQ = 16
N_TP = 8
ROWS = 128
TOKENS = 2048
COLS = 512
FEATS = 4096
SKIP = 256
SLOTS = 8


class Place:
    def __init__(self):
        self.s = lax.axis_index("seq")
        self.p = lax.axis_index("tp")
        s, p = self.s, self.p
        self.c = lax.rem(s, 2)
        self.y = lax.rem(lax.div(s, 2), 4)
        self.zh = lax.div(s, 8)
        self.x = lax.rem(p, 4)
        self.zl = lax.div(p, 4)
        self.mate = (s + 1 - 2 * self.c, p)
        self.up = (self.seq(0, 1), p)
        self.down = (self.seq(0, 3), p)
        self.far = (self.seq(1, 0), p)
        self.right = (s, self.tp(0, 1))
        self.left = (s, self.tp(0, 3))
        self.side = (s, self.tp(1, 0))

    def seq(self, b, dy, other_core=False):
        zh = 1 - self.zh if b else self.zh
        c = 1 - self.c if other_core else self.c
        return (zh * 4 + lax.rem(self.y + dy, 4)) * 2 + c

    def tp(self, b, dx):
        zl = 1 - self.zl if b else self.zl
        return zl * 4 + lax.rem(self.x + dx, 4)


def greet(devices):
    barrier = pltpu.get_barrier_semaphore()
    for dev in devices:
        pl.semaphore_signal(barrier, inc=1, device_id=dev, device_id_type=MESH)
    pl.semaphore_wait(barrier, len(devices))


class Sender:
    def __init__(self, send, recv, here):
        self.send, self.recv, self.here = send, recv, here
        self.started = []

    def start(self, i, src, dst, dev):
        copy = pltpu.make_async_remote_copy(
            src_ref=src, dst_ref=dst, send_sem=self.send.at[i], recv_sem=self.recv.at[i],
            device_id=dev, device_id_type=MESH,
        )
        copy.start()
        self.started.append(copy)

    def wait(self, i, dst):
        pltpu.make_async_remote_copy(
            src_ref=dst, dst_ref=dst, send_sem=self.send.at[i], recv_sem=self.recv.at[i],
            device_id=self.here, device_id_type=MESH,
        ).wait_recv()

    def drain(self):
        for copy in self.started:
            copy.wait_send()
        self.started = []


SEQ_KINDS = 19


def seq_rows(q, half=None):
    if half is None:
        return pl.ds(pl.multiple_of(q * ROWS, ROWS), ROWS)
    return pl.ds(pl.multiple_of(q * ROWS + half * (ROWS // 2), ROWS // 2), ROWS // 2)


def gather_seq(at, net, own, out):
    def blk(b, dy, half=None, other=False):
        return out.at[seq_rows(at.seq(b, dy, other), half)]

    mine = out.at[seq_rows(at.s)]
    net.start(8, own, mine, at.far)
    net.start(0, own, mine, at.up)
    net.start(1, own, mine, at.down)
    net.start(9, own, mine, at.mate)
    yield
    for b in (0, 1):
        k, m = 4 * b, 9 + 5 * b
        if b:
            net.wait(8, blk(1, 0))
            net.start(4, blk(1, 0), blk(1, 0), at.up)
            net.start(5, blk(1, 0), blk(1, 0), at.down)
            net.start(m, blk(1, 0), blk(1, 0), at.mate)
        net.wait(k, blk(b, 3))
        net.start(k + 2, blk(b, 3, 0), blk(b, 3, 0), at.up)
        net.start(m + 1, blk(b, 3), blk(b, 3), at.mate)
        net.wait(k + 1, blk(b, 1))
        net.start(k + 3, blk(b, 1, 1), blk(b, 1, 1), at.down)
        net.start(m + 2, blk(b, 1), blk(b, 1), at.mate)
        yield
    for b in (0, 1):
        k, m = 4 * b, 9 + 5 * b
        net.wait(k + 2, blk(b, 2, 0))
        net.start(m + 3, blk(b, 2, 0), blk(b, 2, 0), at.mate)
        net.wait(k + 3, blk(b, 2, 1))
        net.start(m + 4, blk(b, 2, 1), blk(b, 2, 1), at.mate)
    yield
    for b in (0, 1):
        m = 9 + 5 * b
        net.wait(m, blk(b, 0, None, True))
        net.wait(m + 1, blk(b, 3, None, True))
        net.wait(m + 2, blk(b, 1, None, True))
        net.wait(m + 3, blk(b, 2, 0, True))
        net.wait(m + 4, blk(b, 2, 1, True))
    yield


def gather_kernel(x_ref, all_ref, skip_ref, send, recv, send2, recv2, local):
    at = Place()
    here = (at.s, at.p)
    half_p = lax.div(at.s, 2)
    stay = half_p == at.p
    around = [at.mate, at.up, at.down, at.far, at.right, at.left, at.side]
    barrier = pltpu.get_barrier_semaphore()
    for dev in around:
        pl.semaphore_signal(barrier, inc=1, device_id=dev, device_id_type=MESH)

    same, cross = (2 * at.p + at.c, half_p), (2 * at.p + 1 - at.c, half_p)
    pl.semaphore_signal(barrier, inc=1, device_id=cross, device_id_type=MESH)

    @pl.when(jnp.logical_not(stay))
    def _():
        pl.semaphore_signal(barrier, inc=1, device_id=same, device_id_type=MESH)

    pl.semaphore_wait(barrier, len(around) + 2 - stay.astype(jnp.int32))

    keep = pltpu.make_async_copy(x_ref, all_ref.at[seq_rows(at.s)], local.at[0])
    keep.start()
    net = Sender(send, recv, here)
    net2 = Sender(send2, recv2, here)
    steps = gather_seq(at, net, x_ref, all_ref)
    next(steps)

    def part(h):
        return x_ref.at[:, pl.ds(pl.multiple_of(h * SKIP, SKIP), SKIP)]

    land = skip_ref.at[seq_rows(at.s)]
    net2.start(1, part(1 - at.c), land, cross)
    from_same = skip_ref.at[seq_rows(2 * at.p + at.c)]
    from_cross = skip_ref.at[seq_rows(2 * at.p + 1 - at.c)]

    @pl.when(jnp.logical_not(stay))
    def _():
        copy = pltpu.make_async_remote_copy(
            src_ref=part(at.c), dst_ref=land, send_sem=send2.at[0], recv_sem=recv2.at[0],
            device_id=same, device_id_type=MESH,
        )
        copy.start()
        copy.wait_send()
        net2.wait(0, from_same)

    @pl.when(stay)
    def _():
        copy = pltpu.make_async_copy(part(at.c), land, local.at[1])
        copy.start()
        copy.wait()

    net2.wait(1, from_cross)

    def piece(b, dx, half=None):
        q = at.tp(b, dx)
        if half is None:
            return skip_ref.at[pl.ds(pl.multiple_of(q * 256, 256), 256)]
        return skip_ref.at[pl.ds(pl.multiple_of(q * 256 + half * 128, 128), 128)]

    net2.start(10, piece(0, 0), piece(0, 0), at.side)
    net2.start(2, piece(0, 0), piece(0, 0), at.right)
    net2.start(3, piece(0, 0), piece(0, 0), at.left)
    next(steps)
    net2.wait(10, piece(1, 0))
    net2.start(6, piece(1, 0), piece(1, 0), at.right)
    net2.start(7, piece(1, 0), piece(1, 0), at.left)
    next(steps)
    for b in (0, 1):
        k = 2 + 4 * b
        net2.wait(k, piece(b, 3))
        net2.start(k + 2, piece(b, 3, 0), piece(b, 3, 0), at.right)
        net2.wait(k + 1, piece(b, 1))
        net2.start(k + 3, piece(b, 1, 1), piece(b, 1, 1), at.left)
    next(steps)
    for b in (0, 1):
        k = 2 + 4 * b
        net2.wait(k + 2, piece(b, 2, 0))
        net2.wait(k + 3, piece(b, 2, 1))
    next(steps)
    keep.wait()
    net.drain()
    net2.drain()


def gather(x):
    return pl.pallas_call(
        gather_kernel,
        out_shape=[
            jax.ShapeDtypeStruct((TOKENS, COLS), BF16),
            jax.ShapeDtypeStruct((TOKENS, SKIP), BF16),
        ],
        in_specs=[pl.BlockSpec(memory_space=pl.ANY)],
        out_specs=[pl.BlockSpec(memory_space=pl.ANY)] * 2,
        scratch_shapes=[
            pltpu.SemaphoreType.DMA((SEQ_KINDS,)),
            pltpu.SemaphoreType.DMA((SEQ_KINDS,)),
            pltpu.SemaphoreType.DMA((11,)),
            pltpu.SemaphoreType.DMA((11,)),
            pltpu.SemaphoreType.DMA((2,)),
        ],
        compiler_params=pltpu.CompilerParams(
            collective_id=0, has_side_effects=True, vmem_limit_bytes=VMEM_LIMIT
        ),
        name="gather_inputs",
    )(x)


def pick_kernel(with_bias, x_ref, id_ref, w_ref, *rest):
    b_ref, o_ref = rest if with_bias else (None, rest[0])
    ids = id_ref[...]
    low = ids & 127
    high = ids >> 7
    width = 1024
    acc = jnp.zeros(ids.shape, F32)
    for c in range(FEATS // width):
        cols = slice(c * width, (c + 1) * width)
        dots = lax.dot_general(
            x_ref[...], w_ref[cols, :], (((1,), (1,)), ((), ())), preferred_element_type=F32
        )
        if with_bias:
            dots = dots + b_ref[:, cols]
        for g in range(width // 128):
            got = jnp.take_along_axis(
                dots[:, g * 128 : (g + 1) * 128], low, axis=1, mode="promise_in_bounds"
            )
            acc = jnp.where(high == c * (width // 128) + g, got, acc)
    for r in range(ids.shape[0] // 128):
        turned = acc[r * 128 : (r + 1) * 128, :].T
        o_ref[:, r * 128 : (r + 1) * 128] = turned[:SLOTS, :]


def pick(name, x, ids, w, bias=None, rows=256):
    specs = [
        pl.BlockSpec((rows, COLS), lambda i: (i, 0)),
        pl.BlockSpec((rows, 128), lambda i: (i, 0)),
        pl.BlockSpec((FEATS, COLS), lambda i: (0, 0)),
    ]
    args = [x, ids, w]
    if bias is not None:
        specs.append(pl.BlockSpec((1, FEATS), lambda i: (0, 0)))
        args.append(bias)
    return pl.pallas_call(
        functools.partial(pick_kernel, bias is not None),
        grid=(TOKENS // rows,),
        in_specs=specs,
        out_specs=pl.BlockSpec((SLOTS, rows), lambda i: (0, i)),
        out_shape=jax.ShapeDtypeStruct((SLOTS, TOKENS), F32),
        compiler_params=pltpu.CompilerParams(vmem_limit_bytes=VMEM_LIMIT),
        name=name,
    )(*args)


def sum_kernel(x_ref, o_ref, parts, send, recv, send2, recv2):
    at = Place()
    width = TOKENS // N_TP
    here = (at.s, at.p)
    peers = [(at.s, lax.rem(at.p + d, N_TP)) for d in range(1, N_TP)]
    greet(peers)

    def lanes(q):
        return pl.ds(pl.multiple_of(q * width, width), width)

    net = Sender(send, recv, here)
    for d in range(1, N_TP):
        net.start(d, x_ref.at[:, lanes(peers[d - 1][1])], parts.at[d], peers[d - 1])
    total = x_ref[:, lanes(at.p)]
    for d in range(1, N_TP):
        net.wait(d, parts.at[d])
        total = total + parts[d]
    o_ref[:, lanes(at.p)] = total
    net2 = Sender(send2, recv2, here)
    for d in range(1, N_TP):
        net2.start(d, o_ref.at[:, lanes(at.p)], o_ref.at[:, lanes(at.p)], peers[d - 1])
    for d in range(1, N_TP):
        net2.wait(d, o_ref.at[:, lanes(lax.rem(at.p + N_TP - d, N_TP))])
    net.drain()
    net2.drain()


def sum_tp(x, number, name):
    return pl.pallas_call(
        sum_kernel,
        out_shape=jax.ShapeDtypeStruct((SLOTS, TOKENS), F32),
        in_specs=[pl.BlockSpec(memory_space=pltpu.VMEM)],
        out_specs=pl.BlockSpec(memory_space=pltpu.VMEM),
        scratch_shapes=[pltpu.VMEM((N_TP, SLOTS, TOKENS // N_TP), F32)]
        + [pltpu.SemaphoreType.DMA((N_TP,))] * 4,
        compiler_params=pltpu.CompilerParams(
            collective_id=number, has_side_effects=True, vmem_limit_bytes=VMEM_LIMIT
        ),
        name=name,
    )(x)


def decode_kernel(key_ref, pre_ref, base_ref, w_ref, xs_ref, ws_ref, o_ref, a_ref):
    rows = key_ref.shape[0]
    filler = jnp.zeros((128 - SLOTS, 128), F32)
    for t in range(rows // 128):
        act = jnp.maximum(pre_ref[:, t * 128 : (t + 1) * 128], 0.0)
        act = jnp.concatenate([act, filler], axis=0).T
        for r in range(8):
            line = slice(t * 128 + r * 16, t * 128 + (r + 1) * 16)
            key = key_ref[line, :]
            val = act[r * 16 : (r + 1) * 16, :]
            keys, vals = [], []
            for j in range(SLOTS):
                keys.append(jnp.broadcast_to(key[:, j : j + 1], (16, 128)).astype(BF16))
                vals.append(jnp.broadcast_to(val[:, j : j + 1], (16, 128)).astype(BF16))
            for g in range(FEATS // 128):
                base = base_ref[:, g * 128 : (g + 1) * 128]
                acc = jnp.zeros((16, 128), BF16)
                for j in range(SLOTS):
                    acc = jnp.where(keys[j] == base, vals[j], acc)
                a_ref[line, g * 128 : (g + 1) * 128] = acc
    o_ref[...] = jnp.dot(a_ref[...], w_ref[...], preferred_element_type=F32) + jnp.dot(
        xs_ref[...], ws_ref[...], preferred_element_type=F32
    )


def decode(key, pre, base, w, xs, ws, rows=256):
    return pl.pallas_call(
        decode_kernel,
        grid=(TOKENS // rows,),
        in_specs=[
            pl.BlockSpec((rows, SLOTS), lambda i: (i, 0)),
            pl.BlockSpec((SLOTS, rows), lambda i: (0, i)),
            pl.BlockSpec((16, FEATS), lambda i: (0, 0)),
            pl.BlockSpec((FEATS, COLS), lambda i: (0, 0)),
            pl.BlockSpec((rows, SKIP), lambda i: (i, 0)),
            pl.BlockSpec((SKIP, COLS), lambda i: (0, 0)),
        ],
        out_specs=pl.BlockSpec((rows, COLS), lambda i: (i, 0)),
        out_shape=jax.ShapeDtypeStruct((TOKENS, COLS), F32),
        scratch_shapes=[pltpu.VMEM((rows, FEATS), BF16)],
        compiler_params=pltpu.CompilerParams(vmem_limit_bytes=VMEM_LIMIT),
        name="decode",
    )(key, pre, base, w, xs, ws)


def residual_kernel(
    part, target, bias, recon, all_ref, mrecv, out_buf, half_in, full_in, far_out, far_in, res,
    msend, mrcv, ysend, yrcv, send, recv, local,
):
    at = Place()
    here = (at.s, at.p)
    greet([at.mate, at.up, at.down, at.far])
    mnet = Sender(msend, mrcv, here)
    ynet = Sender(ysend, yrcv, here)
    order = [(b, dy) for b in (1, 0) for dy in (2, 1, 3, 0)]
    for k, (b, dy) in enumerate(order):
        mnet.start(k, part.at[seq_rows(at.seq(b, dy, True))], mrecv.at[k], at.mate)
    H = ROWS // 2

    def pair(k, half=None):
        b, dy = order[k]
        rows = seq_rows(at.seq(b, dy), half)
        mine = slice(0, ROWS) if half is None else slice(half * H, (half + 1) * H)
        return part[rows, :] + mrecv[k, mine, :]

    for i, b in enumerate((1, 0)):
        k = 4 * i
        mnet.wait(k, mrecv.at[k])
        out_buf[3 * i] = pair(k).astype(BF16)
        ynet.start(4 * i, out_buf.at[3 * i, pl.ds(0, H)], half_in.at[2 * i], at.up)
        ynet.start(4 * i + 1, out_buf.at[3 * i, pl.ds(H, H)], half_in.at[2 * i + 1], at.down)
    for i, b in enumerate((1, 0)):
        k = 4 * i
        mnet.wait(k + 1, mrecv.at[k + 1])
        out_buf[3 * i + 1, H:, :] = pair(k + 1, 1).astype(BF16)
        ynet.wait(4 * i, half_in.at[2 * i])
        out_buf[3 * i + 1, :H, :] = (pair(k + 1, 0) + half_in[2 * i].astype(F32)).astype(BF16)
        ynet.start(4 * i + 2, out_buf.at[3 * i + 1], full_in.at[2 * i], at.up)
        mnet.wait(k + 2, mrecv.at[k + 2])
        out_buf[3 * i + 2, :H, :] = pair(k + 2, 0).astype(BF16)
        ynet.wait(4 * i + 1, half_in.at[2 * i + 1])
        out_buf[3 * i + 2, H:, :] = (pair(k + 2, 1) + half_in[2 * i + 1].astype(F32)).astype(BF16)
        ynet.start(4 * i + 3, out_buf.at[3 * i + 2], full_in.at[2 * i + 1], at.down)
    mnet.wait(3, mrecv.at[3])
    total = pair(3)
    ynet.wait(2, full_in.at[0])
    ynet.wait(3, full_in.at[1])
    far_out[...] = total + full_in[0].astype(F32) + full_in[1].astype(F32)
    ynet.start(8, far_out, far_in, at.far)
    mnet.wait(7, mrecv.at[7])
    total = pair(7)
    ynet.wait(6, full_in.at[2])
    ynet.wait(7, full_in.at[3])
    total = total + full_in[2].astype(F32) + full_in[3].astype(F32) + bias[...]
    ynet.wait(8, far_in)
    total = total + far_in[...]
    recon[...] = total.astype(BF16)
    res[...] = (total - target[...].astype(F32)).astype(BF16)
    keep = pltpu.make_async_copy(res, all_ref.at[seq_rows(at.s)], local.at[0])
    keep.start()
    net = Sender(send, recv, here)
    for _ in gather_seq(at, net, res, all_ref):
        pass
    keep.wait()
    mnet.drain()
    ynet.drain()
    net.drain()


def residuals(part, target, bias):
    vm = pl.BlockSpec(memory_space=pltpu.VMEM)
    dma = pltpu.SemaphoreType.DMA
    return pl.pallas_call(
        residual_kernel,
        out_shape=[
            jax.ShapeDtypeStruct((ROWS, COLS), BF16),
            jax.ShapeDtypeStruct((TOKENS, COLS), BF16),
        ],
        in_specs=[vm, vm, vm],
        out_specs=[vm, pl.BlockSpec(memory_space=pl.ANY)],
        scratch_shapes=[
            pltpu.VMEM((8, ROWS, COLS), F32),
            pltpu.VMEM((6, ROWS, COLS), BF16),
            pltpu.VMEM((4, ROWS // 2, COLS), BF16),
            pltpu.VMEM((4, ROWS, COLS), BF16),
            pltpu.VMEM((ROWS, COLS), F32),
            pltpu.VMEM((ROWS, COLS), F32),
            pltpu.VMEM((ROWS, COLS), BF16),
            dma((8,)), dma((8,)), dma((9,)), dma((9,)),
            dma((SEQ_KINDS,)), dma((SEQ_KINDS,)), dma((1,)),
        ],
        compiler_params=pltpu.CompilerParams(
            collective_id=2, has_side_effects=True, vmem_limit_bytes=VMEM_LIMIT
        ),
        name="residuals",
    )(part, target, bias)


def grad_kernel(
    key_ref, pre_ref, back_ref, base_ref, x_ref, r_ref, ge_ref, gd_ref, st_ref, at_ref
):
    feats = base_ref.shape[0]
    for t in range(TOKENS // 128):
        lanes = slice(t * 128, (t + 1) * 128)
        pre = pre_ref[:, lanes]
        slope = jnp.where(pre > 0.0, back_ref[:, lanes], 0.0)
        act = jnp.maximum(pre, 0.0)
        key = key_ref[:, lanes]
        keys, slopes, acts = [], [], []
        for j in range(SLOTS):
            row = slice(j, j + 1)
            keys.append(jnp.broadcast_to(key[row, :], (16, 128)).astype(BF16))
            slopes.append(jnp.broadcast_to(slope[row, :], (16, 128)).astype(BF16))
            acts.append(jnp.broadcast_to(act[row, :], (16, 128)).astype(BF16))
        for r in range(feats // 16):
            lines = slice(r * 16, (r + 1) * 16)
            base = base_ref[lines, :]
            s_acc = jnp.zeros((16, 128), BF16)
            a_acc = jnp.zeros((16, 128), BF16)
            for j in range(SLOTS):
                hit = keys[j] == base
                s_acc = jnp.where(hit, slopes[j], s_acc)
                a_acc = jnp.where(hit, acts[j], a_acc)
            st_ref[lines, lanes] = s_acc
            at_ref[lines, lanes] = a_acc
    ge_ref[...] = jnp.dot(st_ref[...], x_ref[...], preferred_element_type=F32).astype(BF16)
    gd_ref[...] = jnp.dot(at_ref[...], r_ref[...], preferred_element_type=F32).astype(BF16)


def grads(key, pre, back, base, x, r, feats=512):
    slots = pl.BlockSpec((SLOTS, TOKENS), lambda i: (0, 0))
    whole = pl.BlockSpec((TOKENS, COLS), lambda i: (0, 0))
    out = pl.BlockSpec((feats, COLS), lambda i: (i, 0))
    return pl.pallas_call(
        grad_kernel,
        grid=(FEATS // feats,),
        in_specs=[slots, slots, slots, pl.BlockSpec((feats, 128), lambda i: (i, 0)), whole, whole],
        out_specs=[out, out],
        out_shape=[jax.ShapeDtypeStruct((FEATS, COLS), BF16)] * 2,
        scratch_shapes=[pltpu.VMEM((feats, TOKENS), BF16)] * 2,
        compiler_params=pltpu.CompilerParams(vmem_limit_bytes=VMEM_LIMIT),
        name="grads",
    )(key, pre, back, base, x, r)


def small_kernel(id_ref, pre_ref, back_ref, xs_ref, r_ref, gb_ref, gs_ref, bd_ref):
    total = jnp.zeros((FEATS // 128, 128), F32)
    contract = (((0,), (0,)), ((), ()))
    pairs = (((1,), (1,)), ((), ()))
    for t in range(TOKENS // 512):
        lanes = slice(t * 512, (t + 1) * 512)
        ids = id_ref[:, lanes]
        high, low = ids >> 7, ids & 127
        slope = jnp.where(pre_ref[:, lanes] > 0.0, back_ref[:, lanes], 0.0)
        top = slope.astype(BF16).astype(F32)
        rest = slope - top
        rest_top = rest.astype(BF16).astype(F32)
        last = rest - rest_top
        lines = lax.broadcasted_iota(jnp.int32, (FEATS // 128, 512), 0)
        lanes128 = lax.broadcasted_iota(jnp.int32, (128, 512), 0)
        for j in range(SLOTS):
            row = slice(j, j + 1)
            one = jnp.where(high[row, :] == lines, 1.0, 0.0).astype(BF16)
            hit = low[row, :] == lanes128
            for value in (top, rest_top, last):
                table = jnp.where(hit, value[row, :], 0.0).astype(BF16)
                total += lax.dot_general(one, table, pairs, preferred_element_type=F32)
    gb_ref[...] = total
    gs_ref[...] = lax.dot_general(
        xs_ref[...], r_ref[...], contract, preferred_element_type=F32
    ).astype(BF16)
    bd_ref[...] = jnp.dot(jnp.ones((8, TOKENS), BF16), r_ref[...], preferred_element_type=F32)


def small_grads(ids, pre, back, xs, r):
    return pl.pallas_call(
        small_kernel,
        in_specs=[pl.BlockSpec(memory_space=pltpu.VMEM)] * 5,
        out_specs=[pl.BlockSpec(memory_space=pltpu.VMEM)] * 3,
        out_shape=[
            jax.ShapeDtypeStruct((FEATS // 128, 128), F32),
            jax.ShapeDtypeStruct((SKIP, COLS), BF16),
            jax.ShapeDtypeStruct((8, COLS), F32),
        ],
        compiler_params=pltpu.CompilerParams(vmem_limit_bytes=VMEM_LIMIT),
        name="small_grads",
    )(ids, pre, back, xs, r)


def shards(inputs, target, feature_slots, w_enc, b_enc, w_dec, b_dec, w_skip):
    ids = feature_slots[:, 0, :]
    ids_t = ids.T
    tiled = jnp.tile(jnp.maximum(ids, 0), (1, 128 // SLOTS))

    def key_of(number):
        high = jnp.left_shift(jnp.uint32(1), (number >> 7).astype(jnp.uint32)).astype(F32)
        return (128 + (number & 127)).astype(F32) * high

    key = jnp.where(ids >= 0, key_of(jnp.maximum(ids, 0)), -1.0)
    key_t = jnp.where(ids_t >= 0, key_of(jnp.maximum(ids_t, 0)), -1.0)
    base = key_of(jnp.arange(FEATS, dtype=jnp.int32)).astype(BF16)
    base_row = jnp.broadcast_to(base[None, :], (16, FEATS))
    base_col = jnp.broadcast_to(base[:, None], (FEATS, 128))
    bias = jnp.where(lax.axis_index("tp") == 0, b_enc, 0.0)[None, :]

    all_x, x_skip = gather(inputs)
    pre = sum_tp(pick("encode", all_x, tiled, w_enc, bias), 1, "sum_pre")
    part = decode(key, pre, base_row, w_dec, x_skip, w_skip)
    recon, all_r = residuals(part, target, b_dec[None, :])
    back = sum_tp(pick("backward", all_r, tiled, w_dec), 1, "sum_back")
    grad_enc, grad_dec = grads(key_t, pre, back, base_col, all_x, all_r)
    grad_benc, grad_skip, grad_bdec = small_grads(ids_t, pre, back, x_skip, all_r)
    return recon, grad_enc, grad_dec, grad_benc.reshape(-1), grad_bdec[0], grad_skip


def solution(mesh):
    in_specs = (
        P("seq", "tp"),
        P("seq", "tp"),
        P(None, "seq", None),
        P("seq", "tp"),
        P("seq"),
        P("seq", "tp"),
        P("tp"),
        P("seq", "tp"),
    )
    out_specs = (P("seq", "tp"), P("seq", "tp"), P("seq", "tp"), P("seq"), P("tp"), P("seq", "tp"))
    return jax.shard_map(shards, mesh=mesh, in_specs=in_specs, out_specs=out_specs, check_vma=False)
```

```python
import functools

import jax
import jax.numpy as jnp
from jax import lax
from jax.experimental import pallas as pl
from jax.experimental.pallas import tpu as pltpu
from jax.sharding import PartitionSpec as P

MESH = pl.DeviceIdType.MESH
BF16 = jnp.bfloat16
F32 = jnp.float32
VMEM_LIMIT = 56 << 20

N_SEQ = 16
N_TP = 8
ROWS = 128
TOKENS = 2048
COLS = 512
FEATS = 4096
SKIP = 256
SLOTS = 8


class Place:
    def __init__(self):
        self.s = lax.axis_index("seq")
        self.p = lax.axis_index("tp")
        s, p = self.s, self.p
        self.c = lax.rem(s, 2)
        self.y = lax.rem(lax.div(s, 2), 4)
        self.zh = lax.div(s, 8)
        self.x = lax.rem(p, 4)
        self.zl = lax.div(p, 4)
        self.mate = (s + 1 - 2 * self.c, p)
        self.up = (self.seq(0, 1), p)
        self.down = (self.seq(0, 3), p)
        self.far = (self.seq(1, 0), p)
        self.right = (s, self.tp(0, 1))
        self.left = (s, self.tp(0, 3))
        self.side = (s, self.tp(1, 0))

    def seq(self, b, dy, other_core=False):
        zh = 1 - self.zh if b else self.zh
        c = 1 - self.c if other_core else self.c
        return (zh * 4 + lax.rem(self.y + dy, 4)) * 2 + c

    def tp(self, b, dx):
        zl = 1 - self.zl if b else self.zl
        return zl * 4 + lax.rem(self.x + dx, 4)


def greet(devices):
    barrier = pltpu.get_barrier_semaphore()
    for dev in devices:
        pl.semaphore_signal(barrier, inc=1, device_id=dev, device_id_type=MESH)
    pl.semaphore_wait(barrier, len(devices))


class Sender:
    def __init__(self, send, recv, here):
        self.send, self.recv, self.here = send, recv, here

    def copy(self, i, src, dst, dev):
        return pltpu.make_async_remote_copy(
            src_ref=src, dst_ref=dst, send_sem=self.send.at[i], recv_sem=self.recv.at[i],
            device_id=dev, device_id_type=MESH,
        )

    def start(self, i, src, dst, dev):
        self.copy(i, src, dst, dev).start()

    def wait(self, i, dst):
        self.copy(i, dst, dst, self.here).wait_recv()

    def sent(self, i, like):
        self.copy(i, like, like, self.here).wait_send()


def choose(k, values):
    out = values[0]
    for i, v in enumerate(values[1:], 1):
        out = jnp.where(k == i, v, out)
    return out


def seq_rows(q, half=None):
    if half is None:
        return pl.ds(pl.multiple_of(q * ROWS, ROWS), ROWS)
    return pl.ds(pl.multiple_of(q * ROWS + half * (ROWS // 2), ROWS // 2), ROWS // 2)


def key_of(number):
    value = (128 + (number & 127)).astype(F32)
    for bit in range(5):
        value = value * jnp.where((number & (128 << bit)) != 0, float(2 ** (2**bit)), 1.0)
    return value


PAIR = 2 * ROWS
PICK_ORDER = ((0, 0), (0, 3), (0, 1), (1, 0), (0, 2), (1, 3), (1, 1), (1, 2))
SEQ_KINDS = 19
HALVES = (2, 3, 6, 7, 12, 13, 17, 18)


def pick_slots(rows, w_ref, ids, bias):
    width = 256
    accs = [jnp.zeros((8, PAIR), F32) for _ in range(SLOTS)]
    for c in range(FEATS // width):
        lines = slice(c * width, (c + 1) * width)
        dots = lax.dot_general(
            w_ref[lines, :], rows, (((1,), (1,)), ((), ())), preferred_element_type=F32
        )
        if bias is not None:
            dots = dots + jnp.concatenate([bias[lines, :]] * 2, axis=1)
        for j in range(SLOTS):
            row = ids[j : j + 1, :]
            tree = dots
            for bit in range(4, -1, -1):
                half = tree.shape[0] // 2
                upper = jnp.broadcast_to((row & (8 << bit)) != 0, (half, PAIR))
                tree = jnp.where(upper, tree[half:], tree[:half])
            here = jnp.broadcast_to((row >> 8) == c, (8, PAIR))
            accs[j] = jnp.where(here, tree, accs[j])
    line = lax.broadcasted_iota(jnp.int32, (8, PAIR), 0)
    out = []
    for j in range(SLOTS):
        hit = line == (ids[j : j + 1, :] & 7)
        out.append(jnp.sum(jnp.where(hit, accs[j], 0.0), axis=0, keepdims=True))
    return jnp.concatenate(out, axis=0)


def gather_and_pick(at, net, pnet, own, rows_ref, w_ref, id_ref, bias, parts, out_ref, keep, extra):
    def blk(b, dy, half=None, other=False):
        return rows_ref.at[seq_rows(at.seq(b, dy, other), half)]

    mine = rows_ref.at[seq_rows(at.s)]
    net.start(9, own, mine, at.mate)
    net.start(8, own, mine, at.far)
    net.start(0, own, mine, at.up)
    net.start(1, own, mine, at.down)
    extra(0)
    keep()
    net.wait(9, blk(0, 0, None, True))

    def ring(b):
        k, m = 4 * b, 9 + 5 * b
        net.wait(k, blk(b, 3))
        net.start(k + 2, blk(b, 3, 0), blk(b, 3, 0), at.up)
        net.start(m + 1, blk(b, 3), blk(b, 3), at.mate)
        net.wait(k + 1, blk(b, 1))
        net.start(k + 3, blk(b, 1, 1), blk(b, 1, 1), at.down)
        net.start(m + 2, blk(b, 1), blk(b, 1), at.mate)

    def last(b):
        k, m = 4 * b, 9 + 5 * b
        net.wait(k + 2, blk(b, 2, 0))
        net.start(m + 3, blk(b, 2, 0), blk(b, 2, 0), at.mate)
        net.wait(k + 3, blk(b, 2, 1))
        net.start(m + 4, blk(b, 2, 1), blk(b, 2, 1), at.mate)

    def step(i):
        if i == 1:
            ring(0)
            net.wait(8, blk(1, 0))
            net.start(4, blk(1, 0), blk(1, 0), at.up)
            net.start(5, blk(1, 0), blk(1, 0), at.down)
            net.start(14, blk(1, 0), blk(1, 0), at.mate)
            net.wait(10, blk(0, 3, None, True))
        if i == 2:
            net.wait(11, blk(0, 1, None, True))
        if i == 3:
            ring(1)
            last(0)
            net.wait(14, blk(1, 0, None, True))
        if i == 4:
            net.wait(12, blk(0, 2, 0, True))
            net.wait(13, blk(0, 2, 1, True))
        if i == 5:
            last(1)
            net.wait(15, blk(1, 3, None, True))
        if i == 6:
            net.wait(16, blk(1, 1, None, True))
        if i == 7:
            net.wait(17, blk(1, 2, 0, True))
            net.wait(18, blk(1, 2, 1, True))
        extra(i)

    def pair_of(k):
        return choose(k, [lax.div(at.seq(b, dy), 2) for b, dy in PICK_ORDER])

    def lanes(k):
        return pl.ds(pl.multiple_of(pair_of(k) * PAIR, PAIR), PAIR)

    def body(k, carry):
        for i in range(1, 8):
            pl.when(k == i)(functools.partial(step, i))
        q = pair_of(k)
        rows = rows_ref[pl.ds(pl.multiple_of(q * PAIR, PAIR), PAIR), :]
        parts[k, at.p] = pick_slots(rows, w_ref, id_ref[:, lanes(k)], bias)
        for d in range(1, N_TP):
            here = parts.at[k, at.p]
            pnet.start((k, d), here, here, (at.s, lax.rem(at.p + d, N_TP)))
        return carry

    lax.fori_loop(0, 8, body, 0)
    extra(8)

    def add_up(k, carry):
        for d in range(1, N_TP):
            pnet.wait((k, d), parts.at[k, lax.rem(at.p + N_TP - d, N_TP)])
        total = parts[k, 0]
        for q in range(1, N_TP):
            total = total + parts[k, q]
        out_ref[:, lanes(k)] = total
        return carry

    lax.fori_loop(0, 8, add_up, 0)
    for i in range(SEQ_KINDS):
        net.sent(i, rows_ref.at[pl.ds(0, ROWS // 2 if i in HALVES else ROWS)])

    def done(k, carry):
        for d in range(1, N_TP):
            pnet.sent((k, d), parts.at[k, at.p])
        return carry

    lax.fori_loop(0, 8, done, 0)


def encode_kernel(
    x_ref, id_ref, w_hbm, b_ref, all_ref, skip_ref, pre_ref, w_ref, bias, parts,
    send, recv, psend, precv, send2, recv2, local,
):
    at = Place()
    here = (at.s, at.p)
    load = pltpu.make_async_copy(w_hbm, w_ref, local.at[0])
    load.start()
    own = pltpu.make_async_copy(x_ref, all_ref.at[seq_rows(at.s)], local.at[1])
    own.start()

    half_p = lax.div(at.s, 2)
    stay = half_p == at.p
    peers = [(at.s, lax.rem(at.p + d, N_TP)) for d in range(1, N_TP)]
    same, cross = (2 * at.p + at.c, half_p), (2 * at.p + 1 - at.c, half_p)
    around = [at.mate, at.up, at.down, at.far, cross] + peers
    barrier = pltpu.get_barrier_semaphore()
    for dev in around:
        pl.semaphore_signal(barrier, inc=1, device_id=dev, device_id_type=MESH)

    @pl.when(jnp.logical_not(stay))
    def _():
        pl.semaphore_signal(barrier, inc=1, device_id=same, device_id_type=MESH)

    first = lax.axis_index("tp") == 0
    for g in range(FEATS // 128):
        row = jnp.where(first, b_ref[g : g + 1, :], 0.0)
        bias[g * 128 : (g + 1) * 128, :] = jnp.broadcast_to(row, (128, 128)).T
    pl.semaphore_wait(barrier, len(around) + 1 - stay.astype(jnp.int32))

    net, pnet, net2 = Sender(send, recv, here), Sender2(psend, precv, here), Sender(send2, recv2, here)

    def part(h):
        return x_ref.at[:, pl.ds(pl.multiple_of(h * SKIP, SKIP), SKIP)]

    land = skip_ref.at[seq_rows(at.s)]
    inside = pltpu.make_async_copy(part(at.c), land, local.at[2])

    def piece(b, dx, half=None):
        q = at.tp(b, dx)
        if half is None:
            return skip_ref.at[pl.ds(pl.multiple_of(q * 256, 256), 256)]
        return skip_ref.at[pl.ds(pl.multiple_of(q * 256 + half * 128, 128), 128)]

    def ring(b):
        k = 2 + 4 * b
        net2.wait(k, piece(b, 3))
        net2.start(k + 2, piece(b, 3, 0), piece(b, 3, 0), at.right)
        net2.wait(k + 1, piece(b, 1))
        net2.start(k + 3, piece(b, 1, 1), piece(b, 1, 1), at.left)

    def extra(i):
        if i == 0:
            net2.start(1, part(1 - at.c), land, cross)

            @pl.when(jnp.logical_not(stay))
            def _():
                net2.start(0, part(at.c), land, same)

            @pl.when(stay)
            def _():
                inside.start()

        if i == 1:
            net2.wait(1, skip_ref.at[seq_rows(2 * at.p + 1 - at.c)])

            @pl.when(jnp.logical_not(stay))
            def _():
                net2.wait(0, skip_ref.at[seq_rows(2 * at.p + at.c)])

            @pl.when(stay)
            def _():
                pltpu.make_async_copy(part(at.c), land, local.at[2]).wait()

            net2.start(10, piece(0, 0), piece(0, 0), at.side)
            net2.start(2, piece(0, 0), piece(0, 0), at.right)
            net2.start(3, piece(0, 0), piece(0, 0), at.left)
        if i == 3:
            net2.wait(10, piece(1, 0))
            net2.start(6, piece(1, 0), piece(1, 0), at.right)
            net2.start(7, piece(1, 0), piece(1, 0), at.left)
            ring(0)
        if i == 5:
            ring(1)
        if i == 8:
            for b in (0, 1):
                net2.wait(4 + 4 * b, piece(b, 2, 0))
                net2.wait(5 + 4 * b, piece(b, 2, 1))

    def keep():
        load.wait()
        own.wait()

    gather_and_pick(at, net, pnet, x_ref, all_ref, w_ref, id_ref, bias, parts, pre_ref, keep, extra)

    @pl.when(jnp.logical_not(stay))
    def _():
        net2.sent(0, land)

    net2.sent(1, land)
    for i in range(2, 11):
        net2.sent(i, skip_ref.at[pl.ds(0, 128 if i in (4, 5, 8, 9) else 256)])


class Sender2(Sender):
    def copy(self, i, src, dst, dev):
        return pltpu.make_async_remote_copy(
            src_ref=src, dst_ref=dst, send_sem=self.send.at[i[0], i[1]],
            recv_sem=self.recv.at[i[0], i[1]], device_id=dev, device_id_type=MESH,
        )


def encode(x, ids, w, bias):
    vm = pl.BlockSpec(memory_space=pltpu.VMEM)
    hbm = pl.BlockSpec(memory_space=pl.ANY)
    dma = pltpu.SemaphoreType.DMA
    return pl.pallas_call(
        encode_kernel,
        out_shape=[
            jax.ShapeDtypeStruct((TOKENS, COLS), BF16),
            jax.ShapeDtypeStruct((TOKENS, SKIP), BF16),
            jax.ShapeDtypeStruct((SLOTS, TOKENS), F32),
        ],
        in_specs=[hbm, vm, hbm, vm],
        out_specs=[vm, vm, vm],
        scratch_shapes=[
            pltpu.VMEM((FEATS, COLS), BF16),
            pltpu.VMEM((FEATS, 128), F32),
            pltpu.VMEM((8, N_TP, SLOTS, PAIR), F32),
            dma((SEQ_KINDS,)), dma((SEQ_KINDS,)), dma((8, N_TP)), dma((8, N_TP)),
            dma((11,)), dma((11,)), dma((3,)),
        ],
        compiler_params=pltpu.CompilerParams(
            collective_id=0, has_side_effects=True, vmem_limit_bytes=VMEM_LIMIT
        ),
        name="encode",
    )(x, ids, w, bias)


SUM_ORDER = tuple((b, dy) for b in (1, 0) for dy in (2, 1, 3, 0))
SLAB = 32


def residual_kernel(
    pre_ref, id_ref, w_hbm, xs_ref, ws_ref, target, bias, recon, all_ref, back_ref,
    w_ref, base, table, turned, part, mrecv, out_buf, half_in, full_in, far_out, far_in, res, parts,
    msend, mrcv, ysend, yrcv, send, recv, psend, precv, local,
):
    at = Place()
    here = (at.s, at.p)
    load = pltpu.make_async_copy(w_hbm, w_ref, local.at[0])
    load.start()
    peers = [(at.s, lax.rem(at.p + d, N_TP)) for d in range(1, N_TP)]
    around = [at.mate, at.up, at.down, at.far] + peers
    barrier = pltpu.get_barrier_semaphore()
    for dev in around:
        pl.semaphore_signal(barrier, inc=1, device_id=dev, device_id_type=MESH)
    base[...] = key_of(lax.broadcasted_iota(jnp.int32, (SLAB, FEATS), 1)).astype(BF16)
    pl.semaphore_wait(barrier, len(around))
    load.wait()

    mnet, ynet = Sender(msend, mrcv, here), Sender(ysend, yrcv, here)
    H = ROWS // 2

    def pair(k, half=None):
        b, dy = SUM_ORDER[k]
        rows = seq_rows(at.seq(b, dy), half)
        mine = slice(0, ROWS) if half is None else slice(half * H, (half + 1) * H)
        return part[rows, :] + mrecv[k, mine, :]

    def opposite(i):
        mnet.wait(4 * i, mrecv.at[4 * i])
        out_buf[3 * i] = pair(4 * i).astype(BF16)
        ynet.start(4 * i, out_buf.at[3 * i, pl.ds(0, H)], half_in.at[2 * i], at.up)
        ynet.start(4 * i + 1, out_buf.at[3 * i, pl.ds(H, H)], half_in.at[2 * i + 1], at.down)

    def upward(i):
        k = 4 * i + 1
        mnet.wait(k, mrecv.at[k])
        out_buf[3 * i + 1, H:, :] = pair(k, 1).astype(BF16)
        ynet.wait(4 * i, half_in.at[2 * i])
        out_buf[3 * i + 1, :H, :] = (pair(k, 0) + half_in[2 * i].astype(F32)).astype(BF16)
        ynet.start(4 * i + 2, out_buf.at[3 * i + 1], full_in.at[2 * i], at.up)

    def downward(i):
        k = 4 * i + 2
        mnet.wait(k, mrecv.at[k])
        out_buf[3 * i + 2, :H, :] = pair(k, 0).astype(BF16)
        ynet.wait(4 * i + 1, half_in.at[2 * i + 1])
        out_buf[3 * i + 2, H:, :] = (pair(k, 1) + half_in[2 * i + 1].astype(F32)).astype(BF16)
        ynet.start(4 * i + 3, out_buf.at[3 * i + 2], full_in.at[2 * i + 1], at.down)

    def here_sum(i):
        k = 4 * i + 3
        mnet.wait(k, mrecv.at[k])
        ynet.wait(4 * i + 2, full_in.at[2 * i])
        ynet.wait(4 * i + 3, full_in.at[2 * i + 1])
        return pair(k) + full_in[2 * i].astype(F32) + full_in[2 * i + 1].astype(F32)

    def step(i):
        if i == 1:
            opposite(0)
        if i == 2:
            upward(0)
        if i == 3:
            downward(0)
        if i == 5:
            opposite(1)
            far_out[...] = here_sum(0)
            ynet.start(8, far_out, far_in, at.far)
        if i == 6:
            upward(1)
        if i == 7:
            downward(1)

    filler = jnp.zeros((128 - 2 * SLOTS, 128), F32)

    def body(k, carry):
        q = choose(k, [lax.div(at.seq(b, dy), 2) for b, dy in SUM_ORDER])
        first = pl.multiple_of(q * PAIR, PAIR)
        for t in range(2):
            lanes = pl.ds(pl.multiple_of(first + t * 128, 128), 128)
            ids = id_ref[:, lanes]
            act = jnp.maximum(pre_ref[:, lanes], 0.0)
            key = jnp.where(ids >= 0, key_of(ids), -1.0)
            turned[t * 128 : (t + 1) * 128, :] = jnp.concatenate([act, key, filler], axis=0).T

        def slab(r, carry2):
            line = pl.ds(pl.multiple_of(r * SLAB, SLAB), SLAB)
            both = turned[line, :]
            keys, vals = [], []
            for j in range(SLOTS):
                keys.append(jnp.broadcast_to(both[:, SLOTS + j : SLOTS + j + 1], (SLAB, 128)).astype(BF16))
                vals.append(jnp.broadcast_to(both[:, j : j + 1], (SLAB, 128)).astype(BF16))
            for g in range(FEATS // 128):
                spot = base[:, g * 128 : (g + 1) * 128]
                acc = jnp.zeros((SLAB, 128), BF16)
                for j in range(SLOTS):
                    acc = jnp.where(keys[j] == spot, vals[j], acc)
                table[line, g * 128 : (g + 1) * 128] = acc
            return carry2

        lax.fori_loop(0, PAIR // SLAB, slab, 0)
        rows = pl.ds(first, PAIR)
        part[rows, :] = jnp.dot(table[...], w_ref[...], preferred_element_type=F32) + jnp.dot(
            xs_ref[rows, :], ws_ref[...], preferred_element_type=F32
        )
        mnet.start(k, part.at[seq_rows(2 * q + 1 - at.c)], mrecv.at[k], at.mate)
        for i in range(1, 8):
            pl.when(k == i)(functools.partial(step, i))
        return carry

    lax.fori_loop(0, 8, body, 0)
    total = here_sum(1) + bias[...]
    ynet.wait(8, far_in)
    total = total + far_in[...]
    recon[...] = total.astype(BF16)
    res[...] = (total - target[...].astype(F32)).astype(BF16)
    own = pltpu.make_async_copy(res, all_ref.at[seq_rows(at.s)], local.at[1])
    own.start()
    net, pnet = Sender(send, recv, here), Sender2(psend, precv, here)
    gather_and_pick(
        at, net, pnet, res, all_ref, w_ref, id_ref, None, parts, back_ref, own.wait, lambda i: None
    )
    for k in range(8):
        mnet.sent(k, mrecv.at[k])
    for i in (0, 1):
        ynet.sent(4 * i, half_in.at[0])
        ynet.sent(4 * i + 1, half_in.at[0])
        ynet.sent(4 * i + 2, full_in.at[0])
        ynet.sent(4 * i + 3, full_in.at[0])
    ynet.sent(8, far_out)


def residuals(pre, ids, w, xs, ws, target, bias):
    vm = pl.BlockSpec(memory_space=pltpu.VMEM)
    hbm = pl.BlockSpec(memory_space=pl.ANY)
    dma = pltpu.SemaphoreType.DMA
    return pl.pallas_call(
        residual_kernel,
        out_shape=[
            jax.ShapeDtypeStruct((ROWS, COLS), BF16),
            jax.ShapeDtypeStruct((TOKENS, COLS), BF16),
            jax.ShapeDtypeStruct((SLOTS, TOKENS), F32),
        ],
        in_specs=[vm, vm, hbm, vm, vm, vm, vm],
        out_specs=[vm, vm, vm],
        scratch_shapes=[
            pltpu.VMEM((FEATS, COLS), BF16),
            pltpu.VMEM((SLAB, FEATS), BF16),
            pltpu.VMEM((PAIR, FEATS), BF16),
            pltpu.VMEM((PAIR, 128), F32),
            pltpu.VMEM((TOKENS, COLS), F32),
            pltpu.VMEM((8, ROWS, COLS), F32),
            pltpu.VMEM((6, ROWS, COLS), BF16),
            pltpu.VMEM((4, ROWS // 2, COLS), BF16),
            pltpu.VMEM((4, ROWS, COLS), BF16),
            pltpu.VMEM((ROWS, COLS), F32),
            pltpu.VMEM((ROWS, COLS), F32),
            pltpu.VMEM((ROWS, COLS), BF16),
            pltpu.VMEM((8, N_TP, SLOTS, PAIR), F32),
            dma((8,)), dma((8,)), dma((9,)), dma((9,)),
            dma((SEQ_KINDS,)), dma((SEQ_KINDS,)), dma((8, N_TP)), dma((8, N_TP)), dma((2,)),
        ],
        compiler_params=pltpu.CompilerParams(
            collective_id=1, has_side_effects=True, vmem_limit_bytes=VMEM_LIMIT
        ),
        name="residuals",
    )(pre, ids, w, xs, ws, target, bias)


def grad_kernel(
    id_ref, pre_ref, back_ref, x_ref, r_ref, ge_ref, gd_ref, st_ref, at_ref, base_ref
):
    feats = base_ref.shape[0]
    number = pl.program_id(0) * feats + lax.broadcasted_iota(jnp.int32, (feats, 128), 0)
    base_ref[...] = key_of(number).astype(BF16)
    for t in range(TOKENS // 128):
        lanes = slice(t * 128, (t + 1) * 128)
        pre = pre_ref[:, lanes]
        slope = jnp.where(pre > 0.0, back_ref[:, lanes], 0.0)
        act = jnp.maximum(pre, 0.0)
        ids = id_ref[:, lanes]
        key = jnp.where(ids >= 0, key_of(ids), -1.0)
        keys, slopes, acts = [], [], []
        for j in range(SLOTS):
            row = slice(j, j + 1)
            keys.append(jnp.broadcast_to(key[row, :], (16, 128)).astype(BF16))
            slopes.append(jnp.broadcast_to(slope[row, :], (16, 128)).astype(BF16))
            acts.append(jnp.broadcast_to(act[row, :], (16, 128)).astype(BF16))
        for r in range(feats // 16):
            lines = slice(r * 16, (r + 1) * 16)
            base = base_ref[lines, :]
            s_acc = jnp.zeros((16, 128), BF16)
            a_acc = jnp.zeros((16, 128), BF16)
            for j in range(SLOTS):
                hit = keys[j] == base
                s_acc = jnp.where(hit, slopes[j], s_acc)
                a_acc = jnp.where(hit, acts[j], a_acc)
            st_ref[lines, lanes] = s_acc
            at_ref[lines, lanes] = a_acc
    ge_ref[...] = jnp.dot(st_ref[...], x_ref[...], preferred_element_type=F32).astype(BF16)
    gd_ref[...] = jnp.dot(at_ref[...], r_ref[...], preferred_element_type=F32).astype(BF16)


def grads(ids, pre, back, x, r, feats=512):
    slots = pl.BlockSpec((SLOTS, TOKENS), lambda i: (0, 0))
    whole = pl.BlockSpec((TOKENS, COLS), lambda i: (0, 0))
    out = pl.BlockSpec((feats, COLS), lambda i: (i, 0))
    return pl.pallas_call(
        grad_kernel,
        grid=(FEATS // feats,),
        in_specs=[slots, slots, slots, whole, whole],
        out_specs=[out, out],
        out_shape=[jax.ShapeDtypeStruct((FEATS, COLS), BF16)] * 2,
        scratch_shapes=[pltpu.VMEM((feats, TOKENS), BF16)] * 2 + [pltpu.VMEM((feats, 128), BF16)],
        compiler_params=pltpu.CompilerParams(vmem_limit_bytes=VMEM_LIMIT),
        name="grads",
    )(ids, pre, back, x, r)


def small_kernel(id_ref, pre_ref, back_ref, xs_ref, r_ref, gb_ref, gs_ref, bd_ref):
    total = jnp.zeros((FEATS // 128, 128), F32)
    contract = (((0,), (0,)), ((), ()))
    pairs = (((1,), (1,)), ((), ()))
    for t in range(TOKENS // 512):
        lanes = slice(t * 512, (t + 1) * 512)
        ids = id_ref[:, lanes]
        high, low = ids >> 7, ids & 127
        slope = jnp.where(pre_ref[:, lanes] > 0.0, back_ref[:, lanes], 0.0)
        top = slope.astype(BF16).astype(F32)
        rest = slope - top
        rest_top = rest.astype(BF16).astype(F32)
        last = rest - rest_top
        lines = lax.broadcasted_iota(jnp.int32, (FEATS // 128, 512), 0)
        lanes128 = lax.broadcasted_iota(jnp.int32, (128, 512), 0)
        for j in range(SLOTS):
            row = slice(j, j + 1)
            one = jnp.where(high[row, :] == lines, 1.0, 0.0).astype(BF16)
            hit = low[row, :] == lanes128
            for value in (top, rest_top, last):
                table = jnp.where(hit, value[row, :], 0.0).astype(BF16)
                total += lax.dot_general(one, table, pairs, preferred_element_type=F32)
    gb_ref[...] = total
    gs_ref[...] = lax.dot_general(
        xs_ref[...], r_ref[...], contract, preferred_element_type=F32
    ).astype(BF16)
    bd_ref[...] = jnp.dot(jnp.ones((8, TOKENS), BF16), r_ref[...], preferred_element_type=F32)


def small_grads(ids, pre, back, xs, r):
    return pl.pallas_call(
        small_kernel,
        in_specs=[pl.BlockSpec(memory_space=pltpu.VMEM)] * 5,
        out_specs=[pl.BlockSpec(memory_space=pltpu.VMEM)] * 3,
        out_shape=[
            jax.ShapeDtypeStruct((FEATS // 128, 128), F32),
            jax.ShapeDtypeStruct((SKIP, COLS), BF16),
            jax.ShapeDtypeStruct((8, COLS), F32),
        ],
        compiler_params=pltpu.CompilerParams(vmem_limit_bytes=VMEM_LIMIT),
        name="small_grads",
    )(ids, pre, back, xs, r)


def shards(inputs, target, feature_slots, w_enc, b_enc, w_dec, b_dec, w_skip):
    ids = feature_slots[:, 0, :].T
    all_x, x_skip, pre = encode(inputs, ids, w_enc, b_enc.reshape(FEATS // 128, 128))
    recon, all_r, back = residuals(pre, ids, w_dec, x_skip, w_skip, target, b_dec[None, :])
    grad_enc, grad_dec = grads(ids, pre, back, all_x, all_r)
    grad_benc, grad_skip, grad_bdec = small_grads(ids, pre, back, x_skip, all_r)
    return recon, grad_enc, grad_dec, grad_benc.reshape(-1), grad_bdec[0], grad_skip


def solution(mesh):
    in_specs = (
        P("seq", "tp"),
        P("seq", "tp"),
        P(None, "seq", None),
        P("seq", "tp"),
        P("seq"),
        P("seq", "tp"),
        P("tp"),
        P("seq", "tp"),
    )
    out_specs = (P("seq", "tp"), P("seq", "tp"), P("seq", "tp"), P("seq"), P("tp"), P("seq", "tp"))
    return jax.shard_map(shards, mesh=mesh, in_specs=in_specs, out_specs=out_specs, check_vma=False)
```

```python
import functools

import jax
import jax.numpy as jnp
from jax import lax
from jax.experimental import pallas as pl
from jax.experimental.pallas import tpu as pltpu
from jax.sharding import PartitionSpec as P

MESH = pl.DeviceIdType.MESH
BF16 = jnp.bfloat16
F32 = jnp.float32
VMEM_LIMIT = 56 << 20

N_SEQ = 16
N_TP = 8
ROWS = 128
TOKENS = 2048
COLS = 512
FEATS = 4096
SKIP = 256
SLOTS = 8


class Place:
    def __init__(self):
        self.s = lax.axis_index("seq")
        self.p = lax.axis_index("tp")
        s, p = self.s, self.p
        self.c = lax.rem(s, 2)
        self.y = lax.rem(lax.div(s, 2), 4)
        self.zh = lax.div(s, 8)
        self.x = lax.rem(p, 4)
        self.zl = lax.div(p, 4)
        self.mate = (s + 1 - 2 * self.c, p)
        self.up = (self.seq(0, 1), p)
        self.down = (self.seq(0, 3), p)
        self.far = (self.seq(1, 0), p)
        self.right = (s, self.tp(0, 1))
        self.left = (s, self.tp(0, 3))
        self.side = (s, self.tp(1, 0))

    def seq(self, b, dy, other_core=False):
        zh = 1 - self.zh if b else self.zh
        c = 1 - self.c if other_core else self.c
        return (zh * 4 + lax.rem(self.y + dy, 4)) * 2 + c

    def tp(self, b, dx):
        zl = 1 - self.zl if b else self.zl
        return zl * 4 + lax.rem(self.x + dx, 4)


def greet(devices):
    barrier = pltpu.get_barrier_semaphore()
    for dev in devices:
        pl.semaphore_signal(barrier, inc=1, device_id=dev, device_id_type=MESH)
    pl.semaphore_wait(barrier, len(devices))


class Sender:
    def __init__(self, send, recv, here):
        self.send, self.recv, self.here = send, recv, here

    def copy(self, i, src, dst, dev):
        return pltpu.make_async_remote_copy(
            src_ref=src, dst_ref=dst, send_sem=self.send.at[i], recv_sem=self.recv.at[i],
            device_id=dev, device_id_type=MESH,
        )

    def start(self, i, src, dst, dev):
        self.copy(i, src, dst, dev).start()

    def wait(self, i, dst):
        self.copy(i, dst, dst, self.here).wait_recv()

    def sent(self, i, like):
        self.copy(i, like, like, self.here).wait_send()


def choose(k, values):
    out = values[0]
    for i, v in enumerate(values[1:], 1):
        out = jnp.where(k == i, v, out)
    return out


def seq_rows(q, half=None):
    if half is None:
        return pl.ds(pl.multiple_of(q * ROWS, ROWS), ROWS)
    return pl.ds(pl.multiple_of(q * ROWS + half * (ROWS // 2), ROWS // 2), ROWS // 2)


def key_of(number):
    value = (128 + (number & 127)).astype(F32)
    for bit in range(5):
        value = value * jnp.where((number & (128 << bit)) != 0, float(2 ** (2**bit)), 1.0)
    return value


PAIR = 2 * ROWS
PICK_ORDER = ((0, 0), (0, 3), (0, 1), (1, 0), (0, 2), (1, 3), (1, 1), (1, 2))
SEQ_KINDS = 19
HALVES = (2, 3, 6, 7, 12, 13, 17, 18)


def pick_slots(rows, w_ref, ids, bias):
    width = 256
    accs = [jnp.zeros((8, PAIR), F32) for _ in range(SLOTS)]
    for c in range(FEATS // width):
        lines = slice(c * width, (c + 1) * width)
        dots = lax.dot_general(
            w_ref[lines, :], rows, (((1,), (1,)), ((), ())), preferred_element_type=F32
        )
        if bias is not None:
            dots = dots + jnp.concatenate([bias[lines, :]] * 2, axis=1)
        for j in range(SLOTS):
            row = ids[j : j + 1, :]
            tree = dots
            for bit in range(4, -1, -1):
                half = tree.shape[0] // 2
                upper = jnp.broadcast_to((row & (8 << bit)) != 0, (half, PAIR))
                tree = jnp.where(upper, tree[half:], tree[:half])
            here = jnp.broadcast_to((row >> 8) == c, (8, PAIR))
            accs[j] = jnp.where(here, tree, accs[j])
    line = lax.broadcasted_iota(jnp.int32, (8, PAIR), 0)
    out = []
    for j in range(SLOTS):
        hit = line == (ids[j : j + 1, :] & 7)
        out.append(jnp.sum(jnp.where(hit, accs[j], 0.0), axis=0, keepdims=True))
    return jnp.concatenate(out, axis=0)


def gather_and_pick(at, net, pnet, own, rows_ref, w_ref, id_ref, bias, parts, out_ref, keep, extra):
    def blk(b, dy, half=None, other=False):
        return rows_ref.at[seq_rows(at.seq(b, dy, other), half)]

    mine = rows_ref.at[seq_rows(at.s)]
    net.start(9, own, mine, at.mate)
    net.start(8, own, mine, at.far)
    net.start(0, own, mine, at.up)
    net.start(1, own, mine, at.down)
    extra(0)
    keep()
    net.wait(9, blk(0, 0, None, True))

    def ring(b):
        k, m = 4 * b, 9 + 5 * b
        net.wait(k, blk(b, 3))
        net.start(k + 2, blk(b, 3, 0), blk(b, 3, 0), at.up)
        net.start(m + 1, blk(b, 3), blk(b, 3), at.mate)
        net.wait(k + 1, blk(b, 1))
        net.start(k + 3, blk(b, 1, 1), blk(b, 1, 1), at.down)
        net.start(m + 2, blk(b, 1), blk(b, 1), at.mate)

    def last(b):
        k, m = 4 * b, 9 + 5 * b
        net.wait(k + 2, blk(b, 2, 0))
        net.start(m + 3, blk(b, 2, 0), blk(b, 2, 0), at.mate)
        net.wait(k + 3, blk(b, 2, 1))
        net.start(m + 4, blk(b, 2, 1), blk(b, 2, 1), at.mate)

    def step(i):
        if i == 1:
            ring(0)
            net.wait(8, blk(1, 0))
            net.start(4, blk(1, 0), blk(1, 0), at.up)
            net.start(5, blk(1, 0), blk(1, 0), at.down)
            net.start(14, blk(1, 0), blk(1, 0), at.mate)
            net.wait(10, blk(0, 3, None, True))
        if i == 2:
            net.wait(11, blk(0, 1, None, True))
        if i == 3:
            ring(1)
            last(0)
            net.wait(14, blk(1, 0, None, True))
        if i == 4:
            net.wait(12, blk(0, 2, 0, True))
            net.wait(13, blk(0, 2, 1, True))
        if i == 5:
            last(1)
            net.wait(15, blk(1, 3, None, True))
        if i == 6:
            net.wait(16, blk(1, 1, None, True))
        if i == 7:
            net.wait(17, blk(1, 2, 0, True))
            net.wait(18, blk(1, 2, 1, True))
        extra(i)

    def pair_of(k):
        return choose(k, [lax.div(at.seq(b, dy), 2) for b, dy in PICK_ORDER])

    def lanes(k):
        return pl.ds(pl.multiple_of(pair_of(k) * PAIR, PAIR), PAIR)

    def body(k, carry):
        for i in range(1, 8):
            pl.when(k == i)(functools.partial(step, i))
        q = pair_of(k)
        rows = rows_ref[pl.ds(pl.multiple_of(q * PAIR, PAIR), PAIR), :]
        parts[k, at.p] = pick_slots(rows, w_ref, id_ref[:, lanes(k)], bias)
        for d in range(1, N_TP):
            here = parts.at[k, at.p]
            pnet.start((k, d), here, here, (at.s, lax.rem(at.p + d, N_TP)))
        return carry

    lax.fori_loop(0, 8, body, 0)
    extra(8)

    def add_up(k, carry):
        for d in range(1, N_TP):
            pnet.wait((k, d), parts.at[k, lax.rem(at.p + N_TP - d, N_TP)])
        total = parts[k, 0]
        for q in range(1, N_TP):
            total = total + parts[k, q]
        out_ref[:, lanes(k)] = total
        return carry

    lax.fori_loop(0, 8, add_up, 0)
    for i in range(SEQ_KINDS):
        net.sent(i, rows_ref.at[pl.ds(0, ROWS // 2 if i in HALVES else ROWS)])

    def done(k, carry):
        for d in range(1, N_TP):
            pnet.sent((k, d), parts.at[k, at.p])
        return carry

    lax.fori_loop(0, 8, done, 0)


def encode_kernel(
    x_ref, id_ref, w_hbm, b_ref, all_ref, skip_ref, pre_ref, base_row, base_col, w_ref, bias, parts,
    send, recv, psend, precv, send2, recv2, local,
):
    at = Place()
    here = (at.s, at.p)
    load = pltpu.make_async_copy(w_hbm, w_ref, local.at[0])
    load.start()
    own = pltpu.make_async_copy(x_ref, all_ref.at[seq_rows(at.s)], local.at[1])
    own.start()

    half_p = lax.div(at.s, 2)
    stay = half_p == at.p
    peers = [(at.s, lax.rem(at.p + d, N_TP)) for d in range(1, N_TP)]
    same, cross = (2 * at.p + at.c, half_p), (2 * at.p + 1 - at.c, half_p)
    around = [at.mate, at.up, at.down, at.far, cross] + peers
    barrier = pltpu.get_barrier_semaphore()
    for dev in around:
        pl.semaphore_signal(barrier, inc=1, device_id=dev, device_id_type=MESH)

    @pl.when(jnp.logical_not(stay))
    def _():
        pl.semaphore_signal(barrier, inc=1, device_id=same, device_id_type=MESH)

    across = (128 + lax.broadcasted_iota(jnp.int32, (SLAB, 128), 1)).astype(F32)
    below = (128 + lax.broadcasted_iota(jnp.int32, (128, 128), 0)).astype(F32)
    first = lax.axis_index("tp") == 0
    for g in range(FEATS // 128):
        base_row[:, g * 128 : (g + 1) * 128] = (across * float(2**g)).astype(BF16)
        base_col[g * 128 : (g + 1) * 128, :] = (below * float(2**g)).astype(BF16)
        row = jnp.where(first, b_ref[g : g + 1, :], 0.0)
        bias[g * 128 : (g + 1) * 128, :] = jnp.broadcast_to(row, (128, 128)).T
    pl.semaphore_wait(barrier, len(around) + 1 - stay.astype(jnp.int32))

    net, pnet, net2 = Sender(send, recv, here), Sender2(psend, precv, here), Sender(send2, recv2, here)

    def part(h):
        return x_ref.at[:, pl.ds(pl.multiple_of(h * SKIP, SKIP), SKIP)]

    land = skip_ref.at[seq_rows(at.s)]
    inside = pltpu.make_async_copy(part(at.c), land, local.at[2])

    def piece(b, dx, half=None):
        q = at.tp(b, dx)
        if half is None:
            return skip_ref.at[pl.ds(pl.multiple_of(q * 256, 256), 256)]
        return skip_ref.at[pl.ds(pl.multiple_of(q * 256 + half * 128, 128), 128)]

    def ring(b):
        k = 2 + 4 * b
        net2.wait(k, piece(b, 3))
        net2.start(k + 2, piece(b, 3, 0), piece(b, 3, 0), at.right)
        net2.wait(k + 1, piece(b, 1))
        net2.start(k + 3, piece(b, 1, 1), piece(b, 1, 1), at.left)

    def extra(i):
        if i == 0:
            net2.start(1, part(1 - at.c), land, cross)

            @pl.when(jnp.logical_not(stay))
            def _():
                net2.start(0, part(at.c), land, same)

            @pl.when(stay)
            def _():
                inside.start()

        if i == 2:
            net2.wait(1, skip_ref.at[seq_rows(2 * at.p + 1 - at.c)])

            @pl.when(jnp.logical_not(stay))
            def _():
                net2.wait(0, skip_ref.at[seq_rows(2 * at.p + at.c)])

            @pl.when(stay)
            def _():
                pltpu.make_async_copy(part(at.c), land, local.at[2]).wait()

            net2.start(10, piece(0, 0), piece(0, 0), at.side)
            net2.start(2, piece(0, 0), piece(0, 0), at.right)
            net2.start(3, piece(0, 0), piece(0, 0), at.left)
        if i == 4:
            net2.wait(10, piece(1, 0))
            net2.start(6, piece(1, 0), piece(1, 0), at.right)
            net2.start(7, piece(1, 0), piece(1, 0), at.left)
            ring(0)
        if i == 6:
            ring(1)
        if i == 8:
            for b in (0, 1):
                net2.wait(4 + 4 * b, piece(b, 2, 0))
                net2.wait(5 + 4 * b, piece(b, 2, 1))

    def keep():
        load.wait()
        own.wait()

    gather_and_pick(at, net, pnet, x_ref, all_ref, w_ref, id_ref, bias, parts, pre_ref, keep, extra)

    @pl.when(jnp.logical_not(stay))
    def _():
        net2.sent(0, land)

    net2.sent(1, land)
    for i in range(2, 11):
        net2.sent(i, skip_ref.at[pl.ds(0, 128 if i in (4, 5, 8, 9) else 256)])


class Sender2(Sender):
    def copy(self, i, src, dst, dev):
        return pltpu.make_async_remote_copy(
            src_ref=src, dst_ref=dst, send_sem=self.send.at[i[0], i[1]],
            recv_sem=self.recv.at[i[0], i[1]], device_id=dev, device_id_type=MESH,
        )


def encode(x, ids, w, bias):
    vm = pl.BlockSpec(memory_space=pltpu.VMEM)
    hbm = pl.BlockSpec(memory_space=pl.ANY)
    dma = pltpu.SemaphoreType.DMA
    return pl.pallas_call(
        encode_kernel,
        out_shape=[
            jax.ShapeDtypeStruct((TOKENS, COLS), BF16),
            jax.ShapeDtypeStruct((TOKENS, SKIP), BF16),
            jax.ShapeDtypeStruct((SLOTS, TOKENS), F32),
            jax.ShapeDtypeStruct((SLAB, FEATS), BF16),
            jax.ShapeDtypeStruct((FEATS, 128), BF16),
        ],
        in_specs=[hbm, vm, hbm, vm],
        out_specs=[vm] * 5,
        scratch_shapes=[
            pltpu.VMEM((FEATS, COLS), BF16),
            pltpu.VMEM((FEATS, 128), F32),
            pltpu.VMEM((8, N_TP, SLOTS, PAIR), F32),
            dma((SEQ_KINDS,)), dma((SEQ_KINDS,)), dma((8, N_TP)), dma((8, N_TP)),
            dma((11,)), dma((11,)), dma((3,)),
        ],
        compiler_params=pltpu.CompilerParams(
            collective_id=0, has_side_effects=True, vmem_limit_bytes=VMEM_LIMIT
        ),
        name="encode",
    )(x, ids, w, bias)


SUM_ORDER = tuple((b, dy) for b in (1, 0) for dy in (2, 1, 3, 0))
SLAB = 32


def residual_kernel(
    pre_ref, id_ref, w_hbm, xs_ref, ws_ref, target, bias, base, recon, all_ref, back_ref, skip_grad,
    bias_grad, w_ref, table, turned, part, mrecv, out_buf, half_in, full_in, far_out, far_in, res, parts,
    msend, mrcv, ysend, yrcv, send, recv, psend, precv, local,
):
    at = Place()
    here = (at.s, at.p)
    load = pltpu.make_async_copy(w_hbm, w_ref, local.at[0])
    load.start()
    peers = [(at.s, lax.rem(at.p + d, N_TP)) for d in range(1, N_TP)]
    around = [at.mate, at.up, at.down, at.far] + peers
    barrier = pltpu.get_barrier_semaphore()
    for dev in around:
        pl.semaphore_signal(barrier, inc=1, device_id=dev, device_id_type=MESH)
    pl.semaphore_wait(barrier, len(around))
    load.wait()

    mnet, ynet = Sender(msend, mrcv, here), Sender(ysend, yrcv, here)
    H = ROWS // 2

    def pair(k, half=None):
        b, dy = SUM_ORDER[k]
        rows = seq_rows(at.seq(b, dy), half)
        mine = slice(0, ROWS) if half is None else slice(half * H, (half + 1) * H)
        return part[rows, :] + mrecv[k, mine, :]

    def opposite(i):
        mnet.wait(4 * i, mrecv.at[4 * i])
        out_buf[3 * i] = pair(4 * i).astype(BF16)
        ynet.start(4 * i, out_buf.at[3 * i, pl.ds(0, H)], half_in.at[2 * i], at.up)
        ynet.start(4 * i + 1, out_buf.at[3 * i, pl.ds(H, H)], half_in.at[2 * i + 1], at.down)

    def upward(i):
        k = 4 * i + 1
        mnet.wait(k, mrecv.at[k])
        out_buf[3 * i + 1, H:, :] = pair(k, 1).astype(BF16)
        ynet.wait(4 * i, half_in.at[2 * i])
        out_buf[3 * i + 1, :H, :] = (pair(k, 0) + half_in[2 * i].astype(F32)).astype(BF16)
        ynet.start(4 * i + 2, out_buf.at[3 * i + 1], full_in.at[2 * i], at.up)

    def downward(i):
        k = 4 * i + 2
        mnet.wait(k, mrecv.at[k])
        out_buf[3 * i + 2, :H, :] = pair(k, 0).astype(BF16)
        ynet.wait(4 * i + 1, half_in.at[2 * i + 1])
        out_buf[3 * i + 2, H:, :] = (pair(k, 1) + half_in[2 * i + 1].astype(F32)).astype(BF16)
        ynet.start(4 * i + 3, out_buf.at[3 * i + 2], full_in.at[2 * i + 1], at.down)

    def here_sum(i):
        k = 4 * i + 3
        mnet.wait(k, mrecv.at[k])
        ynet.wait(4 * i + 2, full_in.at[2 * i])
        ynet.wait(4 * i + 3, full_in.at[2 * i + 1])
        return pair(k) + full_in[2 * i].astype(F32) + full_in[2 * i + 1].astype(F32)

    def step(i):
        if i == 1:
            opposite(0)
        if i == 2:
            upward(0)
        if i == 3:
            downward(0)
        if i == 5:
            opposite(1)
            far_out[...] = here_sum(0)
            ynet.start(8, far_out, far_in, at.far)
        if i == 6:
            upward(1)
        if i == 7:
            downward(1)

    filler = jnp.zeros((128 - 2 * SLOTS, 128), F32)

    def body(k, carry):
        q = choose(k, [lax.div(at.seq(b, dy), 2) for b, dy in SUM_ORDER])
        first = pl.multiple_of(q * PAIR, PAIR)
        for t in range(2):
            lanes = pl.ds(pl.multiple_of(first + t * 128, 128), 128)
            ids = id_ref[:, lanes]
            act = jnp.maximum(pre_ref[:, lanes], 0.0)
            key = jnp.where(ids >= 0, key_of(ids), -1.0)
            turned[t * 128 : (t + 1) * 128, :] = jnp.concatenate([act, key, filler], axis=0).T

        def slab(r, carry2):
            line = pl.ds(pl.multiple_of(r * SLAB, SLAB), SLAB)
            both = turned[line, :]
            keys, vals = [], []
            for j in range(SLOTS):
                keys.append(jnp.broadcast_to(both[:, SLOTS + j : SLOTS + j + 1], (SLAB, 128)).astype(BF16))
                vals.append(jnp.broadcast_to(both[:, j : j + 1], (SLAB, 128)).astype(BF16))
            for g in range(FEATS // 128):
                spot = base[:, g * 128 : (g + 1) * 128]
                acc = jnp.zeros((SLAB, 128), BF16)
                for j in range(SLOTS):
                    acc = jnp.where(keys[j] == spot, vals[j], acc)
                table[line, g * 128 : (g + 1) * 128] = acc
            return carry2

        lax.fori_loop(0, PAIR // SLAB, slab, 0)
        rows = pl.ds(first, PAIR)
        part[rows, :] = jnp.dot(table[...], w_ref[...], preferred_element_type=F32) + jnp.dot(
            xs_ref[rows, :], ws_ref[...], preferred_element_type=F32
        )
        mnet.start(k, part.at[seq_rows(2 * q + 1 - at.c)], mrecv.at[k], at.mate)
        for i in range(1, 8):
            pl.when(k == i)(functools.partial(step, i))
        return carry

    lax.fori_loop(0, 8, body, 0)
    total = here_sum(1) + bias[...]
    ynet.wait(8, far_in)
    total = total + far_in[...]
    recon[...] = total.astype(BF16)
    res[...] = (total - target[...].astype(F32)).astype(BF16)
    own = pltpu.make_async_copy(res, all_ref.at[seq_rows(at.s)], local.at[1])
    own.start()
    net, pnet = Sender(send, recv, here), Sender2(psend, precv, here)

    def extra(i):
        if i == 8:
            skip_grad[...] = lax.dot_general(
                xs_ref[...], all_ref[...], (((0,), (0,)), ((), ())), preferred_element_type=F32
            ).astype(BF16)
            ones = jnp.ones((8, TOKENS), BF16)
            bias_grad[...] = jnp.dot(ones, all_ref[...], preferred_element_type=F32)

    gather_and_pick(
        at, net, pnet, res, all_ref, w_ref, id_ref, None, parts, back_ref, own.wait, extra
    )
    for k in range(8):
        mnet.sent(k, mrecv.at[k])
    for i in (0, 1):
        ynet.sent(4 * i, half_in.at[0])
        ynet.sent(4 * i + 1, half_in.at[0])
        ynet.sent(4 * i + 2, full_in.at[0])
        ynet.sent(4 * i + 3, full_in.at[0])
    ynet.sent(8, far_out)


def residuals(pre, ids, w, xs, ws, target, bias, base):
    vm = pl.BlockSpec(memory_space=pltpu.VMEM)
    hbm = pl.BlockSpec(memory_space=pl.ANY)
    dma = pltpu.SemaphoreType.DMA
    return pl.pallas_call(
        residual_kernel,
        out_shape=[
            jax.ShapeDtypeStruct((ROWS, COLS), BF16),
            jax.ShapeDtypeStruct((TOKENS, COLS), BF16),
            jax.ShapeDtypeStruct((SLOTS, TOKENS), F32),
            jax.ShapeDtypeStruct((SKIP, COLS), BF16),
            jax.ShapeDtypeStruct((8, COLS), F32),
        ],
        in_specs=[vm, vm, hbm, vm, vm, vm, vm, vm],
        out_specs=[vm] * 5,
        scratch_shapes=[
            pltpu.VMEM((FEATS, COLS), BF16),
            pltpu.VMEM((PAIR, FEATS), BF16),
            pltpu.VMEM((PAIR, 128), F32),
            pltpu.VMEM((TOKENS, COLS), F32),
            pltpu.VMEM((8, ROWS, COLS), F32),
            pltpu.VMEM((6, ROWS, COLS), BF16),
            pltpu.VMEM((4, ROWS // 2, COLS), BF16),
            pltpu.VMEM((4, ROWS, COLS), BF16),
            pltpu.VMEM((ROWS, COLS), F32),
            pltpu.VMEM((ROWS, COLS), F32),
            pltpu.VMEM((ROWS, COLS), BF16),
            pltpu.VMEM((8, N_TP, SLOTS, PAIR), F32),
            dma((8,)), dma((8,)), dma((9,)), dma((9,)),
            dma((SEQ_KINDS,)), dma((SEQ_KINDS,)), dma((8, N_TP)), dma((8, N_TP)), dma((2,)),
        ],
        compiler_params=pltpu.CompilerParams(
            collective_id=1, has_side_effects=True, vmem_limit_bytes=VMEM_LIMIT
        ),
        name="residuals",
    )(pre, ids, w, xs, ws, target, bias, base)


def grad_kernel(
    id_ref, pre_ref, back_ref, base_ref, x_ref, r_ref, ge_ref, gd_ref, gb_ref, st_ref, at_ref
):
    feats = base_ref.shape[0]

    @pl.when(pl.program_id(0) == 0)
    def _():
        gb_ref[...] = bias_grads(id_ref, pre_ref, back_ref)

    for t in range(TOKENS // 128):
        lanes = slice(t * 128, (t + 1) * 128)
        pre = pre_ref[:, lanes]
        slope = jnp.where(pre > 0.0, back_ref[:, lanes], 0.0)
        act = jnp.maximum(pre, 0.0)
        ids = id_ref[:, lanes]
        key = jnp.where(ids >= 0, key_of(ids), -1.0)
        keys, slopes, acts = [], [], []
        for j in range(SLOTS):
            row = slice(j, j + 1)
            keys.append(jnp.broadcast_to(key[row, :], (16, 128)).astype(BF16))
            slopes.append(jnp.broadcast_to(slope[row, :], (16, 128)).astype(BF16))
            acts.append(jnp.broadcast_to(act[row, :], (16, 128)).astype(BF16))
        for r in range(feats // 16):
            lines = slice(r * 16, (r + 1) * 16)
            base = base_ref[lines, :]
            s_acc = jnp.zeros((16, 128), BF16)
            a_acc = jnp.zeros((16, 128), BF16)
            for j in range(SLOTS):
                hit = keys[j] == base
                s_acc = jnp.where(hit, slopes[j], s_acc)
                a_acc = jnp.where(hit, acts[j], a_acc)
            st_ref[lines, lanes] = s_acc
            at_ref[lines, lanes] = a_acc
    ge_ref[...] = jnp.dot(st_ref[...], x_ref[...], preferred_element_type=F32).astype(BF16)
    gd_ref[...] = jnp.dot(at_ref[...], r_ref[...], preferred_element_type=F32).astype(BF16)


def grads(ids, pre, back, base, x, r, feats=1024):
    slots = pl.BlockSpec((SLOTS, TOKENS), lambda i: (0, 0))
    whole = pl.BlockSpec((TOKENS, COLS), lambda i: (0, 0))
    out = pl.BlockSpec((feats, COLS), lambda i: (i, 0))
    return pl.pallas_call(
        grad_kernel,
        grid=(FEATS // feats,),
        in_specs=[slots, slots, slots, pl.BlockSpec((feats, 128), lambda i: (i, 0)), whole, whole],
        out_specs=[out, out, pl.BlockSpec((FEATS // 128, 128), lambda i: (0, 0))],
        out_shape=[jax.ShapeDtypeStruct((FEATS, COLS), BF16)] * 2
        + [jax.ShapeDtypeStruct((FEATS // 128, 128), F32)],
        scratch_shapes=[pltpu.VMEM((feats, TOKENS), BF16)] * 2,
        compiler_params=pltpu.CompilerParams(vmem_limit_bytes=VMEM_LIMIT),
        name="grads",
    )(ids, pre, back, base, x, r)


def bias_grads(id_ref, pre_ref, back_ref):
    total = jnp.zeros((FEATS // 128, 128), F32)
    pairs = (((1,), (1,)), ((), ()))
    ids = id_ref[...]
    high, low = ids >> 7, ids & 127
    slope = jnp.where(pre_ref[...] > 0.0, back_ref[...], 0.0)
    top = slope.astype(BF16).astype(F32)
    rest = slope - top
    lines = lax.broadcasted_iota(jnp.int32, (FEATS // 128, TOKENS), 0)
    lines128 = lax.broadcasted_iota(jnp.int32, (128, TOKENS), 0)
    for j in range(SLOTS):
        row = slice(j, j + 1)
        one = jnp.where(high[row, :] == lines, 1.0, 0.0).astype(BF16)
        hit = low[row, :] == lines128
        for value in (top, rest):
            table = jnp.where(hit, value[row, :], 0.0).astype(BF16)
            total += lax.dot_general(one, table, pairs, preferred_element_type=F32)
    return total


def shards(inputs, target, feature_slots, w_enc, b_enc, w_dec, b_dec, w_skip):
    ids = feature_slots[:, 0, :].T
    all_x, x_skip, pre, base_row, base_col = encode(inputs, ids, w_enc, b_enc.reshape(FEATS // 128, 128))
    recon, all_r, back, grad_skip, grad_bdec = residuals(
        pre, ids, w_dec, x_skip, w_skip, target, b_dec[None, :], base_row
    )
    grad_enc, grad_dec, grad_benc = grads(ids, pre, back, base_col, all_x, all_r)
    return recon, grad_enc, grad_dec, grad_benc.reshape(-1), grad_bdec[0], grad_skip


def solution(mesh):
    in_specs = (
        P("seq", "tp"),
        P("seq", "tp"),
        P(None, "seq", None),
        P("seq", "tp"),
        P("seq"),
        P("seq", "tp"),
        P("tp"),
        P("seq", "tp"),
    )
    out_specs = (P("seq", "tp"), P("seq", "tp"), P("seq", "tp"), P("seq"), P("tp"), P("seq", "tp"))
    return jax.shard_map(shards, mesh=mesh, in_specs=in_specs, out_specs=out_specs, check_vma=False)
```

```python
import functools

import jax
import jax.numpy as jnp
from jax import lax
from jax.experimental import pallas as pl
from jax.experimental.pallas import tpu as pltpu
from jax.sharding import PartitionSpec as P

MESH = pl.DeviceIdType.MESH
BF16 = jnp.bfloat16
F32 = jnp.float32
VMEM_LIMIT = 56 << 20

N_SEQ = 16
N_TP = 8
ROWS = 128
TOKENS = 2048
COLS = 512
FEATS = 4096
SKIP = 256
SLOTS = 8


class Place:
    def __init__(self):
        self.s = lax.axis_index("seq")
        self.p = lax.axis_index("tp")
        s, p = self.s, self.p
        self.c = lax.rem(s, 2)
        self.y = lax.rem(lax.div(s, 2), 4)
        self.zh = lax.div(s, 8)
        self.x = lax.rem(p, 4)
        self.zl = lax.div(p, 4)
        self.mate = (s + 1 - 2 * self.c, p)
        self.up = (self.seq(0, 1), p)
        self.down = (self.seq(0, 3), p)
        self.far = (self.seq(1, 0), p)
        self.right = (s, self.tp(0, 1))
        self.left = (s, self.tp(0, 3))
        self.side = (s, self.tp(1, 0))

    def seq(self, b, dy, other_core=False):
        zh = 1 - self.zh if b else self.zh
        c = 1 - self.c if other_core else self.c
        return (zh * 4 + lax.rem(self.y + dy, 4)) * 2 + c

    def tp(self, b, dx):
        zl = 1 - self.zl if b else self.zl
        return zl * 4 + lax.rem(self.x + dx, 4)


def greet(devices):
    barrier = pltpu.get_barrier_semaphore()
    for dev in devices:
        pl.semaphore_signal(barrier, inc=1, device_id=dev, device_id_type=MESH)
    pl.semaphore_wait(barrier, len(devices))


class Sender:
    def __init__(self, send, recv, here):
        self.send, self.recv, self.here = send, recv, here

    def copy(self, i, src, dst, dev):
        return pltpu.make_async_remote_copy(
            src_ref=src, dst_ref=dst, send_sem=self.send.at[i], recv_sem=self.recv.at[i],
            device_id=dev, device_id_type=MESH,
        )

    def start(self, i, src, dst, dev):
        self.copy(i, src, dst, dev).start()

    def wait(self, i, dst):
        self.copy(i, dst, dst, self.here).wait_recv()

    def sent(self, i, like):
        self.copy(i, like, like, self.here).wait_send()


def choose(k, values):
    out = values[0]
    for i, v in enumerate(values[1:], 1):
        out = jnp.where(k == i, v, out)
    return out


def seq_rows(q, half=None):
    if half is None:
        return pl.ds(pl.multiple_of(q * ROWS, ROWS), ROWS)
    return pl.ds(pl.multiple_of(q * ROWS + half * (ROWS // 2), ROWS // 2), ROWS // 2)


def key_of(number):
    value = (128 + (number & 127)).astype(F32)
    for bit in range(5):
        value = value * jnp.where((number & (128 << bit)) != 0, float(2 ** (2**bit)), 1.0)
    return value


PAIR = 2 * ROWS
PICK_ORDER = ((0, 0), (0, 3), (0, 1), (1, 0), (0, 2), (1, 3), (1, 1), (1, 2))
SEQ_KINDS = 19
HALVES = (2, 3, 6, 7, 12, 13, 17, 18)


def pick_slots(rows, w_ref, ids, bias):
    width = 256
    accs = [jnp.zeros((8, PAIR), F32) for _ in range(SLOTS)]
    for c in range(FEATS // width):
        lines = slice(c * width, (c + 1) * width)
        dots = lax.dot_general(
            w_ref[lines, :], rows, (((1,), (1,)), ((), ())), preferred_element_type=F32
        )
        if bias is not None:
            dots = dots + jnp.concatenate([bias[lines, :]] * 2, axis=1)
        for j in range(SLOTS):
            row = ids[j : j + 1, :]

            def narrow(tree, down_to):
                while tree.shape[0] > down_to:
                    half = tree.shape[0] // 2
                    upper = jnp.broadcast_to((row & half) != 0, (half, PAIR))
                    tree = jnp.where(upper, tree[half:], tree[:half])
                return tree

            blocks = [narrow(dots[64 * i : 64 * (i + 1)], 8) for i in range(width // 64)]
            tree = blocks
            bit = 64
            while len(tree) > 1:
                upper = jnp.broadcast_to((row & bit) != 0, (8, PAIR))
                tree = [jnp.where(upper, b, a) for a, b in zip(tree[::2], tree[1::2])]
                bit *= 2
            tree = tree[0]
            here = jnp.broadcast_to((row >> 8) == c, (8, PAIR))
            accs[j] = jnp.where(here, tree, accs[j])
    line = lax.broadcasted_iota(jnp.int32, (8, PAIR), 0)
    out = []
    for j in range(SLOTS):
        hit = line == (ids[j : j + 1, :] & 7)
        out.append(jnp.sum(jnp.where(hit, accs[j], 0.0), axis=0, keepdims=True))
    return jnp.concatenate(out, axis=0)


def gather_and_pick(at, net, pnet, own, rows_ref, w_ref, id_ref, bias, parts, keep, extra):
    def blk(b, dy, half=None, other=False):
        return rows_ref.at[seq_rows(at.seq(b, dy, other), half)]

    mine = rows_ref.at[seq_rows(at.s)]
    net.start(9, own, mine, at.mate)
    net.start(8, own, mine, at.far)
    net.start(0, own, mine, at.up)
    net.start(1, own, mine, at.down)
    extra(0)
    keep()
    net.wait(9, blk(0, 0, None, True))

    def ring(b):
        k, m = 4 * b, 9 + 5 * b
        net.wait(k, blk(b, 3))
        net.start(k + 2, blk(b, 3, 0), blk(b, 3, 0), at.up)
        net.start(m + 1, blk(b, 3), blk(b, 3), at.mate)
        net.wait(k + 1, blk(b, 1))
        net.start(k + 3, blk(b, 1, 1), blk(b, 1, 1), at.down)
        net.start(m + 2, blk(b, 1), blk(b, 1), at.mate)

    def last(b):
        k, m = 4 * b, 9 + 5 * b
        net.wait(k + 2, blk(b, 2, 0))
        net.start(m + 3, blk(b, 2, 0), blk(b, 2, 0), at.mate)
        net.wait(k + 3, blk(b, 2, 1))
        net.start(m + 4, blk(b, 2, 1), blk(b, 2, 1), at.mate)

    def step(i):
        if i == 1:
            ring(0)
            net.wait(8, blk(1, 0))
            net.start(4, blk(1, 0), blk(1, 0), at.up)
            net.start(5, blk(1, 0), blk(1, 0), at.down)
            net.start(14, blk(1, 0), blk(1, 0), at.mate)
            net.wait(10, blk(0, 3, None, True))
        if i == 2:
            net.wait(11, blk(0, 1, None, True))
        if i == 3:
            ring(1)
            last(0)
            net.wait(14, blk(1, 0, None, True))
        if i == 4:
            net.wait(12, blk(0, 2, 0, True))
            net.wait(13, blk(0, 2, 1, True))
        if i == 5:
            last(1)
            net.wait(15, blk(1, 3, None, True))
        if i == 6:
            net.wait(16, blk(1, 1, None, True))
        if i == 7:
            net.wait(17, blk(1, 2, 0, True))
            net.wait(18, blk(1, 2, 1, True))
        extra(i)

    def body(k, carry):
        for i in range(1, 8):
            pl.when(k == i)(functools.partial(step, i))
        span = pair_lanes(at, PICK_ORDER, k)
        parts[k, at.p] = pick_slots(rows_ref[span, :], w_ref, id_ref[:, span], bias)
        for d in range(1, N_TP):
            here = parts.at[k, at.p]
            pnet.start((k, d), here, here, (at.s, lax.rem(at.p + d, N_TP)))
        return carry

    lax.fori_loop(0, 8, body, 0)


def pair_lanes(at, order, k):
    q = choose(k, [lax.div(at.seq(b, dy), 2) for b, dy in order])
    return pl.ds(pl.multiple_of(q * PAIR, PAIR), PAIR)


def add_up(at, pnet, parts, out_ref, k):
    for d in range(1, N_TP):
        pnet.wait((k, d), parts.at[k, lax.rem(at.p + N_TP - d, N_TP)])
    total = parts[k, 0]
    for q in range(1, N_TP):
        total = total + parts[k, q]
    out_ref[:, pair_lanes(at, PICK_ORDER, k)] = total


def all_sent(at, net, pnet, rows_ref, parts):
    for i in range(SEQ_KINDS):
        net.sent(i, rows_ref.at[pl.ds(0, ROWS // 2 if i in HALVES else ROWS)])

    def done(k, carry):
        for d in range(1, N_TP):
            pnet.sent((k, d), parts.at[k, at.p])
        return carry

    lax.fori_loop(0, 8, done, 0)


SUM_ORDER = ((0, 2), (1, 2), (1, 1), (1, 3), (1, 0), (0, 1), (0, 3), (0, 0))
SLAB = 32


class Sender2(Sender):
    def copy(self, i, src, dst, dev):
        return pltpu.make_async_remote_copy(
            src_ref=src, dst_ref=dst, send_sem=self.send.at[i[0], i[1]],
            recv_sem=self.recv.at[i[0], i[1]], device_id=dev, device_id_type=MESH,
        )


def step_kernel(
    x_ref, id_ref, we_hbm, b_ref, wd_hbm, ws_ref, target, dec_bias,
    recon, x_hbm, r_hbm, pre_ref, back_ref, col_hbm, skip_grad, bias_grad,
    we_ref, wd_ref, all_ref, res_ref, skip_ref, base_row, base_col, bias, enc_parts, back_parts,
    table, turned, part, mrecv, out_buf, half_in, full_in, far_out, far_in, res,
    send, recv, psend, precv, send2, recv2, msend, mrcv, ysend, yrcv, send3, recv3, psend3, precv3,
    local,
):
    at = Place()
    here = (at.s, at.p)
    load = pltpu.make_async_copy(we_hbm, we_ref, local.at[0])
    load.start()
    own = pltpu.make_async_copy(x_ref, all_ref.at[seq_rows(at.s)], local.at[1])
    own.start()
    load_dec = pltpu.make_async_copy(wd_hbm, wd_ref, local.at[3])
    load_dec.start()

    half_p = lax.div(at.s, 2)
    stay = half_p == at.p
    peers = [(at.s, lax.rem(at.p + d, N_TP)) for d in range(1, N_TP)]
    same, cross = (2 * at.p + at.c, half_p), (2 * at.p + 1 - at.c, half_p)
    around = [at.mate, at.up, at.down, at.far, cross] + peers
    barrier = pltpu.get_barrier_semaphore()
    for dev in around:
        pl.semaphore_signal(barrier, inc=1, device_id=dev, device_id_type=MESH)

    @pl.when(jnp.logical_not(stay))
    def _():
        pl.semaphore_signal(barrier, inc=1, device_id=same, device_id_type=MESH)

    across = (128 + lax.broadcasted_iota(jnp.int32, (SLAB, 128), 1)).astype(F32)
    below = (128 + lax.broadcasted_iota(jnp.int32, (128, 128), 0)).astype(F32)
    first = lax.axis_index("tp") == 0
    for g in range(FEATS // 128):
        base_row[:, g * 128 : (g + 1) * 128] = (across * float(2**g)).astype(BF16)
        base_col[g * 128 : (g + 1) * 128, :] = (below * float(2**g)).astype(BF16)
        row = jnp.where(first, b_ref[g : g + 1, :], 0.0)
        bias[g * 128 : (g + 1) * 128, :] = jnp.broadcast_to(row, (128, 128)).T
    pl.semaphore_wait(barrier, len(around) + 1 - stay.astype(jnp.int32))

    net, pnet, net2 = Sender(send, recv, here), Sender2(psend, precv, here), Sender(send2, recv2, here)

    def columns(h):
        return x_ref.at[:, pl.ds(pl.multiple_of(h * SKIP, SKIP), SKIP)]

    land = skip_ref.at[seq_rows(at.s)]
    inside = pltpu.make_async_copy(columns(at.c), land, local.at[2])

    def piece(b, dx, half=None):
        q = at.tp(b, dx)
        if half is None:
            return skip_ref.at[pl.ds(pl.multiple_of(q * 256, 256), 256)]
        return skip_ref.at[pl.ds(pl.multiple_of(q * 256 + half * 128, 128), 128)]

    def ring(b):
        k = 2 + 4 * b
        net2.wait(k, piece(b, 3))
        net2.start(k + 2, piece(b, 3, 0), piece(b, 3, 0), at.right)
        net2.wait(k + 1, piece(b, 1))
        net2.start(k + 3, piece(b, 1, 1), piece(b, 1, 1), at.left)

    def extra(i):
        if i == 0:
            net2.start(1, columns(1 - at.c), land, cross)

            @pl.when(jnp.logical_not(stay))
            def _():
                net2.start(0, columns(at.c), land, same)

            @pl.when(stay)
            def _():
                inside.start()

        if i == 2:
            net2.wait(1, skip_ref.at[seq_rows(2 * at.p + 1 - at.c)])

            @pl.when(jnp.logical_not(stay))
            def _():
                net2.wait(0, skip_ref.at[seq_rows(2 * at.p + at.c)])

            @pl.when(stay)
            def _():
                pltpu.make_async_copy(columns(at.c), land, local.at[2]).wait()

            net2.start(10, piece(0, 0), piece(0, 0), at.side)
            net2.start(2, piece(0, 0), piece(0, 0), at.right)
            net2.start(3, piece(0, 0), piece(0, 0), at.left)
        if i == 4:
            net2.wait(10, piece(1, 0))
            net2.start(6, piece(1, 0), piece(1, 0), at.right)
            net2.start(7, piece(1, 0), piece(1, 0), at.left)
            ring(0)
        if i == 6:
            ring(1)
        if i == 8:
            for b in (0, 1):
                net2.wait(4 + 4 * b, piece(b, 2, 0))
                net2.wait(5 + 4 * b, piece(b, 2, 1))

    def keep():
        load.wait()
        own.wait()

    gather_and_pick(at, net, pnet, x_ref, all_ref, we_ref, id_ref, bias, enc_parts, keep, extra)
    extra(8)
    out_x = pltpu.make_async_copy(all_ref, x_hbm, local.at[4])
    out_x.start()
    out_col = pltpu.make_async_copy(base_col, col_hbm, local.at[5])
    out_col.start()
    load_dec.wait()

    mnet, ynet = Sender(msend, mrcv, here), Sender(ysend, yrcv, here)
    H = ROWS // 2

    def pair(k, half=None):
        b, dy = SUM_ORDER[k]
        rows = seq_rows(at.seq(b, dy), half)
        mine = slice(0, ROWS) if half is None else slice(half * H, (half + 1) * H)
        return part[rows, :] + mrecv[k, mine, :]

    def opposite(i):
        k = SUM_ORDER.index((1 - i, 2))
        mnet.wait(k, mrecv.at[k])
        out_buf[3 * i] = pair(k).astype(BF16)
        ynet.start(4 * i, out_buf.at[3 * i, pl.ds(0, H)], half_in.at[2 * i], at.up)
        ynet.start(4 * i + 1, out_buf.at[3 * i, pl.ds(H, H)], half_in.at[2 * i + 1], at.down)

    def upward(i):
        k = SUM_ORDER.index((1 - i, 1))
        mnet.wait(k, mrecv.at[k])
        out_buf[3 * i + 1, H:, :] = pair(k, 1).astype(BF16)
        ynet.wait(4 * i, half_in.at[2 * i])
        out_buf[3 * i + 1, :H, :] = (pair(k, 0) + half_in[2 * i].astype(F32)).astype(BF16)
        ynet.start(4 * i + 2, out_buf.at[3 * i + 1], full_in.at[2 * i], at.up)

    def downward(i):
        k = SUM_ORDER.index((1 - i, 3))
        mnet.wait(k, mrecv.at[k])
        out_buf[3 * i + 2, :H, :] = pair(k, 0).astype(BF16)
        ynet.wait(4 * i + 1, half_in.at[2 * i + 1])
        out_buf[3 * i + 2, H:, :] = (pair(k, 1) + half_in[2 * i + 1].astype(F32)).astype(BF16)
        ynet.start(4 * i + 3, out_buf.at[3 * i + 2], full_in.at[2 * i + 1], at.down)

    def here_sum(i):
        k = SUM_ORDER.index((1 - i, 0))
        mnet.wait(k, mrecv.at[k])
        ynet.wait(4 * i + 2, full_in.at[2 * i])
        ynet.wait(4 * i + 3, full_in.at[2 * i + 1])
        return pair(k) + full_in[2 * i].astype(F32) + full_in[2 * i + 1].astype(F32)

    def step(i):
        if i == 1:
            opposite(1)
        if i == 2:
            opposite(0)
        if i == 3:
            upward(0)
        if i == 4:
            downward(0)
        if i == 6:
            far_out[...] = here_sum(0)
            ynet.start(8, far_out, far_in, at.far)
            upward(1)
        if i == 7:
            downward(1)

    filler = jnp.zeros((128 - 2 * SLOTS, 128), F32)

    def body(k, carry):
        add_up(at, pnet, enc_parts, pre_ref, choose(k, [PICK_ORDER.index(o) for o in SUM_ORDER]))
        q = choose(k, [lax.div(at.seq(b, dy), 2) for b, dy in SUM_ORDER])
        first = pl.multiple_of(q * PAIR, PAIR)
        for t in range(2):
            lanes = pl.ds(pl.multiple_of(first + t * 128, 128), 128)
            ids = id_ref[:, lanes]
            act = jnp.maximum(pre_ref[:, lanes], 0.0)
            key = jnp.where(ids >= 0, key_of(ids), -1.0)
            turned[t * 128 : (t + 1) * 128, :] = jnp.concatenate([act, key, filler], axis=0).T

        def slab(r, carry2):
            line = pl.ds(pl.multiple_of(r * SLAB, SLAB), SLAB)
            both = turned[line, :]
            keys, vals = [], []
            for j in range(SLOTS):
                keys.append(jnp.broadcast_to(both[:, SLOTS + j : SLOTS + j + 1], (SLAB, 128)).astype(BF16))
                vals.append(jnp.broadcast_to(both[:, j : j + 1], (SLAB, 128)).astype(BF16))
            for g in range(FEATS // 128):
                spot = base_row[:, g * 128 : (g + 1) * 128]
                acc = jnp.zeros((SLAB, 128), BF16)
                for j in range(SLOTS):
                    acc = jnp.where(keys[j] == spot, vals[j], acc)
                table[line, g * 128 : (g + 1) * 128] = acc
            return carry2

        lax.fori_loop(0, PAIR // SLAB, slab, 0)
        rows = pl.ds(first, PAIR)
        part[rows, :] = jnp.dot(table[...], wd_ref[...], preferred_element_type=F32) + jnp.dot(
            skip_ref[rows, :], ws_ref[...], preferred_element_type=F32
        )
        mnet.start(k, part.at[seq_rows(2 * q + 1 - at.c)], mrecv.at[k], at.mate)
        for i in range(1, 8):
            pl.when(k == i)(functools.partial(step, i))
        return carry

    lax.fori_loop(0, 8, body, 0)
    total = here_sum(1) + dec_bias[...]
    ynet.wait(8, far_in)
    total = total + far_in[...]
    recon[...] = total.astype(BF16)
    res[...] = (total - target[...].astype(F32)).astype(BF16)
    own = pltpu.make_async_copy(res, res_ref.at[seq_rows(at.s)], local.at[6])
    own.start()
    net3, pnet3 = Sender(send3, recv3, here), Sender2(psend3, precv3, here)
    gather_and_pick(
        at, net3, pnet3, res, res_ref, wd_ref, id_ref, None, back_parts, own.wait, lambda i: None
    )
    out_r = pltpu.make_async_copy(res_ref, r_hbm, local.at[7])
    out_r.start()
    skip_grad[...] = lax.dot_general(
        skip_ref[...], res_ref[...], (((0,), (0,)), ((), ())), preferred_element_type=F32
    ).astype(BF16)
    ones = jnp.ones((8, TOKENS), BF16)
    bias_grad[...] = jnp.dot(ones, res_ref[...], preferred_element_type=F32)[:1]

    def add_back(k, carry):
        add_up(at, pnet3, back_parts, back_ref, k)
        return carry

    lax.fori_loop(0, 8, add_back, 0)
    all_sent(at, net, pnet, all_ref, enc_parts)
    all_sent(at, net3, pnet3, res_ref, back_parts)

    @pl.when(jnp.logical_not(stay))
    def _():
        net2.sent(0, land)

    net2.sent(1, land)
    for i in range(2, 11):
        net2.sent(i, skip_ref.at[pl.ds(0, 128 if i in (4, 5, 8, 9) else 256)])
    for k in range(8):
        mnet.sent(k, mrecv.at[k])
    for i in (0, 1):
        ynet.sent(4 * i, half_in.at[0])
        ynet.sent(4 * i + 1, half_in.at[0])
        ynet.sent(4 * i + 2, full_in.at[0])
        ynet.sent(4 * i + 3, full_in.at[0])
    ynet.sent(8, far_out)
    out_x.wait()
    out_col.wait()
    out_r.wait()


def step(x, ids, w_enc, b_enc, w_dec, w_skip, target, b_dec):
    vm = pl.BlockSpec(memory_space=pltpu.VMEM)
    hbm = pl.BlockSpec(memory_space=pl.ANY)
    dma = pltpu.SemaphoreType.DMA
    return pl.pallas_call(
        step_kernel,
        out_shape=[
            jax.ShapeDtypeStruct((ROWS, COLS), BF16),
            jax.ShapeDtypeStruct((TOKENS, COLS), BF16),
            jax.ShapeDtypeStruct((TOKENS, COLS), BF16),
            jax.ShapeDtypeStruct((SLOTS, TOKENS), F32),
            jax.ShapeDtypeStruct((SLOTS, TOKENS), F32),
            jax.ShapeDtypeStruct((FEATS, 128), BF16),
            jax.ShapeDtypeStruct((SKIP, COLS), BF16),
            jax.ShapeDtypeStruct((1, COLS), F32),
        ],
        in_specs=[hbm, vm, hbm, vm, hbm, vm, vm, vm],
        out_specs=[vm, hbm, hbm, vm, vm, hbm, vm, vm],
        scratch_shapes=[
            pltpu.VMEM((FEATS, COLS), BF16),
            pltpu.VMEM((FEATS, COLS), BF16),
            pltpu.VMEM((TOKENS, COLS), BF16),
            pltpu.VMEM((TOKENS, COLS), BF16),
            pltpu.VMEM((TOKENS, SKIP), BF16),
            pltpu.VMEM((SLAB, FEATS), BF16),
            pltpu.VMEM((FEATS, 128), BF16),
            pltpu.VMEM((FEATS, 128), F32),
            pltpu.VMEM((8, N_TP, SLOTS, PAIR), F32),
            pltpu.VMEM((8, N_TP, SLOTS, PAIR), F32),
            pltpu.VMEM((PAIR, FEATS), BF16),
            pltpu.VMEM((PAIR, 128), F32),
            pltpu.VMEM((TOKENS, COLS), F32),
            pltpu.VMEM((8, ROWS, COLS), F32),
            pltpu.VMEM((6, ROWS, COLS), BF16),
            pltpu.VMEM((4, ROWS // 2, COLS), BF16),
            pltpu.VMEM((4, ROWS, COLS), BF16),
            pltpu.VMEM((ROWS, COLS), F32),
            pltpu.VMEM((ROWS, COLS), F32),
            pltpu.VMEM((ROWS, COLS), BF16),
            dma((SEQ_KINDS,)), dma((SEQ_KINDS,)), dma((8, N_TP)), dma((8, N_TP)),
            dma((11,)), dma((11,)), dma((8,)), dma((8,)), dma((9,)), dma((9,)),
            dma((SEQ_KINDS,)), dma((SEQ_KINDS,)), dma((8, N_TP)), dma((8, N_TP)), dma((8,)),
        ],
        compiler_params=pltpu.CompilerParams(
            collective_id=0, has_side_effects=True, vmem_limit_bytes=VMEM_LIMIT
        ),
        name="step",
    )(x, ids, w_enc, b_enc, w_dec, w_skip, target, b_dec)


def grad_kernel(
    id_ref, pre_ref, back_ref, base_ref, x_ref, r_ref, ge_ref, gd_ref, gb_ref, st_ref, at_ref
):
    feats = base_ref.shape[0]

    @pl.when(pl.program_id(0) == 0)
    def _():
        gb_ref[...] = bias_grads(id_ref, pre_ref, back_ref)

    for t in range(TOKENS // 128):
        lanes = slice(t * 128, (t + 1) * 128)
        pre = pre_ref[:, lanes]
        slope = jnp.where(pre > 0.0, back_ref[:, lanes], 0.0)
        act = jnp.maximum(pre, 0.0)
        ids = id_ref[:, lanes]
        key = jnp.where(ids >= 0, key_of(ids), -1.0)
        keys, slopes, acts = [], [], []
        for j in range(SLOTS):
            row = slice(j, j + 1)
            keys.append(jnp.broadcast_to(key[row, :], (16, 128)).astype(BF16))
            slopes.append(jnp.broadcast_to(slope[row, :], (16, 128)).astype(BF16))
            acts.append(jnp.broadcast_to(act[row, :], (16, 128)).astype(BF16))
        for r in range(feats // 16):
            lines = slice(r * 16, (r + 1) * 16)
            base = base_ref[lines, :]
            s_acc = jnp.zeros((16, 128), BF16)
            a_acc = jnp.zeros((16, 128), BF16)
            for j in range(SLOTS):
                hit = keys[j] == base
                s_acc = jnp.where(hit, slopes[j], s_acc)
                a_acc = jnp.where(hit, acts[j], a_acc)
            st_ref[lines, lanes] = s_acc
            at_ref[lines, lanes] = a_acc
    ge_ref[...] = jnp.dot(st_ref[...], x_ref[...], preferred_element_type=F32).astype(BF16)
    gd_ref[...] = jnp.dot(at_ref[...], r_ref[...], preferred_element_type=F32).astype(BF16)


def grads(ids, pre, back, base, x, r, feats=1024):
    slots = pl.BlockSpec((SLOTS, TOKENS), lambda i: (0, 0))
    whole = pl.BlockSpec((TOKENS, COLS), lambda i: (0, 0))
    out = pl.BlockSpec((feats, COLS), lambda i: (i, 0))
    return pl.pallas_call(
        grad_kernel,
        grid=(FEATS // feats,),
        in_specs=[slots, slots, slots, pl.BlockSpec((feats, 128), lambda i: (i, 0)), whole, whole],
        out_specs=[out, out, pl.BlockSpec((FEATS // 128, 128), lambda i: (0, 0))],
        out_shape=[jax.ShapeDtypeStruct((FEATS, COLS), BF16)] * 2
        + [jax.ShapeDtypeStruct((FEATS // 128, 128), F32)],
        scratch_shapes=[pltpu.VMEM((feats, TOKENS), BF16)] * 2,
        compiler_params=pltpu.CompilerParams(vmem_limit_bytes=VMEM_LIMIT),
        name="grads",
    )(ids, pre, back, base, x, r)


def bias_grads(id_ref, pre_ref, back_ref):
    total = jnp.zeros((FEATS // 128, 128), F32)
    pairs = (((1,), (1,)), ((), ()))
    ids = id_ref[...]
    high, low = ids >> 7, ids & 127
    slope = jnp.where(pre_ref[...] > 0.0, back_ref[...], 0.0)
    top = slope.astype(BF16).astype(F32)
    rest = slope - top
    lines = lax.broadcasted_iota(jnp.int32, (FEATS // 128, TOKENS), 0)
    lines128 = lax.broadcasted_iota(jnp.int32, (128, TOKENS), 0)
    for j in range(SLOTS):
        row = slice(j, j + 1)
        one = jnp.where(high[row, :] == lines, 1.0, 0.0).astype(BF16)
        hit = low[row, :] == lines128
        for value in (top, rest):
            table = jnp.where(hit, value[row, :], 0.0).astype(BF16)
            total += lax.dot_general(one, table, pairs, preferred_element_type=F32)
    return total


def shards(inputs, target, feature_slots, w_enc, b_enc, w_dec, b_dec, w_skip):
    ids = feature_slots[:, 0, :].T
    recon, all_x, all_r, pre, back, base, grad_skip, grad_bdec = step(
        inputs, ids, w_enc, b_enc.reshape(FEATS // 128, 128), w_dec, w_skip, target, b_dec[None, :]
    )
    grad_enc, grad_dec, grad_benc = grads(ids, pre, back, base, all_x, all_r)
    return recon, grad_enc, grad_dec, grad_benc.reshape(-1), grad_bdec.reshape(-1), grad_skip


def solution(mesh):
    in_specs = (
        P("seq", "tp"),
        P("seq", "tp"),
        P(None, "seq", None),
        P("seq", "tp"),
        P("seq"),
        P("seq", "tp"),
        P("tp"),
        P("seq", "tp"),
    )
    out_specs = (P("seq", "tp"), P("seq", "tp"), P("seq", "tp"), P("seq"), P("tp"), P("seq", "tp"))
    return jax.shard_map(shards, mesh=mesh, in_specs=in_specs, out_specs=out_specs, check_vma=False)
```

```python
import functools

import jax
import jax.numpy as jnp
from jax import lax
from jax.experimental import pallas as pl
from jax.experimental.pallas import tpu as pltpu
from jax.sharding import PartitionSpec as P

MESH = pl.DeviceIdType.MESH
BF16 = jnp.bfloat16
F32 = jnp.float32
VMEM_LIMIT = 56 << 20

N_SEQ = 16
N_TP = 8
ROWS = 128
TOKENS = 2048
COLS = 512
FEATS = 4096
SKIP = 256
SLOTS = 8


class Place:
    def __init__(self):
        self.s = lax.axis_index("seq")
        self.p = lax.axis_index("tp")
        s, p = self.s, self.p
        self.c = lax.rem(s, 2)
        self.y = lax.rem(lax.div(s, 2), 4)
        self.zh = lax.div(s, 8)
        self.x = lax.rem(p, 4)
        self.zl = lax.div(p, 4)
        self.mate = (s + 1 - 2 * self.c, p)
        self.up = (self.seq(0, 1), p)
        self.down = (self.seq(0, 3), p)
        self.far = (self.seq(1, 0), p)
        self.right = (s, self.tp(0, 1))
        self.left = (s, self.tp(0, 3))
        self.side = (s, self.tp(1, 0))

    def seq(self, b, dy, other_core=False):
        zh = 1 - self.zh if b else self.zh
        c = 1 - self.c if other_core else self.c
        return (zh * 4 + lax.rem(self.y + dy, 4)) * 2 + c

    def tp(self, b, dx):
        zl = 1 - self.zl if b else self.zl
        return zl * 4 + lax.rem(self.x + dx, 4)


def greet(devices):
    barrier = pltpu.get_barrier_semaphore()
    for dev in devices:
        pl.semaphore_signal(barrier, inc=1, device_id=dev, device_id_type=MESH)
    pl.semaphore_wait(barrier, len(devices))


class Sender:
    def __init__(self, send, recv, here):
        self.send, self.recv, self.here = send, recv, here

    def copy(self, i, src, dst, dev):
        return pltpu.make_async_remote_copy(
            src_ref=src, dst_ref=dst, send_sem=self.send.at[i], recv_sem=self.recv.at[i],
            device_id=dev, device_id_type=MESH,
        )

    def start(self, i, src, dst, dev):
        self.copy(i, src, dst, dev).start()

    def wait(self, i, dst):
        self.copy(i, dst, dst, self.here).wait_recv()

    def sent(self, i, like):
        self.copy(i, like, like, self.here).wait_send()


def choose(k, values):
    out = values[0]
    for i, v in enumerate(values[1:], 1):
        out = jnp.where(k == i, v, out)
    return out


def seq_rows(q, half=None):
    if half is None:
        return pl.ds(pl.multiple_of(q * ROWS, ROWS), ROWS)
    return pl.ds(pl.multiple_of(q * ROWS + half * (ROWS // 2), ROWS // 2), ROWS // 2)


def key_of(number):
    value = (128 + (number & 127)).astype(F32)
    for bit in range(5):
        value = value * jnp.where((number & (128 << bit)) != 0, float(2 ** (2**bit)), 1.0)
    return value


PAIR = 2 * ROWS
PICK_ORDER = (
    ((0, 0, False), (0, 0, True)),
    ((0, 3, False), (0, 1, False)),
    ((0, 3, True), (0, 1, True)),
    ((1, 0, False), (1, 0, True)),
    ((0, 2, False), (0, 2, True)),
    ((1, 3, False), (1, 1, False)),
    ((1, 3, True), (1, 1, True)),
    ((1, 2, False), (1, 2, True)),
)
SEQ_KINDS = 19
HALVES = (2, 3, 6, 7, 12, 13, 17, 18)


def pick_slots(rows, w_ref, ids, bias):
    width = 256
    accs = [jnp.zeros((8, PAIR), F32) for _ in range(SLOTS)]
    for c in range(FEATS // width):
        lines = slice(c * width, (c + 1) * width)
        dots = lax.dot_general(
            w_ref[lines, :], rows, (((1,), (1,)), ((), ())), preferred_element_type=F32
        )
        if bias is not None:
            dots = dots + jnp.concatenate([bias[lines, :]] * 2, axis=1)
        for j in range(SLOTS):
            row = ids[j : j + 1, :]

            def narrow(tree, down_to):
                while tree.shape[0] > down_to:
                    half = tree.shape[0] // 2
                    upper = jnp.broadcast_to((row & half) != 0, (half, PAIR))
                    tree = jnp.where(upper, tree[half:], tree[:half])
                return tree

            blocks = [narrow(dots[64 * i : 64 * (i + 1)], 8) for i in range(width // 64)]
            tree = blocks
            bit = 64
            while len(tree) > 1:
                upper = jnp.broadcast_to((row & bit) != 0, (8, PAIR))
                tree = [jnp.where(upper, b, a) for a, b in zip(tree[::2], tree[1::2])]
                bit *= 2
            tree = tree[0]
            here = jnp.broadcast_to((row >> 8) == c, (8, PAIR))
            accs[j] = jnp.where(here, tree, accs[j])
    line = lax.broadcasted_iota(jnp.int32, (8, PAIR), 0)
    out = []
    for j in range(SLOTS):
        hit = line == (ids[j : j + 1, :] & 7)
        out.append(jnp.sum(jnp.where(hit, accs[j], 0.0), axis=0, keepdims=True))
    return jnp.concatenate(out, axis=0)


def gather_and_pick(at, net, pnet, own, rows_ref, w_ref, id_ref, bias, parts, keep, extra):
    def blk(b, dy, half=None, other=False):
        return rows_ref.at[seq_rows(at.seq(b, dy, other), half)]

    mine = rows_ref.at[seq_rows(at.s)]
    net.start(9, own, mine, at.mate)
    net.start(8, own, mine, at.far)
    net.start(0, own, mine, at.up)
    net.start(1, own, mine, at.down)
    extra(0)
    keep()
    net.wait(9, blk(0, 0, None, True))

    def ring(b):
        k, m = 4 * b, 9 + 5 * b
        net.wait(k, blk(b, 3))
        net.start(k + 2, blk(b, 3, 0), blk(b, 3, 0), at.up)
        net.start(m + 1, blk(b, 3), blk(b, 3), at.mate)
        net.wait(k + 1, blk(b, 1))
        net.start(k + 3, blk(b, 1, 1), blk(b, 1, 1), at.down)
        net.start(m + 2, blk(b, 1), blk(b, 1), at.mate)

    def last(b):
        k, m = 4 * b, 9 + 5 * b
        net.wait(k + 2, blk(b, 2, 0))
        net.start(m + 3, blk(b, 2, 0), blk(b, 2, 0), at.mate)
        net.wait(k + 3, blk(b, 2, 1))
        net.start(m + 4, blk(b, 2, 1), blk(b, 2, 1), at.mate)

    def step(i):
        if i == 1:
            ring(0)
        if i == 2:
            net.wait(8, blk(1, 0))
            net.start(4, blk(1, 0), blk(1, 0), at.up)
            net.start(5, blk(1, 0), blk(1, 0), at.down)
            net.start(14, blk(1, 0), blk(1, 0), at.mate)
            net.wait(10, blk(0, 3, None, True))
            net.wait(11, blk(0, 1, None, True))
        if i == 3:
            last(0)
            net.wait(14, blk(1, 0, None, True))
        if i == 4:
            ring(1)
            net.wait(12, blk(0, 2, 0, True))
            net.wait(13, blk(0, 2, 1, True))
        if i == 6:
            last(1)
            net.wait(15, blk(1, 3, None, True))
            net.wait(16, blk(1, 1, None, True))
        if i == 7:
            net.wait(17, blk(1, 2, 0, True))
            net.wait(18, blk(1, 2, 1, True))
        extra(i)

    def body(k, carry):
        for i in range(1, 8):
            pl.when(k == i)(functools.partial(step, i))
        one, two = blocks_of(at, k)
        rows = jnp.concatenate([rows_ref[one, :], rows_ref[two, :]], axis=0)
        ids = jnp.concatenate([id_ref[:, one], id_ref[:, two]], axis=1)
        parts[k, at.p] = pick_slots(rows, w_ref, ids, bias)
        for d in range(1, N_TP):
            here = parts.at[k, at.p]
            pnet.start((k, d), here, here, (at.s, lax.rem(at.p + d, N_TP)))
        return carry

    lax.fori_loop(0, 8, body, 0)


def blocks_of(at, k):
    return [seq_rows(choose(k, [at.seq(*both[i]) for both in PICK_ORDER])) for i in (0, 1)]


def add_up(at, pnet, parts, out_ref, k):
    for d in range(1, N_TP):
        pnet.wait((k, d), parts.at[k, lax.rem(at.p + N_TP - d, N_TP)])
    total = parts[k, 0]
    for q in range(1, N_TP):
        total = total + parts[k, q]
    one, two = blocks_of(at, k)
    out_ref[:, one] = total[:, :ROWS]
    out_ref[:, two] = total[:, ROWS:]


def all_sent(at, net, pnet, rows_ref, parts):
    for i in range(SEQ_KINDS):
        net.sent(i, rows_ref.at[pl.ds(0, ROWS // 2 if i in HALVES else ROWS)])

    def done(k, carry):
        for d in range(1, N_TP):
            pnet.sent((k, d), parts.at[k, at.p])
        return carry

    lax.fori_loop(0, 8, done, 0)


SUM_ORDER = ((0, 2), (1, 2), (1, 1), (1, 3), (1, 0), (0, 1), (0, 3), (0, 0))
NEEDED = (4, 7, 5, 3, 1, 2, 0)
SLAB = 32


class Sender2(Sender):
    def copy(self, i, src, dst, dev):
        return pltpu.make_async_remote_copy(
            src_ref=src, dst_ref=dst, send_sem=self.send.at[i[0], i[1]],
            recv_sem=self.recv.at[i[0], i[1]], device_id=dev, device_id_type=MESH,
        )


def step_kernel(
    x_ref, id_ref, we_hbm, b_ref, wd_hbm, ws_ref, target, dec_bias,
    recon, x_hbm, r_hbm, pre_ref, back_ref, col_hbm, skip_grad, bias_grad,
    we_ref, wd_ref, all_ref, res_ref, skip_ref, base_row, base_col, bias, enc_parts, back_parts,
    table, turned, part, mrecv, out_buf, half_in, full_in, far_out, far_in, res,
    send, recv, psend, precv, send2, recv2, msend, mrcv, ysend, yrcv, send3, recv3, psend3, precv3,
    local,
):
    at = Place()
    here = (at.s, at.p)
    load = pltpu.make_async_copy(we_hbm, we_ref, local.at[0])
    load.start()
    own = pltpu.make_async_copy(x_ref, all_ref.at[seq_rows(at.s)], local.at[1])
    own.start()
    load_dec = pltpu.make_async_copy(wd_hbm, wd_ref, local.at[3])
    load_dec.start()

    half_p = lax.div(at.s, 2)
    stay = half_p == at.p
    peers = [(at.s, lax.rem(at.p + d, N_TP)) for d in range(1, N_TP)]
    same, cross = (2 * at.p + at.c, half_p), (2 * at.p + 1 - at.c, half_p)
    around = [at.mate, at.up, at.down, at.far, cross] + peers
    barrier = pltpu.get_barrier_semaphore()
    for dev in around:
        pl.semaphore_signal(barrier, inc=1, device_id=dev, device_id_type=MESH)

    @pl.when(jnp.logical_not(stay))
    def _():
        pl.semaphore_signal(barrier, inc=1, device_id=same, device_id_type=MESH)

    across = (128 + lax.broadcasted_iota(jnp.int32, (SLAB, 128), 1)).astype(F32)
    below = (128 + lax.broadcasted_iota(jnp.int32, (128, 128), 0)).astype(F32)
    first = lax.axis_index("tp") == 0
    for g in range(FEATS // 128):
        base_row[:, g * 128 : (g + 1) * 128] = (across * float(2**g)).astype(BF16)
        base_col[g * 128 : (g + 1) * 128, :] = (below * float(2**g)).astype(BF16)
        row = jnp.where(first, b_ref[g : g + 1, :], 0.0)
        bias[g * 128 : (g + 1) * 128, :] = jnp.broadcast_to(row, (128, 128)).T
    pl.semaphore_wait(barrier, len(around) + 1 - stay.astype(jnp.int32))

    net, pnet, net2 = Sender(send, recv, here), Sender2(psend, precv, here), Sender(send2, recv2, here)

    def columns(h):
        return x_ref.at[:, pl.ds(pl.multiple_of(h * SKIP, SKIP), SKIP)]

    land = skip_ref.at[seq_rows(at.s)]
    inside = pltpu.make_async_copy(columns(at.c), land, local.at[2])

    def piece(b, dx, half=None):
        q = at.tp(b, dx)
        if half is None:
            return skip_ref.at[pl.ds(pl.multiple_of(q * 256, 256), 256)]
        return skip_ref.at[pl.ds(pl.multiple_of(q * 256 + half * 128, 128), 128)]

    def ring(b):
        k = 2 + 4 * b
        net2.wait(k, piece(b, 3))
        net2.start(k + 2, piece(b, 3, 0), piece(b, 3, 0), at.right)
        net2.wait(k + 1, piece(b, 1))
        net2.start(k + 3, piece(b, 1, 1), piece(b, 1, 1), at.left)

    def extra(i):
        if i == 0:
            net2.start(1, columns(1 - at.c), land, cross)

            @pl.when(jnp.logical_not(stay))
            def _():
                net2.start(0, columns(at.c), land, same)

            @pl.when(stay)
            def _():
                inside.start()

        if i == 1:
            net2.wait(1, skip_ref.at[seq_rows(2 * at.p + 1 - at.c)])

            @pl.when(jnp.logical_not(stay))
            def _():
                net2.wait(0, skip_ref.at[seq_rows(2 * at.p + at.c)])

            @pl.when(stay)
            def _():
                pltpu.make_async_copy(columns(at.c), land, local.at[2]).wait()

            net2.start(10, piece(0, 0), piece(0, 0), at.side)
            net2.start(2, piece(0, 0), piece(0, 0), at.right)
            net2.start(3, piece(0, 0), piece(0, 0), at.left)
        if i == 3:
            net2.wait(10, piece(1, 0))
            net2.start(6, piece(1, 0), piece(1, 0), at.right)
            net2.start(7, piece(1, 0), piece(1, 0), at.left)
            ring(0)
        if i == 5:
            ring(1)
        if i == 8:
            for b in (0, 1):
                net2.wait(4 + 4 * b, piece(b, 2, 0))
                net2.wait(5 + 4 * b, piece(b, 2, 1))

    def keep():
        load.wait()
        own.wait()

    gather_and_pick(at, net, pnet, x_ref, all_ref, we_ref, id_ref, bias, enc_parts, keep, extra)
    extra(8)
    out_x = pltpu.make_async_copy(all_ref, x_hbm, local.at[4])
    out_x.start()
    out_col = pltpu.make_async_copy(base_col, col_hbm, local.at[5])
    out_col.start()
    load_dec.wait()

    mnet, ynet = Sender(msend, mrcv, here), Sender(ysend, yrcv, here)
    H = ROWS // 2

    def pair(k, half=None):
        b, dy = SUM_ORDER[k]
        rows = seq_rows(at.seq(b, dy), half)
        mine = slice(0, ROWS) if half is None else slice(half * H, (half + 1) * H)
        return part[rows, :] + mrecv[k, mine, :]

    def opposite(i):
        k = SUM_ORDER.index((1 - i, 2))
        mnet.wait(k, mrecv.at[k])
        out_buf[3 * i] = pair(k).astype(BF16)
        ynet.start(4 * i, out_buf.at[3 * i, pl.ds(0, H)], half_in.at[2 * i], at.up)
        ynet.start(4 * i + 1, out_buf.at[3 * i, pl.ds(H, H)], half_in.at[2 * i + 1], at.down)

    def upward(i):
        k = SUM_ORDER.index((1 - i, 1))
        mnet.wait(k, mrecv.at[k])
        out_buf[3 * i + 1, H:, :] = pair(k, 1).astype(BF16)
        ynet.wait(4 * i, half_in.at[2 * i])
        out_buf[3 * i + 1, :H, :] = (pair(k, 0) + half_in[2 * i].astype(F32)).astype(BF16)
        ynet.start(4 * i + 2, out_buf.at[3 * i + 1], full_in.at[2 * i], at.up)

    def downward(i):
        k = SUM_ORDER.index((1 - i, 3))
        mnet.wait(k, mrecv.at[k])
        out_buf[3 * i + 2, :H, :] = pair(k, 0).astype(BF16)
        ynet.wait(4 * i + 1, half_in.at[2 * i + 1])
        out_buf[3 * i + 2, H:, :] = (pair(k, 1) + half_in[2 * i + 1].astype(F32)).astype(BF16)
        ynet.start(4 * i + 3, out_buf.at[3 * i + 2], full_in.at[2 * i + 1], at.down)

    def here_sum(i):
        k = SUM_ORDER.index((1 - i, 0))
        mnet.wait(k, mrecv.at[k])
        ynet.wait(4 * i + 2, full_in.at[2 * i])
        ynet.wait(4 * i + 3, full_in.at[2 * i + 1])
        return pair(k) + full_in[2 * i].astype(F32) + full_in[2 * i + 1].astype(F32)

    def step(i):
        if i == 1:
            opposite(1)
        if i == 2:
            opposite(0)
        if i == 3:
            upward(0)
        if i == 4:
            downward(0)
        if i == 6:
            far_out[...] = here_sum(0)
            ynet.start(8, far_out, far_in, at.far)
            upward(1)
        if i == 7:
            downward(1)

    filler = jnp.zeros((128 - 2 * SLOTS, 128), F32)

    def body(k, carry):

        @pl.when(k < 7)
        def _():
            add_up(at, pnet, enc_parts, pre_ref, choose(k, NEEDED))

        @pl.when(k == 2)
        def _():
            add_up(at, pnet, enc_parts, pre_ref, 6)

        q = choose(k, [lax.div(at.seq(b, dy), 2) for b, dy in SUM_ORDER])
        first = pl.multiple_of(q * PAIR, PAIR)
        for t in range(2):
            lanes = pl.ds(pl.multiple_of(first + t * 128, 128), 128)
            ids = id_ref[:, lanes]
            act = jnp.maximum(pre_ref[:, lanes], 0.0)
            key = jnp.where(ids >= 0, key_of(ids), -1.0)
            turned[t * 128 : (t + 1) * 128, :] = jnp.concatenate([act, key, filler], axis=0).T

        def slab(r, carry2):
            line = pl.ds(pl.multiple_of(r * SLAB, SLAB), SLAB)
            both = turned[line, :]
            keys, vals = [], []
            for j in range(SLOTS):
                keys.append(jnp.broadcast_to(both[:, SLOTS + j : SLOTS + j + 1], (SLAB, 128)).astype(BF16))
                vals.append(jnp.broadcast_to(both[:, j : j + 1], (SLAB, 128)).astype(BF16))
            for g in range(FEATS // 128):
                spot = base_row[:, g * 128 : (g + 1) * 128]
                acc = jnp.zeros((SLAB, 128), BF16)
                for j in range(SLOTS):
                    acc = jnp.where(keys[j] == spot, vals[j], acc)
                table[line, g * 128 : (g + 1) * 128] = acc
            return carry2

        lax.fori_loop(0, PAIR // SLAB, slab, 0)
        for i in range(1, 8):
            pl.when(k == i)(functools.partial(step, i))
        rows = pl.ds(first, PAIR)
        part[rows, :] = jnp.dot(table[...], wd_ref[...], preferred_element_type=F32) + jnp.dot(
            skip_ref[rows, :], ws_ref[...], preferred_element_type=F32
        )
        mnet.start(k, part.at[seq_rows(2 * q + 1 - at.c)], mrecv.at[k], at.mate)
        return carry

    lax.fori_loop(0, 8, body, 0)
    total = here_sum(1) + dec_bias[...]
    ynet.wait(8, far_in)
    total = total + far_in[...]
    recon[...] = total.astype(BF16)
    res[...] = (total - target[...].astype(F32)).astype(BF16)
    own = pltpu.make_async_copy(res, res_ref.at[seq_rows(at.s)], local.at[6])
    own.start()
    net3, pnet3 = Sender(send3, recv3, here), Sender2(psend3, precv3, here)
    gather_and_pick(
        at, net3, pnet3, res, res_ref, wd_ref, id_ref, None, back_parts, own.wait, lambda i: None
    )
    out_r = pltpu.make_async_copy(res_ref, r_hbm, local.at[7])
    out_r.start()
    skip_grad[...] = lax.dot_general(
        skip_ref[...], res_ref[...], (((0,), (0,)), ((), ())), preferred_element_type=F32
    ).astype(BF16)
    ones = jnp.ones((8, TOKENS), BF16)
    bias_grad[...] = jnp.dot(ones, res_ref[...], preferred_element_type=F32)[:1]

    def add_back(k, carry):
        add_up(at, pnet3, back_parts, back_ref, k)
        return carry

    lax.fori_loop(0, 8, add_back, 0)
    all_sent(at, net, pnet, all_ref, enc_parts)
    all_sent(at, net3, pnet3, res_ref, back_parts)

    @pl.when(jnp.logical_not(stay))
    def _():
        net2.sent(0, land)

    net2.sent(1, land)
    for i in range(2, 11):
        net2.sent(i, skip_ref.at[pl.ds(0, 128 if i in (4, 5, 8, 9) else 256)])
    for k in range(8):
        mnet.sent(k, mrecv.at[k])
    for i in (0, 1):
        ynet.sent(4 * i, half_in.at[0])
        ynet.sent(4 * i + 1, half_in.at[0])
        ynet.sent(4 * i + 2, full_in.at[0])
        ynet.sent(4 * i + 3, full_in.at[0])
    ynet.sent(8, far_out)
    out_x.wait()
    out_col.wait()
    out_r.wait()


def step(x, ids, w_enc, b_enc, w_dec, w_skip, target, b_dec):
    vm = pl.BlockSpec(memory_space=pltpu.VMEM)
    hbm = pl.BlockSpec(memory_space=pl.ANY)
    dma = pltpu.SemaphoreType.DMA
    return pl.pallas_call(
        step_kernel,
        out_shape=[
            jax.ShapeDtypeStruct((ROWS, COLS), BF16),
            jax.ShapeDtypeStruct((TOKENS, COLS), BF16),
            jax.ShapeDtypeStruct((TOKENS, COLS), BF16),
            jax.ShapeDtypeStruct((SLOTS, TOKENS), F32),
            jax.ShapeDtypeStruct((SLOTS, TOKENS), F32),
            jax.ShapeDtypeStruct((FEATS, 128), BF16),
            jax.ShapeDtypeStruct((SKIP, COLS), BF16),
            jax.ShapeDtypeStruct((1, COLS), F32),
        ],
        in_specs=[hbm, vm, hbm, vm, hbm, vm, vm, vm],
        out_specs=[vm, hbm, hbm, vm, vm, hbm, vm, vm],
        scratch_shapes=[
            pltpu.VMEM((FEATS, COLS), BF16),
            pltpu.VMEM((FEATS, COLS), BF16),
            pltpu.VMEM((TOKENS, COLS), BF16),
            pltpu.VMEM((TOKENS, COLS), BF16),
            pltpu.VMEM((TOKENS, SKIP), BF16),
            pltpu.VMEM((SLAB, FEATS), BF16),
            pltpu.VMEM((FEATS, 128), BF16),
            pltpu.VMEM((FEATS, 128), F32),
            pltpu.VMEM((8, N_TP, SLOTS, PAIR), F32),
            pltpu.VMEM((8, N_TP, SLOTS, PAIR), F32),
            pltpu.VMEM((PAIR, FEATS), BF16),
            pltpu.VMEM((PAIR, 128), F32),
            pltpu.VMEM((TOKENS, COLS), F32),
            pltpu.VMEM((8, ROWS, COLS), F32),
            pltpu.VMEM((6, ROWS, COLS), BF16),
            pltpu.VMEM((4, ROWS // 2, COLS), BF16),
            pltpu.VMEM((4, ROWS, COLS), BF16),
            pltpu.VMEM((ROWS, COLS), F32),
            pltpu.VMEM((ROWS, COLS), F32),
            pltpu.VMEM((ROWS, COLS), BF16),
            dma((SEQ_KINDS,)), dma((SEQ_KINDS,)), dma((8, N_TP)), dma((8, N_TP)),
            dma((11,)), dma((11,)), dma((8,)), dma((8,)), dma((9,)), dma((9,)),
            dma((SEQ_KINDS,)), dma((SEQ_KINDS,)), dma((8, N_TP)), dma((8, N_TP)), dma((8,)),
        ],
        compiler_params=pltpu.CompilerParams(
            collective_id=0, has_side_effects=True, vmem_limit_bytes=VMEM_LIMIT
        ),
        name="step",
    )(x, ids, w_enc, b_enc, w_dec, w_skip, target, b_dec)


def grad_kernel(
    id_ref, pre_ref, back_ref, base_ref, x_ref, r_ref, ge_ref, gd_ref, gb_ref, st_ref, at_ref
):
    feats = base_ref.shape[0]

    @pl.when(pl.program_id(0) == 0)
    def _():
        gb_ref[...] = bias_grads(id_ref, pre_ref, back_ref)

    for t in range(TOKENS // 128):
        lanes = slice(t * 128, (t + 1) * 128)
        pre = pre_ref[:, lanes]
        slope = jnp.where(pre > 0.0, back_ref[:, lanes], 0.0)
        act = jnp.maximum(pre, 0.0)
        ids = id_ref[:, lanes]
        key = jnp.where(ids >= 0, key_of(ids), -1.0)
        keys, slopes, acts = [], [], []
        for j in range(SLOTS):
            row = slice(j, j + 1)
            keys.append(jnp.broadcast_to(key[row, :], (16, 128)).astype(BF16))
            slopes.append(jnp.broadcast_to(slope[row, :], (16, 128)).astype(BF16))
            acts.append(jnp.broadcast_to(act[row, :], (16, 128)).astype(BF16))
        for r in range(feats // 16):
            lines = slice(r * 16, (r + 1) * 16)
            base = base_ref[lines, :]
            s_acc = jnp.zeros((16, 128), BF16)
            a_acc = jnp.zeros((16, 128), BF16)
            for j in range(SLOTS):
                hit = keys[j] == base
                s_acc = jnp.where(hit, slopes[j], s_acc)
                a_acc = jnp.where(hit, acts[j], a_acc)
            st_ref[lines, lanes] = s_acc
            at_ref[lines, lanes] = a_acc
    ge_ref[...] = jnp.dot(st_ref[...], x_ref[...], preferred_element_type=F32).astype(BF16)
    gd_ref[...] = jnp.dot(at_ref[...], r_ref[...], preferred_element_type=F32).astype(BF16)


def grads(ids, pre, back, base, x, r, feats=1024):
    slots = pl.BlockSpec((SLOTS, TOKENS), lambda i: (0, 0))
    whole = pl.BlockSpec((TOKENS, COLS), lambda i: (0, 0))
    out = pl.BlockSpec((feats, COLS), lambda i: (i, 0))
    return pl.pallas_call(
        grad_kernel,
        grid=(FEATS // feats,),
        in_specs=[slots, slots, slots, pl.BlockSpec((feats, 128), lambda i: (i, 0)), whole, whole],
        out_specs=[out, out, pl.BlockSpec((FEATS // 128, 128), lambda i: (0, 0))],
        out_shape=[jax.ShapeDtypeStruct((FEATS, COLS), BF16)] * 2
        + [jax.ShapeDtypeStruct((FEATS // 128, 128), F32)],
        scratch_shapes=[pltpu.VMEM((feats, TOKENS), BF16)] * 2,
        compiler_params=pltpu.CompilerParams(vmem_limit_bytes=VMEM_LIMIT),
        name="grads",
    )(ids, pre, back, base, x, r)


def bias_grads(id_ref, pre_ref, back_ref):
    total = jnp.zeros((FEATS // 128, 256), F32)
    pairs = (((1,), (1,)), ((), ()))
    ids = id_ref[...]
    high, low = ids >> 7, ids & 127
    slope = jnp.where(pre_ref[...] > 0.0, back_ref[...], 0.0)
    top = slope.astype(BF16).astype(F32)
    rest = slope - top
    lines = lax.broadcasted_iota(jnp.int32, (FEATS // 128, TOKENS), 0)
    lines128 = lax.broadcasted_iota(jnp.int32, (128, TOKENS), 0)
    for j in range(SLOTS):
        row = slice(j, j + 1)
        one = jnp.where(high[row, :] == lines, 1.0, 0.0).astype(BF16)
        hit = low[row, :] == lines128
        table = [jnp.where(hit, value[row, :], 0.0).astype(BF16) for value in (top, rest)]
        table = jnp.concatenate(table, axis=0)
        total += lax.dot_general(one, table, pairs, preferred_element_type=F32)
    return total[:, :128] + total[:, 128:]


def shards(inputs, target, feature_slots, w_enc, b_enc, w_dec, b_dec, w_skip):
    ids = feature_slots[:, 0, :].T
    recon, all_x, all_r, pre, back, base, grad_skip, grad_bdec = step(
        inputs, ids, w_enc, b_enc.reshape(FEATS // 128, 128), w_dec, w_skip, target, b_dec[None, :]
    )
    grad_enc, grad_dec, grad_benc = grads(ids, pre, back, base, all_x, all_r)
    return recon, grad_enc, grad_dec, grad_benc.reshape(-1), grad_bdec.reshape(-1), grad_skip


def solution(mesh):
    in_specs = (
        P("seq", "tp"),
        P("seq", "tp"),
        P(None, "seq", None),
        P("seq", "tp"),
        P("seq"),
        P("seq", "tp"),
        P("tp"),
        P("seq", "tp"),
    )
    out_specs = (P("seq", "tp"), P("seq", "tp"), P("seq", "tp"), P("seq"), P("tp"), P("seq", "tp"))
    return jax.shard_map(shards, mesh=mesh, in_specs=in_specs, out_specs=out_specs, check_vma=False)
```

```python
import functools

import jax
import jax.numpy as jnp
from jax import lax
from jax.experimental import pallas as pl
from jax.experimental.pallas import tpu as pltpu
from jax.sharding import PartitionSpec as P

MESH = pl.DeviceIdType.MESH
BF16 = jnp.bfloat16
F32 = jnp.float32
VMEM_LIMIT = 56 << 20

N_SEQ = 16
N_TP = 8
ROWS = 128
TOKENS = 2048
COLS = 512
FEATS = 4096
SKIP = 256
SLOTS = 8


class Place:
    def __init__(self):
        self.s = lax.axis_index("seq")
        self.p = lax.axis_index("tp")
        s, p = self.s, self.p
        self.c = lax.rem(s, 2)
        self.y = lax.rem(lax.div(s, 2), 4)
        self.zh = lax.div(s, 8)
        self.x = lax.rem(p, 4)
        self.zl = lax.div(p, 4)
        self.mate = (s + 1 - 2 * self.c, p)
        self.up = (self.seq(0, 1), p)
        self.down = (self.seq(0, 3), p)
        self.far = (self.seq(1, 0), p)
        self.right = (s, self.tp(0, 1))
        self.left = (s, self.tp(0, 3))
        self.side = (s, self.tp(1, 0))

    def seq(self, b, dy, other_core=False):
        zh = 1 - self.zh if b else self.zh
        c = 1 - self.c if other_core else self.c
        return (zh * 4 + lax.rem(self.y + dy, 4)) * 2 + c

    def tp(self, b, dx):
        zl = 1 - self.zl if b else self.zl
        return zl * 4 + lax.rem(self.x + dx, 4)


def greet(devices):
    barrier = pltpu.get_barrier_semaphore()
    for dev in devices:
        pl.semaphore_signal(barrier, inc=1, device_id=dev, device_id_type=MESH)
    pl.semaphore_wait(barrier, len(devices))


class Sender:
    def __init__(self, send, recv, here):
        self.send, self.recv, self.here = send, recv, here

    def copy(self, i, src, dst, dev):
        return pltpu.make_async_remote_copy(
            src_ref=src, dst_ref=dst, send_sem=self.send.at[i], recv_sem=self.recv.at[i],
            device_id=dev, device_id_type=MESH,
        )

    def start(self, i, src, dst, dev):
        self.copy(i, src, dst, dev).start()

    def wait(self, i, dst):
        self.copy(i, dst, dst, self.here).wait_recv()

    def sent(self, i, like):
        self.copy(i, like, like, self.here).wait_send()


def choose(k, values):
    out = values[0]
    for i, v in enumerate(values[1:], 1):
        out = jnp.where(k == i, v, out)
    return out


def seq_rows(q, half=None):
    if half is None:
        return pl.ds(pl.multiple_of(q * ROWS, ROWS), ROWS)
    return pl.ds(pl.multiple_of(q * ROWS + half * (ROWS // 2), ROWS // 2), ROWS // 2)


def key_of(number):
    value = (128 + (number & 127)).astype(F32)
    for bit in range(5):
        value = value * jnp.where((number & (128 << bit)) != 0, float(2 ** (2**bit)), 1.0)
    return value


PAIR = 2 * ROWS
PICK_ORDER = (
    ((0, 0, False), (0, 0, True)),
    ((0, 3, False), (0, 1, False)),
    ((0, 3, True), (0, 1, True)),
    ((1, 0, False), (1, 0, True)),
    ((0, 2, False), (0, 2, True)),
    ((1, 3, False), (1, 1, False)),
    ((1, 3, True), (1, 1, True)),
    ((1, 2, False), (1, 2, True)),
)
SEQ_KINDS = 19
HALVES = (2, 3, 6, 7, 12, 13, 17, 18)


def pick_slots(rows, w_ref, ids, bias):
    width = 256
    accs = [[jnp.zeros((8, 128), F32)] * SLOTS for _ in range(2)]
    for c in range(FEATS // width):
        lines = slice(c * width, (c + 1) * width)
        dots = lax.dot_general(
            w_ref[lines, :], rows, (((1,), (1,)), ((), ())), preferred_element_type=F32
        )
        for t in range(2):
            part = dots[:, t * 128 : (t + 1) * 128]
            if bias is not None:
                part = part + bias[lines, :]
            accs[t] = [
                pick_row(part, ids[j : j + 1, t * 128 : (t + 1) * 128], c, accs[t][j])
                for j in range(SLOTS)
            ]
    line = lax.broadcasted_iota(jnp.int32, (8, 128), 0)
    out = []
    for j in range(SLOTS):
        both = []
        for t in range(2):
            hit = line == (ids[j : j + 1, t * 128 : (t + 1) * 128] & 7)
            both.append(jnp.sum(jnp.where(hit, accs[t][j], 0.0), axis=0, keepdims=True))
        out.append(jnp.concatenate(both, axis=1))
    return jnp.concatenate(out, axis=0)


def pick_row(dots, row, c, acc):
    def narrow(tree):
        while tree.shape[0] > 8:
            half = tree.shape[0] // 2
            upper = jnp.broadcast_to((row & half) != 0, (half, 128))
            tree = jnp.where(upper, tree[half:], tree[:half])
        return tree

    tree = [narrow(dots[64 * i : 64 * (i + 1)]) for i in range(dots.shape[0] // 64)]
    bit = 64
    while len(tree) > 1:
        upper = jnp.broadcast_to((row & bit) != 0, (8, 128))
        tree = [jnp.where(upper, b, a) for a, b in zip(tree[::2], tree[1::2])]
        bit *= 2
    return jnp.where(jnp.broadcast_to((row >> 8) == c, (8, 128)), tree[0], acc)


def gather_and_pick(at, net, pnet, own, rows_ref, w_ref, id_ref, bias, parts, keep, extra):
    def blk(b, dy, half=None, other=False):
        return rows_ref.at[seq_rows(at.seq(b, dy, other), half)]

    mine = rows_ref.at[seq_rows(at.s)]
    net.start(9, own, mine, at.mate)
    net.start(8, own, mine, at.far)
    net.start(0, own, mine, at.up)
    net.start(1, own, mine, at.down)
    extra(0)
    keep()
    net.wait(9, blk(0, 0, None, True))

    def ring(b):
        k, m = 4 * b, 9 + 5 * b
        net.wait(k, blk(b, 3))
        net.start(k + 2, blk(b, 3, 0), blk(b, 3, 0), at.up)
        net.start(m + 1, blk(b, 3), blk(b, 3), at.mate)
        net.wait(k + 1, blk(b, 1))
        net.start(k + 3, blk(b, 1, 1), blk(b, 1, 1), at.down)
        net.start(m + 2, blk(b, 1), blk(b, 1), at.mate)

    def last(b):
        k, m = 4 * b, 9 + 5 * b
        net.wait(k + 2, blk(b, 2, 0))
        net.start(m + 3, blk(b, 2, 0), blk(b, 2, 0), at.mate)
        net.wait(k + 3, blk(b, 2, 1))
        net.start(m + 4, blk(b, 2, 1), blk(b, 2, 1), at.mate)

    def step(i):
        if i == 1:
            ring(0)
        if i == 2:
            net.wait(8, blk(1, 0))
            net.start(4, blk(1, 0), blk(1, 0), at.up)
            net.start(5, blk(1, 0), blk(1, 0), at.down)
            net.start(14, blk(1, 0), blk(1, 0), at.mate)
            net.wait(10, blk(0, 3, None, True))
            net.wait(11, blk(0, 1, None, True))
        if i == 3:
            last(0)
            net.wait(14, blk(1, 0, None, True))
        if i == 4:
            ring(1)
            net.wait(12, blk(0, 2, 0, True))
            net.wait(13, blk(0, 2, 1, True))
        if i == 6:
            last(1)
            net.wait(15, blk(1, 3, None, True))
            net.wait(16, blk(1, 1, None, True))
        if i == 7:
            net.wait(17, blk(1, 2, 0, True))
            net.wait(18, blk(1, 2, 1, True))
        extra(i)

    def body(k, carry):
        for i in range(1, 8):
            pl.when(k == i)(functools.partial(step, i))
        one, two = blocks_of(at, k)
        rows = jnp.concatenate([rows_ref[one, :], rows_ref[two, :]], axis=0)
        ids = jnp.concatenate([id_ref[:, one], id_ref[:, two]], axis=1)
        parts[k, at.p] = pick_slots(rows, w_ref, ids, bias)
        for d in range(1, N_TP):
            here = parts.at[k, at.p]
            pnet.start((k, d), here, here, (at.s, lax.rem(at.p + d, N_TP)))
        return carry

    lax.fori_loop(0, 8, body, 0)


def blocks_of(at, k):
    return [seq_rows(choose(k, [at.seq(*both[i]) for both in PICK_ORDER])) for i in (0, 1)]


def add_up(at, pnet, parts, out_ref, k):
    for d in range(1, N_TP):
        pnet.wait((k, d), parts.at[k, lax.rem(at.p + N_TP - d, N_TP)])
    total = parts[k, 0]
    for q in range(1, N_TP):
        total = total + parts[k, q]
    one, two = blocks_of(at, k)
    out_ref[:, one] = total[:, :ROWS]
    out_ref[:, two] = total[:, ROWS:]


def all_sent(at, net, pnet, rows_ref, parts):
    for i in range(SEQ_KINDS):
        net.sent(i, rows_ref.at[pl.ds(0, ROWS // 2 if i in HALVES else ROWS)])

    def done(k, carry):
        for d in range(1, N_TP):
            pnet.sent((k, d), parts.at[k, at.p])
        return carry

    lax.fori_loop(0, 8, done, 0)


SUM_ORDER = ((0, 2), (1, 2), (1, 1), (1, 3), (1, 0), (0, 1), (0, 3), (0, 0))
NEEDED = (4, 7, 5, 3, 1, 2, 0)
SLAB = 32


class Sender2(Sender):
    def copy(self, i, src, dst, dev):
        return pltpu.make_async_remote_copy(
            src_ref=src, dst_ref=dst, send_sem=self.send.at[i[0], i[1]],
            recv_sem=self.recv.at[i[0], i[1]], device_id=dev, device_id_type=MESH,
        )


def step_kernel(
    x_ref, id_ref, we_hbm, b_ref, wd_hbm, ws_ref, target, dec_bias,
    recon, x_hbm, r_hbm, pre_ref, back_ref, col_hbm, skip_grad, bias_grad,
    we_ref, wd_ref, all_ref, res_ref, skip_ref, base_row, base_col, bias, enc_parts, back_parts,
    table, turned, part, mrecv, out_buf, half_in, full_in, far_out, far_in, res,
    send, recv, psend, precv, send2, recv2, msend, mrcv, ysend, yrcv, send3, recv3, psend3, precv3,
    local,
):
    at = Place()
    here = (at.s, at.p)
    load = pltpu.make_async_copy(we_hbm, we_ref, local.at[0])
    load.start()
    own = pltpu.make_async_copy(x_ref, all_ref.at[seq_rows(at.s)], local.at[1])
    own.start()
    load_dec = pltpu.make_async_copy(wd_hbm, wd_ref, local.at[3])
    load_dec.start()

    half_p = lax.div(at.s, 2)
    stay = half_p == at.p
    peers = [(at.s, lax.rem(at.p + d, N_TP)) for d in range(1, N_TP)]
    same, cross = (2 * at.p + at.c, half_p), (2 * at.p + 1 - at.c, half_p)
    around = [at.mate, at.up, at.down, at.far, cross] + peers
    barrier = pltpu.get_barrier_semaphore()
    for dev in around:
        pl.semaphore_signal(barrier, inc=1, device_id=dev, device_id_type=MESH)

    @pl.when(jnp.logical_not(stay))
    def _():
        pl.semaphore_signal(barrier, inc=1, device_id=same, device_id_type=MESH)

    across = (128 + lax.broadcasted_iota(jnp.int32, (SLAB, 128), 1)).astype(F32)
    below = (128 + lax.broadcasted_iota(jnp.int32, (128, 128), 0)).astype(F32)
    first = lax.axis_index("tp") == 0
    for g in range(FEATS // 128):
        base_row[:, g * 128 : (g + 1) * 128] = (across * float(2**g)).astype(BF16)
        base_col[g * 128 : (g + 1) * 128, :] = (below * float(2**g)).astype(BF16)
        row = jnp.where(first, b_ref[g : g + 1, :], 0.0)
        bias[g * 128 : (g + 1) * 128, :] = jnp.broadcast_to(row, (128, 128)).T
    pl.semaphore_wait(barrier, len(around) + 1 - stay.astype(jnp.int32))

    net, pnet, net2 = Sender(send, recv, here), Sender2(psend, precv, here), Sender(send2, recv2, here)

    def columns(h):
        return x_ref.at[:, pl.ds(pl.multiple_of(h * SKIP, SKIP), SKIP)]

    land = skip_ref.at[seq_rows(at.s)]
    inside = pltpu.make_async_copy(columns(at.c), land, local.at[2])

    def piece(b, dx, half=None):
        q = at.tp(b, dx)
        if half is None:
            return skip_ref.at[pl.ds(pl.multiple_of(q * 256, 256), 256)]
        return skip_ref.at[pl.ds(pl.multiple_of(q * 256 + half * 128, 128), 128)]

    def ring(b):
        k = 2 + 4 * b
        net2.wait(k, piece(b, 3))
        net2.start(k + 2, piece(b, 3, 0), piece(b, 3, 0), at.right)
        net2.wait(k + 1, piece(b, 1))
        net2.start(k + 3, piece(b, 1, 1), piece(b, 1, 1), at.left)

    def extra(i):
        if i == 0:
            net2.start(1, columns(1 - at.c), land, cross)

            @pl.when(jnp.logical_not(stay))
            def _():
                net2.start(0, columns(at.c), land, same)

            @pl.when(stay)
            def _():
                inside.start()

        if i == 1:
            net2.wait(1, skip_ref.at[seq_rows(2 * at.p + 1 - at.c)])

            @pl.when(jnp.logical_not(stay))
            def _():
                net2.wait(0, skip_ref.at[seq_rows(2 * at.p + at.c)])

            @pl.when(stay)
            def _():
                pltpu.make_async_copy(columns(at.c), land, local.at[2]).wait()

            net2.start(10, piece(0, 0), piece(0, 0), at.side)
            net2.start(2, piece(0, 0), piece(0, 0), at.right)
            net2.start(3, piece(0, 0), piece(0, 0), at.left)
        if i == 3:
            net2.wait(10, piece(1, 0))
            net2.start(6, piece(1, 0), piece(1, 0), at.right)
            net2.start(7, piece(1, 0), piece(1, 0), at.left)
            ring(0)
        if i == 5:
            ring(1)
        if i == 8:
            for b in (0, 1):
                net2.wait(4 + 4 * b, piece(b, 2, 0))
                net2.wait(5 + 4 * b, piece(b, 2, 1))

    def keep():
        load.wait()
        own.wait()

    gather_and_pick(at, net, pnet, x_ref, all_ref, we_ref, id_ref, bias, enc_parts, keep, extra)
    extra(8)
    out_x = pltpu.make_async_copy(all_ref, x_hbm, local.at[4])
    out_x.start()
    out_col = pltpu.make_async_copy(base_col, col_hbm, local.at[5])
    out_col.start()
    load_dec.wait()

    mnet, ynet = Sender(msend, mrcv, here), Sender(ysend, yrcv, here)
    H = ROWS // 2

    def pair(k, half=None):
        b, dy = SUM_ORDER[k]
        rows = seq_rows(at.seq(b, dy), half)
        mine = slice(0, ROWS) if half is None else slice(half * H, (half + 1) * H)
        return part[rows, :] + mrecv[k, mine, :]

    def opposite(i):
        k = SUM_ORDER.index((1 - i, 2))
        mnet.wait(k, mrecv.at[k])
        out_buf[3 * i] = pair(k).astype(BF16)
        ynet.start(4 * i, out_buf.at[3 * i, pl.ds(0, H)], half_in.at[2 * i], at.up)
        ynet.start(4 * i + 1, out_buf.at[3 * i, pl.ds(H, H)], half_in.at[2 * i + 1], at.down)

    def upward(i):
        k = SUM_ORDER.index((1 - i, 1))
        mnet.wait(k, mrecv.at[k])
        out_buf[3 * i + 1, H:, :] = pair(k, 1).astype(BF16)
        ynet.wait(4 * i, half_in.at[2 * i])
        out_buf[3 * i + 1, :H, :] = (pair(k, 0) + half_in[2 * i].astype(F32)).astype(BF16)
        ynet.start(4 * i + 2, out_buf.at[3 * i + 1], full_in.at[2 * i], at.up)

    def downward(i):
        k = SUM_ORDER.index((1 - i, 3))
        mnet.wait(k, mrecv.at[k])
        out_buf[3 * i + 2, :H, :] = pair(k, 0).astype(BF16)
        ynet.wait(4 * i + 1, half_in.at[2 * i + 1])
        out_buf[3 * i + 2, H:, :] = (pair(k, 1) + half_in[2 * i + 1].astype(F32)).astype(BF16)
        ynet.start(4 * i + 3, out_buf.at[3 * i + 2], full_in.at[2 * i + 1], at.down)

    def here_sum(i):
        k = SUM_ORDER.index((1 - i, 0))
        mnet.wait(k, mrecv.at[k])
        ynet.wait(4 * i + 2, full_in.at[2 * i])
        ynet.wait(4 * i + 3, full_in.at[2 * i + 1])
        return pair(k) + full_in[2 * i].astype(F32) + full_in[2 * i + 1].astype(F32)

    def step(i):
        if i == 1:
            opposite(1)
        if i == 2:
            opposite(0)
        if i == 3:
            upward(0)
        if i == 4:
            downward(0)
        if i == 6:
            far_out[...] = here_sum(0)
            ynet.start(8, far_out, far_in, at.far)
            upward(1)
        if i == 7:
            downward(1)

    filler = jnp.zeros((128 - 2 * SLOTS, 128), F32)

    def body(k, carry):

        @pl.when(k < 7)
        def _():
            add_up(at, pnet, enc_parts, pre_ref, choose(k, NEEDED))

        @pl.when(k == 2)
        def _():
            add_up(at, pnet, enc_parts, pre_ref, 6)

        q = choose(k, [lax.div(at.seq(b, dy), 2) for b, dy in SUM_ORDER])
        first = pl.multiple_of(q * PAIR, PAIR)
        for t in range(2):
            lanes = pl.ds(pl.multiple_of(first + t * 128, 128), 128)
            ids = id_ref[:, lanes]
            act = jnp.maximum(pre_ref[:, lanes], 0.0)
            key = jnp.where(ids >= 0, key_of(ids), -1.0)
            turned[t * 128 : (t + 1) * 128, :] = jnp.concatenate([act, key, filler], axis=0).T

        def slab(r, carry2):
            line = pl.ds(pl.multiple_of(r * SLAB, SLAB), SLAB)
            both = turned[line, :]
            keys, vals = [], []
            for j in range(SLOTS):
                keys.append(jnp.broadcast_to(both[:, SLOTS + j : SLOTS + j + 1], (SLAB, 128)).astype(BF16))
                vals.append(jnp.broadcast_to(both[:, j : j + 1], (SLAB, 128)).astype(BF16))
            for g in range(FEATS // 128):
                spot = base_row[:, g * 128 : (g + 1) * 128]
                acc = jnp.zeros((SLAB, 128), BF16)
                for j in range(SLOTS):
                    acc = jnp.where(keys[j] == spot, vals[j], acc)
                table[line, g * 128 : (g + 1) * 128] = acc
            return carry2

        lax.fori_loop(0, PAIR // SLAB, slab, 0)
        for i in range(1, 8):
            pl.when(k == i)(functools.partial(step, i))
        rows = pl.ds(first, PAIR)
        part[rows, :] = jnp.dot(table[...], wd_ref[...], preferred_element_type=F32) + jnp.dot(
            skip_ref[rows, :], ws_ref[...], preferred_element_type=F32
        )
        mnet.start(k, part.at[seq_rows(2 * q + 1 - at.c)], mrecv.at[k], at.mate)
        return carry

    lax.fori_loop(0, 8, body, 0)
    total = here_sum(1) + dec_bias[...]
    ynet.wait(8, far_in)
    total = total + far_in[...]
    recon[...] = total.astype(BF16)
    res[...] = (total - target[...].astype(F32)).astype(BF16)
    own = pltpu.make_async_copy(res, res_ref.at[seq_rows(at.s)], local.at[6])
    own.start()
    net3, pnet3 = Sender(send3, recv3, here), Sender2(psend3, precv3, here)
    gather_and_pick(
        at, net3, pnet3, res, res_ref, wd_ref, id_ref, None, back_parts, own.wait, lambda i: None
    )
    out_r = pltpu.make_async_copy(res_ref, r_hbm, local.at[7])
    out_r.start()
    skip_grad[...] = lax.dot_general(
        skip_ref[...], res_ref[...], (((0,), (0,)), ((), ())), preferred_element_type=F32
    ).astype(BF16)
    ones = jnp.ones((8, TOKENS), BF16)
    bias_grad[...] = jnp.dot(ones, res_ref[...], preferred_element_type=F32)[:1]

    def add_back(k, carry):
        add_up(at, pnet3, back_parts, back_ref, k)
        return carry

    lax.fori_loop(0, 8, add_back, 0)
    all_sent(at, net, pnet, all_ref, enc_parts)
    all_sent(at, net3, pnet3, res_ref, back_parts)

    @pl.when(jnp.logical_not(stay))
    def _():
        net2.sent(0, land)

    net2.sent(1, land)
    for i in range(2, 11):
        net2.sent(i, skip_ref.at[pl.ds(0, 128 if i in (4, 5, 8, 9) else 256)])
    for k in range(8):
        mnet.sent(k, mrecv.at[k])
    for i in (0, 1):
        ynet.sent(4 * i, half_in.at[0])
        ynet.sent(4 * i + 1, half_in.at[0])
        ynet.sent(4 * i + 2, full_in.at[0])
        ynet.sent(4 * i + 3, full_in.at[0])
    ynet.sent(8, far_out)
    out_x.wait()
    out_col.wait()
    out_r.wait()


def step(x, ids, w_enc, b_enc, w_dec, w_skip, target, b_dec):
    vm = pl.BlockSpec(memory_space=pltpu.VMEM)
    hbm = pl.BlockSpec(memory_space=pl.ANY)
    dma = pltpu.SemaphoreType.DMA
    return pl.pallas_call(
        step_kernel,
        out_shape=[
            jax.ShapeDtypeStruct((ROWS, COLS), BF16),
            jax.ShapeDtypeStruct((TOKENS, COLS), BF16),
            jax.ShapeDtypeStruct((TOKENS, COLS), BF16),
            jax.ShapeDtypeStruct((SLOTS, TOKENS), F32),
            jax.ShapeDtypeStruct((SLOTS, TOKENS), F32),
            jax.ShapeDtypeStruct((FEATS, 128), BF16),
            jax.ShapeDtypeStruct((SKIP, COLS), BF16),
            jax.ShapeDtypeStruct((1, COLS), F32),
        ],
        in_specs=[hbm, vm, hbm, vm, hbm, vm, vm, vm],
        out_specs=[vm, hbm, hbm, vm, vm, hbm, vm, vm],
        scratch_shapes=[
            pltpu.VMEM((FEATS, COLS), BF16),
            pltpu.VMEM((FEATS, COLS), BF16),
            pltpu.VMEM((TOKENS, COLS), BF16),
            pltpu.VMEM((TOKENS, COLS), BF16),
            pltpu.VMEM((TOKENS, SKIP), BF16),
            pltpu.VMEM((SLAB, FEATS), BF16),
            pltpu.VMEM((FEATS, 128), BF16),
            pltpu.VMEM((FEATS, 128), F32),
            pltpu.VMEM((8, N_TP, SLOTS, PAIR), F32),
            pltpu.VMEM((8, N_TP, SLOTS, PAIR), F32),
            pltpu.VMEM((PAIR, FEATS), BF16),
            pltpu.VMEM((PAIR, 128), F32),
            pltpu.VMEM((TOKENS, COLS), F32),
            pltpu.VMEM((8, ROWS, COLS), F32),
            pltpu.VMEM((6, ROWS, COLS), BF16),
            pltpu.VMEM((4, ROWS // 2, COLS), BF16),
            pltpu.VMEM((4, ROWS, COLS), BF16),
            pltpu.VMEM((ROWS, COLS), F32),
            pltpu.VMEM((ROWS, COLS), F32),
            pltpu.VMEM((ROWS, COLS), BF16),
            dma((SEQ_KINDS,)), dma((SEQ_KINDS,)), dma((8, N_TP)), dma((8, N_TP)),
            dma((11,)), dma((11,)), dma((8,)), dma((8,)), dma((9,)), dma((9,)),
            dma((SEQ_KINDS,)), dma((SEQ_KINDS,)), dma((8, N_TP)), dma((8, N_TP)), dma((8,)),
        ],
        compiler_params=pltpu.CompilerParams(
            collective_id=0, has_side_effects=True, vmem_limit_bytes=VMEM_LIMIT
        ),
        name="step",
    )(x, ids, w_enc, b_enc, w_dec, w_skip, target, b_dec)


def grad_kernel(
    id_ref, pre_ref, back_ref, base_ref, x_ref, r_ref, c_in, gs_in, bd_in,
    ge_ref, gd_ref, gb_ref, c_ref, gs_ref, bd_ref, st_ref, at_ref
):
    feats = base_ref.shape[0]

    @pl.when(pl.program_id(0) == 0)
    def _():
        gb_ref[...] = bias_grads(id_ref, pre_ref, back_ref)
        c_ref[...] = c_in[...]
        gs_ref[...] = gs_in[...]
        bd_ref[...] = bd_in[...]

    for t in range(TOKENS // 128):
        lanes = slice(t * 128, (t + 1) * 128)
        pre = pre_ref[:, lanes]
        slope = jnp.where(pre > 0.0, back_ref[:, lanes], 0.0)
        act = jnp.maximum(pre, 0.0)
        ids = id_ref[:, lanes]
        key = jnp.where(ids >= 0, key_of(ids), -1.0)
        keys, slopes, acts = [], [], []
        for j in range(SLOTS):
            row = slice(j, j + 1)
            keys.append(jnp.broadcast_to(key[row, :], (16, 128)).astype(BF16))
            slopes.append(jnp.broadcast_to(slope[row, :], (16, 128)).astype(BF16))
            acts.append(jnp.broadcast_to(act[row, :], (16, 128)).astype(BF16))
        for r in range(feats // 16):
            lines = slice(r * 16, (r + 1) * 16)
            base = base_ref[lines, :]
            s_acc = jnp.zeros((16, 128), BF16)
            a_acc = jnp.zeros((16, 128), BF16)
            for j in range(SLOTS):
                hit = keys[j] == base
                s_acc = jnp.where(hit, slopes[j], s_acc)
                a_acc = jnp.where(hit, acts[j], a_acc)
            st_ref[lines, lanes] = s_acc
            at_ref[lines, lanes] = a_acc
    ge_ref[...] = jnp.dot(st_ref[...], x_ref[...], preferred_element_type=F32).astype(BF16)
    gd_ref[...] = jnp.dot(at_ref[...], r_ref[...], preferred_element_type=F32).astype(BF16)


def grads(ids, pre, back, base, x, r, recon, grad_skip, grad_bdec, feats=1024):
    slots = pl.BlockSpec((SLOTS, TOKENS), lambda i: (0, 0))
    whole = pl.BlockSpec((TOKENS, COLS), lambda i: (0, 0))
    out = pl.BlockSpec((feats, COLS), lambda i: (i, 0))
    small = [pl.BlockSpec(v.shape, lambda i: (0, 0)) for v in (recon, grad_skip, grad_bdec)]
    return pl.pallas_call(
        grad_kernel,
        grid=(FEATS // feats,),
        in_specs=[slots, slots, slots, pl.BlockSpec((feats, 128), lambda i: (i, 0)), whole, whole]
        + small,
        out_specs=[out, out, pl.BlockSpec((FEATS // 128, 128), lambda i: (0, 0))] + small,
        out_shape=[jax.ShapeDtypeStruct((FEATS, COLS), BF16)] * 2
        + [jax.ShapeDtypeStruct((FEATS // 128, 128), F32)]
        + [jax.ShapeDtypeStruct(v.shape, v.dtype) for v in (recon, grad_skip, grad_bdec)],
        scratch_shapes=[pltpu.VMEM((feats, TOKENS), BF16)] * 2,
        compiler_params=pltpu.CompilerParams(vmem_limit_bytes=VMEM_LIMIT),
        name="grads",
    )(ids, pre, back, base, x, r, recon, grad_skip, grad_bdec)


def bias_grads(id_ref, pre_ref, back_ref):
    total = jnp.zeros((FEATS // 128, 256), F32)
    pairs = (((1,), (1,)), ((), ()))
    ids = id_ref[...]
    high, low = ids >> 7, ids & 127
    slope = jnp.where(pre_ref[...] > 0.0, back_ref[...], 0.0)
    top = slope.astype(BF16).astype(F32)
    rest = slope - top
    lines = lax.broadcasted_iota(jnp.int32, (FEATS // 128, TOKENS), 0)
    lines128 = lax.broadcasted_iota(jnp.int32, (128, TOKENS), 0)
    for j in range(SLOTS):
        row = slice(j, j + 1)
        one = jnp.where(high[row, :] == lines, 1.0, 0.0).astype(BF16)
        hit = low[row, :] == lines128
        table = [jnp.where(hit, value[row, :], 0.0).astype(BF16) for value in (top, rest)]
        table = jnp.concatenate(table, axis=0)
        total += lax.dot_general(one, table, pairs, preferred_element_type=F32)
    return total[:, :128] + total[:, 128:]


def shards(inputs, target, feature_slots, w_enc, b_enc, w_dec, b_dec, w_skip):
    ids = feature_slots[:, 0, :].T
    recon, all_x, all_r, pre, back, base, grad_skip, grad_bdec = step(
        inputs, ids, w_enc, b_enc.reshape(FEATS // 128, 128), w_dec, w_skip, target, b_dec[None, :]
    )
    grad_enc, grad_dec, grad_benc, recon, grad_skip, grad_bdec = grads(
        ids, pre, back, base, all_x, all_r, recon, grad_skip, grad_bdec
    )
    return recon, grad_enc, grad_dec, grad_benc.reshape(-1), grad_bdec.reshape(-1), grad_skip


def solution(mesh):
    in_specs = (
        P("seq", "tp"),
        P("seq", "tp"),
        P(None, "seq", None),
        P("seq", "tp"),
        P("seq"),
        P("seq", "tp"),
        P("tp"),
        P("seq", "tp"),
    )
    out_specs = (P("seq", "tp"), P("seq", "tp"), P("seq", "tp"), P("seq"), P("tp"), P("seq", "tp"))
    return jax.shard_map(shards, mesh=mesh, in_specs=in_specs, out_specs=out_specs, check_vma=False)
```

```python
import functools

import jax
import jax.numpy as jnp
from jax import lax
from jax.experimental import pallas as pl
from jax.experimental.pallas import tpu as pltpu
from jax.sharding import PartitionSpec as P

MESH = pl.DeviceIdType.MESH
BF16 = jnp.bfloat16
F32 = jnp.float32
VMEM_LIMIT = 56 << 20

N_SEQ = 16
N_TP = 8
ROWS = 128
TOKENS = 2048
COLS = 512
FEATS = 4096
SKIP = 256
SLOTS = 8


class Place:
    def __init__(self):
        self.s = lax.axis_index("seq")
        self.p = lax.axis_index("tp")
        s, p = self.s, self.p
        self.c = lax.rem(s, 2)
        self.y = lax.rem(lax.div(s, 2), 4)
        self.zh = lax.div(s, 8)
        self.x = lax.rem(p, 4)
        self.zl = lax.div(p, 4)
        self.mate = (s + 1 - 2 * self.c, p)
        self.up = (self.seq(0, 1), p)
        self.down = (self.seq(0, 3), p)
        self.far = (self.seq(1, 0), p)
        self.right = (s, self.tp(0, 1))
        self.left = (s, self.tp(0, 3))
        self.side = (s, self.tp(1, 0))

    def seq(self, b, dy, other_core=False):
        zh = 1 - self.zh if b else self.zh
        c = 1 - self.c if other_core else self.c
        return (zh * 4 + lax.rem(self.y + dy, 4)) * 2 + c

    def tp(self, b, dx):
        zl = 1 - self.zl if b else self.zl
        return zl * 4 + lax.rem(self.x + dx, 4)


def greet(devices):
    barrier = pltpu.get_barrier_semaphore()
    for dev in devices:
        pl.semaphore_signal(barrier, inc=1, device_id=dev, device_id_type=MESH)
    pl.semaphore_wait(barrier, len(devices))


class Sender:
    def __init__(self, send, recv, here):
        self.send, self.recv, self.here = send, recv, here

    def copy(self, i, src, dst, dev):
        return pltpu.make_async_remote_copy(
            src_ref=src, dst_ref=dst, send_sem=self.send.at[i], recv_sem=self.recv.at[i],
            device_id=dev, device_id_type=MESH,
        )

    def start(self, i, src, dst, dev):
        self.copy(i, src, dst, dev).start()

    def wait(self, i, dst):
        self.copy(i, dst, dst, self.here).wait_recv()

    def sent(self, i, like):
        self.copy(i, like, like, self.here).wait_send()


def choose(k, values):
    out = values[0]
    for i, v in enumerate(values[1:], 1):
        out = jnp.where(k == i, v, out)
    return out


def seq_rows(q, half=None):
    if half is None:
        return pl.ds(pl.multiple_of(q * ROWS, ROWS), ROWS)
    return pl.ds(pl.multiple_of(q * ROWS + half * (ROWS // 2), ROWS // 2), ROWS // 2)


def key_of(number):
    value = (128 + (number & 127)).astype(F32)
    for bit in range(5):
        value = value * jnp.where((number & (128 << bit)) != 0, float(2 ** (2**bit)), 1.0)
    return value


PAIR = 2 * ROWS
PICK_ORDER = (
    ((0, 0, False), (0, 0, True)),
    ((0, 3, False), (0, 1, False)),
    ((0, 3, True), (0, 1, True)),
    ((1, 0, False), (1, 0, True)),
    ((0, 2, False), (0, 2, True)),
    ((1, 3, False), (1, 1, False)),
    ((1, 3, True), (1, 1, True)),
    ((1, 2, False), (1, 2, True)),
)
SEQ_KINDS = 19
HALVES = (2, 3, 6, 7, 12, 13, 17, 18)


def pick_slots(rows, w_ref, ids, bias):
    width = 256
    accs = [[jnp.zeros((8, 128), F32)] * SLOTS for _ in range(2)]
    for c in range(FEATS // width):
        lines = slice(c * width, (c + 1) * width)
        dots = lax.dot_general(
            w_ref[lines, :], rows, (((1,), (1,)), ((), ())), preferred_element_type=F32
        )
        for t in range(2):
            part = dots[:, t * 128 : (t + 1) * 128]
            if bias is not None:
                part = part + bias[lines, :]
            accs[t] = [
                pick_row(part, ids[j : j + 1, t * 128 : (t + 1) * 128], c, accs[t][j])
                for j in range(SLOTS)
            ]
    line = lax.broadcasted_iota(jnp.int32, (8, 128), 0)
    out = []
    for j in range(SLOTS):
        both = []
        for t in range(2):
            hit = line == (ids[j : j + 1, t * 128 : (t + 1) * 128] & 7)
            both.append(jnp.sum(jnp.where(hit, accs[t][j], 0.0), axis=0, keepdims=True))
        out.append(jnp.concatenate(both, axis=1))
    return jnp.concatenate(out, axis=0)


def pick_row(dots, row, c, acc):
    def narrow(tree):
        while tree.shape[0] > 8:
            half = tree.shape[0] // 2
            upper = jnp.broadcast_to((row & half) != 0, (half, 128))
            tree = jnp.where(upper, tree[half:], tree[:half])
        return tree

    tree = [narrow(dots[64 * i : 64 * (i + 1)]) for i in range(dots.shape[0] // 64)]
    bit = 64
    while len(tree) > 1:
        upper = jnp.broadcast_to((row & bit) != 0, (8, 128))
        tree = [jnp.where(upper, b, a) for a, b in zip(tree[::2], tree[1::2])]
        bit *= 2
    return jnp.where(jnp.broadcast_to((row >> 8) == c, (8, 128)), tree[0], acc)


def gather_and_pick(at, net, pnet, own, rows_ref, w_ref, id_ref, bias, parts, keep, extra):
    def blk(b, dy, half=None, other=False):
        return rows_ref.at[seq_rows(at.seq(b, dy, other), half)]

    mine = rows_ref.at[seq_rows(at.s)]
    net.start(9, own, mine, at.mate)
    net.start(8, own, mine, at.far)
    net.start(0, own, mine, at.up)
    net.start(1, own, mine, at.down)
    extra(0)
    keep()
    net.wait(9, blk(0, 0, None, True))

    def ring(b):
        k, m = 4 * b, 9 + 5 * b
        net.wait(k, blk(b, 3))
        net.start(k + 2, blk(b, 3, 0), blk(b, 3, 0), at.up)
        net.start(m + 1, blk(b, 3), blk(b, 3), at.mate)
        net.wait(k + 1, blk(b, 1))
        net.start(k + 3, blk(b, 1, 1), blk(b, 1, 1), at.down)
        net.start(m + 2, blk(b, 1), blk(b, 1), at.mate)

    def last(b):
        k, m = 4 * b, 9 + 5 * b
        net.wait(k + 2, blk(b, 2, 0))
        net.start(m + 3, blk(b, 2, 0), blk(b, 2, 0), at.mate)
        net.wait(k + 3, blk(b, 2, 1))
        net.start(m + 4, blk(b, 2, 1), blk(b, 2, 1), at.mate)

    def step(i):
        if i == 1:
            ring(0)
        if i == 2:
            net.wait(8, blk(1, 0))
            net.start(4, blk(1, 0), blk(1, 0), at.up)
            net.start(5, blk(1, 0), blk(1, 0), at.down)
            net.start(14, blk(1, 0), blk(1, 0), at.mate)
            net.wait(10, blk(0, 3, None, True))
            net.wait(11, blk(0, 1, None, True))
        if i == 3:
            last(0)
            net.wait(14, blk(1, 0, None, True))
        if i == 4:
            ring(1)
            net.wait(12, blk(0, 2, 0, True))
            net.wait(13, blk(0, 2, 1, True))
        if i == 6:
            last(1)
            net.wait(15, blk(1, 3, None, True))
            net.wait(16, blk(1, 1, None, True))
        if i == 7:
            net.wait(17, blk(1, 2, 0, True))
            net.wait(18, blk(1, 2, 1, True))
        extra(i)

    def body(k, carry):
        for i in range(1, 8):
            pl.when(k == i)(functools.partial(step, i))
        one, two = blocks_of(at, k)
        rows = jnp.concatenate([rows_ref[one, :], rows_ref[two, :]], axis=0)
        ids = jnp.concatenate([id_ref[:, one], id_ref[:, two]], axis=1)
        parts[k, at.p] = pick_slots(rows, w_ref, ids, bias)
        for d in range(1, N_TP):
            here = parts.at[k, at.p]
            pnet.start((k, d), here, here, (at.s, lax.rem(at.p + d, N_TP)))
        return carry

    lax.fori_loop(0, 8, body, 0)


def blocks_of(at, k):
    return [seq_rows(choose(k, [at.seq(*both[i]) for both in PICK_ORDER])) for i in (0, 1)]


def add_up(at, pnet, parts, out_ref, k):
    for d in range(1, N_TP):
        pnet.wait((k, d), parts.at[k, lax.rem(at.p + N_TP - d, N_TP)])
    total = parts[k, 0]
    for q in range(1, N_TP):
        total = total + parts[k, q]
    one, two = blocks_of(at, k)
    out_ref[:, one] = total[:, :ROWS]
    out_ref[:, two] = total[:, ROWS:]


def all_sent(at, net, pnet, rows_ref, parts):
    for i in range(SEQ_KINDS):
        net.sent(i, rows_ref.at[pl.ds(0, ROWS // 2 if i in HALVES else ROWS)])

    def done(k, carry):
        for d in range(1, N_TP):
            pnet.sent((k, d), parts.at[k, at.p])
        return carry

    lax.fori_loop(0, 8, done, 0)


SUM_ORDER = ((0, 2), (1, 2), (1, 1), (1, 3), (1, 0), (0, 1), (0, 3), (0, 0))
NEEDED = (4, 7, 5, 3, 1, 2, 0)
SLAB = 32


class Sender2(Sender):
    def copy(self, i, src, dst, dev):
        return pltpu.make_async_remote_copy(
            src_ref=src, dst_ref=dst, send_sem=self.send.at[i[0], i[1]],
            recv_sem=self.recv.at[i[0], i[1]], device_id=dev, device_id_type=MESH,
        )


def step_kernel(
    x_ref, id_ref, we_hbm, b_ref, wd_hbm, ws_ref, target, dec_bias,
    recon, x_hbm, r_hbm, pre_ref, back_ref, col_hbm, skip_grad, bias_grad,
    we_ref, wd_ref, all_ref, res_ref, skip_ref, base_row, base_col, bias, enc_parts, back_parts,
    table, turned, part, mrecv, out_buf, half_in, full_in, far_out, far_in, res,
    send, recv, psend, precv, send2, recv2, msend, mrcv, ysend, yrcv, send3, recv3, psend3, precv3,
    local,
):
    at = Place()
    here = (at.s, at.p)
    load = pltpu.make_async_copy(we_hbm, we_ref, local.at[0])
    load.start()
    own = pltpu.make_async_copy(x_ref, all_ref.at[seq_rows(at.s)], local.at[1])
    own.start()
    load_dec = pltpu.make_async_copy(wd_hbm, wd_ref, local.at[3])
    load_dec.start()

    half_p = lax.div(at.s, 2)
    stay = half_p == at.p
    peers = [(at.s, lax.rem(at.p + d, N_TP)) for d in range(1, N_TP)]
    same, cross = (2 * at.p + at.c, half_p), (2 * at.p + 1 - at.c, half_p)
    around = [at.mate, at.up, at.down, at.far, cross] + peers
    barrier = pltpu.get_barrier_semaphore()
    for dev in around:
        pl.semaphore_signal(barrier, inc=1, device_id=dev, device_id_type=MESH)

    @pl.when(jnp.logical_not(stay))
    def _():
        pl.semaphore_signal(barrier, inc=1, device_id=same, device_id_type=MESH)

    across = (128 + lax.broadcasted_iota(jnp.int32, (SLAB, 128), 1)).astype(F32)
    below = (128 + lax.broadcasted_iota(jnp.int32, (128, 128), 0)).astype(F32)
    first = lax.axis_index("tp") == 0
    for g in range(FEATS // 128):
        base_row[:, g * 128 : (g + 1) * 128] = (across * float(2**g)).astype(BF16)
        base_col[g * 128 : (g + 1) * 128, :] = (below * float(2**g)).astype(BF16)
        row = jnp.where(first, b_ref[g : g + 1, :], 0.0)
        bias[g * 128 : (g + 1) * 128, :] = jnp.broadcast_to(row, (128, 128)).T
    pl.semaphore_wait(barrier, len(around) + 1 - stay.astype(jnp.int32))

    net, pnet, net2 = Sender(send, recv, here), Sender2(psend, precv, here), Sender(send2, recv2, here)

    def columns(h):
        return x_ref.at[:, pl.ds(pl.multiple_of(h * SKIP, SKIP), SKIP)]

    land = skip_ref.at[seq_rows(at.s)]
    inside = pltpu.make_async_copy(columns(at.c), land, local.at[2])

    def piece(b, dx, half=None):
        q = at.tp(b, dx)
        if half is None:
            return skip_ref.at[pl.ds(pl.multiple_of(q * 256, 256), 256)]
        return skip_ref.at[pl.ds(pl.multiple_of(q * 256 + half * 128, 128), 128)]

    def ring(b):
        k = 2 + 4 * b
        net2.wait(k, piece(b, 3))
        net2.start(k + 2, piece(b, 3, 0), piece(b, 3, 0), at.right)
        net2.wait(k + 1, piece(b, 1))
        net2.start(k + 3, piece(b, 1, 1), piece(b, 1, 1), at.left)

    def extra(i):
        if i == 0:
            net2.start(1, columns(1 - at.c), land, cross)

            @pl.when(jnp.logical_not(stay))
            def _():
                net2.start(0, columns(at.c), land, same)

            @pl.when(stay)
            def _():
                inside.start()

        if i == 1:
            net2.wait(1, skip_ref.at[seq_rows(2 * at.p + 1 - at.c)])

            @pl.when(jnp.logical_not(stay))
            def _():
                net2.wait(0, skip_ref.at[seq_rows(2 * at.p + at.c)])

            @pl.when(stay)
            def _():
                pltpu.make_async_copy(columns(at.c), land, local.at[2]).wait()

            net2.start(10, piece(0, 0), piece(0, 0), at.side)
            net2.start(2, piece(0, 0), piece(0, 0), at.right)
            net2.start(3, piece(0, 0), piece(0, 0), at.left)
        if i == 3:
            net2.wait(10, piece(1, 0))
            net2.start(6, piece(1, 0), piece(1, 0), at.right)
            net2.start(7, piece(1, 0), piece(1, 0), at.left)
            ring(0)
        if i == 5:
            ring(1)
        if i == 8:
            for b in (0, 1):
                net2.wait(4 + 4 * b, piece(b, 2, 0))
                net2.wait(5 + 4 * b, piece(b, 2, 1))

    def keep():
        load.wait()
        own.wait()

    gather_and_pick(at, net, pnet, x_ref, all_ref, we_ref, id_ref, bias, enc_parts, keep, extra)
    extra(8)
    out_x = pltpu.make_async_copy(all_ref, x_hbm, local.at[4])
    out_x.start()
    out_col = pltpu.make_async_copy(base_col, col_hbm, local.at[5])
    out_col.start()
    load_dec.wait()

    mnet, ynet = Sender(msend, mrcv, here), Sender(ysend, yrcv, here)
    H = ROWS // 2

    def pair(k, half=None):
        b, dy = SUM_ORDER[k]
        rows = seq_rows(at.seq(b, dy), half)
        mine = slice(0, ROWS) if half is None else slice(half * H, (half + 1) * H)
        return part[rows, :] + mrecv[k, mine, :]

    def opposite(i):
        k = SUM_ORDER.index((1 - i, 2))
        mnet.wait(k, mrecv.at[k])
        out_buf[3 * i] = pair(k).astype(BF16)
        ynet.start(4 * i, out_buf.at[3 * i, pl.ds(0, H)], half_in.at[2 * i], at.up)
        ynet.start(4 * i + 1, out_buf.at[3 * i, pl.ds(H, H)], half_in.at[2 * i + 1], at.down)

    def upward(i):
        k = SUM_ORDER.index((1 - i, 1))
        mnet.wait(k, mrecv.at[k])
        out_buf[3 * i + 1, H:, :] = pair(k, 1).astype(BF16)
        ynet.wait(4 * i, half_in.at[2 * i])
        out_buf[3 * i + 1, :H, :] = (pair(k, 0) + half_in[2 * i].astype(F32)).astype(BF16)
        ynet.start(4 * i + 2, out_buf.at[3 * i + 1], full_in.at[2 * i], at.up)

    def downward(i):
        k = SUM_ORDER.index((1 - i, 3))
        mnet.wait(k, mrecv.at[k])
        out_buf[3 * i + 2, :H, :] = pair(k, 0).astype(BF16)
        ynet.wait(4 * i + 1, half_in.at[2 * i + 1])
        out_buf[3 * i + 2, H:, :] = (pair(k, 1) + half_in[2 * i + 1].astype(F32)).astype(BF16)
        ynet.start(4 * i + 3, out_buf.at[3 * i + 2], full_in.at[2 * i + 1], at.down)

    def here_sum(i):
        k = SUM_ORDER.index((1 - i, 0))
        mnet.wait(k, mrecv.at[k])
        ynet.wait(4 * i + 2, full_in.at[2 * i])
        ynet.wait(4 * i + 3, full_in.at[2 * i + 1])
        return pair(k) + full_in[2 * i].astype(F32) + full_in[2 * i + 1].astype(F32)

    def step(i):
        if i == 1:
            opposite(1)
        if i == 2:
            opposite(0)
        if i == 3:
            upward(0)
        if i == 4:
            downward(0)
        if i == 6:
            far_out[...] = here_sum(0).astype(BF16)
            ynet.start(8, far_out, far_in, at.far)
            upward(1)
        if i == 7:
            downward(1)

    filler = jnp.zeros((128 - 2 * SLOTS, 128), F32)

    def body(k, carry):

        @pl.when(k < 7)
        def _():
            add_up(at, pnet, enc_parts, pre_ref, choose(k, NEEDED))

        @pl.when(k == 2)
        def _():
            add_up(at, pnet, enc_parts, pre_ref, 6)

        q = choose(k, [lax.div(at.seq(b, dy), 2) for b, dy in SUM_ORDER])
        first = pl.multiple_of(q * PAIR, PAIR)
        for t in range(2):
            lanes = pl.ds(pl.multiple_of(first + t * 128, 128), 128)
            ids = id_ref[:, lanes]
            act = jnp.maximum(pre_ref[:, lanes], 0.0)
            key = jnp.where(ids >= 0, key_of(ids), -1.0)
            turned[t * 128 : (t + 1) * 128, :] = jnp.concatenate([act, key, filler], axis=0).T

        def slab(r, carry2):
            line = pl.ds(pl.multiple_of(r * SLAB, SLAB), SLAB)
            both = turned[line, :]
            keys, vals = [], []
            for j in range(SLOTS):
                keys.append(jnp.broadcast_to(both[:, SLOTS + j : SLOTS + j + 1], (SLAB, 128)).astype(BF16))
                vals.append(jnp.broadcast_to(both[:, j : j + 1], (SLAB, 128)).astype(BF16))
            for g in range(FEATS // 128):
                spot = base_row[:, g * 128 : (g + 1) * 128]
                acc = jnp.zeros((SLAB, 128), BF16)
                for j in range(SLOTS):
                    acc = jnp.where(keys[j] == spot, vals[j], acc)
                table[line, g * 128 : (g + 1) * 128] = acc
            return carry2

        lax.fori_loop(0, PAIR // SLAB, slab, 0)
        for i in range(1, 8):
            pl.when(k == i)(functools.partial(step, i))
        rows = pl.ds(first, PAIR)
        part[rows, :] = jnp.dot(table[...], wd_ref[...], preferred_element_type=F32) + jnp.dot(
            skip_ref[rows, :], ws_ref[...], preferred_element_type=F32
        )
        mnet.start(k, part.at[seq_rows(2 * q + 1 - at.c)], mrecv.at[k], at.mate)
        return carry

    lax.fori_loop(0, 8, body, 0)
    total = here_sum(1) + dec_bias[...]
    ynet.wait(8, far_in)
    total = total + far_in[...].astype(F32)
    recon[...] = total.astype(BF16)
    res[...] = (total - target[...].astype(F32)).astype(BF16)
    own = pltpu.make_async_copy(res, res_ref.at[seq_rows(at.s)], local.at[6])
    own.start()
    net3, pnet3 = Sender(send3, recv3, here), Sender2(psend3, precv3, here)
    gather_and_pick(
        at, net3, pnet3, res, res_ref, wd_ref, id_ref, None, back_parts, own.wait, lambda i: None
    )
    out_r = pltpu.make_async_copy(res_ref, r_hbm, local.at[7])
    out_r.start()
    skip_grad[...] = lax.dot_general(
        skip_ref[...], res_ref[...], (((0,), (0,)), ((), ())), preferred_element_type=F32
    ).astype(BF16)
    ones = jnp.ones((8, TOKENS), BF16)
    bias_grad[...] = jnp.dot(ones, res_ref[...], preferred_element_type=F32)[:1]

    def add_back(k, carry):
        add_up(at, pnet3, back_parts, back_ref, k)
        return carry

    lax.fori_loop(0, 8, add_back, 0)
    all_sent(at, net, pnet, all_ref, enc_parts)
    all_sent(at, net3, pnet3, res_ref, back_parts)

    @pl.when(jnp.logical_not(stay))
    def _():
        net2.sent(0, land)

    net2.sent(1, land)
    for i in range(2, 11):
        net2.sent(i, skip_ref.at[pl.ds(0, 128 if i in (4, 5, 8, 9) else 256)])
    for k in range(8):
        mnet.sent(k, mrecv.at[k])
    for i in (0, 1):
        ynet.sent(4 * i, half_in.at[0])
        ynet.sent(4 * i + 1, half_in.at[0])
        ynet.sent(4 * i + 2, full_in.at[0])
        ynet.sent(4 * i + 3, full_in.at[0])
    ynet.sent(8, far_out)
    out_x.wait()
    out_col.wait()
    out_r.wait()


def step(x, ids, w_enc, b_enc, w_dec, w_skip, target, b_dec):
    vm = pl.BlockSpec(memory_space=pltpu.VMEM)
    hbm = pl.BlockSpec(memory_space=pl.ANY)
    dma = pltpu.SemaphoreType.DMA
    return pl.pallas_call(
        step_kernel,
        out_shape=[
            jax.ShapeDtypeStruct((ROWS, COLS), BF16),
            jax.ShapeDtypeStruct((TOKENS, COLS), BF16),
            jax.ShapeDtypeStruct((TOKENS, COLS), BF16),
            jax.ShapeDtypeStruct((SLOTS, TOKENS), F32),
            jax.ShapeDtypeStruct((SLOTS, TOKENS), F32),
            jax.ShapeDtypeStruct((FEATS, 128), BF16),
            jax.ShapeDtypeStruct((SKIP, COLS), BF16),
            jax.ShapeDtypeStruct((1, COLS), F32),
        ],
        in_specs=[hbm, vm, hbm, vm, hbm, vm, vm, vm],
        out_specs=[vm, hbm, hbm, vm, vm, hbm, vm, vm],
        scratch_shapes=[
            pltpu.VMEM((FEATS, COLS), BF16),
            pltpu.VMEM((FEATS, COLS), BF16),
            pltpu.VMEM((TOKENS, COLS), BF16),
            pltpu.VMEM((TOKENS, COLS), BF16),
            pltpu.VMEM((TOKENS, SKIP), BF16),
            pltpu.VMEM((SLAB, FEATS), BF16),
            pltpu.VMEM((FEATS, 128), BF16),
            pltpu.VMEM((FEATS, 128), F32),
            pltpu.VMEM((8, N_TP, SLOTS, PAIR), F32),
            pltpu.VMEM((8, N_TP, SLOTS, PAIR), F32),
            pltpu.VMEM((PAIR, FEATS), BF16),
            pltpu.VMEM((PAIR, 128), F32),
            pltpu.VMEM((TOKENS, COLS), F32),
            pltpu.VMEM((8, ROWS, COLS), F32),
            pltpu.VMEM((6, ROWS, COLS), BF16),
            pltpu.VMEM((4, ROWS // 2, COLS), BF16),
            pltpu.VMEM((4, ROWS, COLS), BF16),
            pltpu.VMEM((ROWS, COLS), BF16),
            pltpu.VMEM((ROWS, COLS), BF16),
            pltpu.VMEM((ROWS, COLS), BF16),
            dma((SEQ_KINDS,)), dma((SEQ_KINDS,)), dma((8, N_TP)), dma((8, N_TP)),
            dma((11,)), dma((11,)), dma((8,)), dma((8,)), dma((9,)), dma((9,)),
            dma((SEQ_KINDS,)), dma((SEQ_KINDS,)), dma((8, N_TP)), dma((8, N_TP)), dma((8,)),
        ],
        compiler_params=pltpu.CompilerParams(
            collective_id=0, has_side_effects=True, vmem_limit_bytes=VMEM_LIMIT
        ),
        name="step",
    )(x, ids, w_enc, b_enc, w_dec, w_skip, target, b_dec)


def grad_kernel(
    id_ref, pre_ref, back_ref, base_ref, x_ref, r_ref, c_in, gs_in, bd_in,
    ge_ref, gd_ref, gb_ref, c_ref, gs_ref, bd_ref, st_ref, at_ref
):
    feats = base_ref.shape[0]

    @pl.when(pl.program_id(0) == 0)
    def _():
        gb_ref[...] = bias_grads(id_ref, pre_ref, back_ref)
        c_ref[...] = c_in[...]
        gs_ref[...] = gs_in[...]
        bd_ref[...] = bd_in[...]

    for t in range(TOKENS // 128):
        lanes = slice(t * 128, (t + 1) * 128)
        pre = pre_ref[:, lanes]
        slope = jnp.where(pre > 0.0, back_ref[:, lanes], 0.0)
        act = jnp.maximum(pre, 0.0)
        ids = id_ref[:, lanes]
        key = jnp.where(ids >= 0, key_of(ids), -1.0)
        keys, slopes, acts = [], [], []
        for j in range(SLOTS):
            row = slice(j, j + 1)
            keys.append(jnp.broadcast_to(key[row, :], (16, 128)).astype(BF16))
            slopes.append(jnp.broadcast_to(slope[row, :], (16, 128)).astype(BF16))
            acts.append(jnp.broadcast_to(act[row, :], (16, 128)).astype(BF16))
        for r in range(feats // 16):
            lines = slice(r * 16, (r + 1) * 16)
            base = base_ref[lines, :]
            s_acc = jnp.zeros((16, 128), BF16)
            a_acc = jnp.zeros((16, 128), BF16)
            for j in range(SLOTS):
                hit = keys[j] == base
                s_acc = jnp.where(hit, slopes[j], s_acc)
                a_acc = jnp.where(hit, acts[j], a_acc)
            st_ref[lines, lanes] = s_acc
            at_ref[lines, lanes] = a_acc
    ge_ref[...] = jnp.dot(st_ref[...], x_ref[...], preferred_element_type=F32).astype(BF16)
    gd_ref[...] = jnp.dot(at_ref[...], r_ref[...], preferred_element_type=F32).astype(BF16)


def grads(ids, pre, back, base, x, r, recon, grad_skip, grad_bdec, feats=1024):
    slots = pl.BlockSpec((SLOTS, TOKENS), lambda i: (0, 0))
    whole = pl.BlockSpec((TOKENS, COLS), lambda i: (0, 0))
    out = pl.BlockSpec((feats, COLS), lambda i: (i, 0))
    small = [pl.BlockSpec(v.shape, lambda i: (0, 0)) for v in (recon, grad_skip, grad_bdec)]
    return pl.pallas_call(
        grad_kernel,
        grid=(FEATS // feats,),
        in_specs=[slots, slots, slots, pl.BlockSpec((feats, 128), lambda i: (i, 0)), whole, whole]
        + small,
        out_specs=[out, out, pl.BlockSpec((FEATS // 128, 128), lambda i: (0, 0))] + small,
        out_shape=[jax.ShapeDtypeStruct((FEATS, COLS), BF16)] * 2
        + [jax.ShapeDtypeStruct((FEATS // 128, 128), F32)]
        + [jax.ShapeDtypeStruct(v.shape, v.dtype) for v in (recon, grad_skip, grad_bdec)],
        scratch_shapes=[pltpu.VMEM((feats, TOKENS), BF16)] * 2,
        compiler_params=pltpu.CompilerParams(vmem_limit_bytes=VMEM_LIMIT),
        name="grads",
    )(ids, pre, back, base, x, r, recon, grad_skip, grad_bdec)


def bias_grads(id_ref, pre_ref, back_ref):
    total = jnp.zeros((FEATS // 128, 256), F32)
    pairs = (((1,), (1,)), ((), ()))
    ids = id_ref[...]
    high, low = ids >> 7, ids & 127
    slope = jnp.where(pre_ref[...] > 0.0, back_ref[...], 0.0)
    top = slope.astype(BF16).astype(F32)
    rest = slope - top
    lines = lax.broadcasted_iota(jnp.int32, (FEATS // 128, TOKENS), 0)
    lines128 = lax.broadcasted_iota(jnp.int32, (128, TOKENS), 0)
    for j in range(SLOTS):
        row = slice(j, j + 1)
        one = jnp.where(high[row, :] == lines, 1.0, 0.0).astype(BF16)
        hit = low[row, :] == lines128
        table = [jnp.where(hit, value[row, :], 0.0).astype(BF16) for value in (top, rest)]
        table = jnp.concatenate(table, axis=0)
        total += lax.dot_general(one, table, pairs, preferred_element_type=F32)
    return total[:, :128] + total[:, 128:]


def shards(inputs, target, feature_slots, w_enc, b_enc, w_dec, b_dec, w_skip):
    ids = feature_slots[:, 0, :].T
    recon, all_x, all_r, pre, back, base, grad_skip, grad_bdec = step(
        inputs, ids, w_enc, b_enc.reshape(FEATS // 128, 128), w_dec, w_skip, target, b_dec[None, :]
    )
    grad_enc, grad_dec, grad_benc, recon, grad_skip, grad_bdec = grads(
        ids, pre, back, base, all_x, all_r, recon, grad_skip, grad_bdec
    )
    return recon, grad_enc, grad_dec, grad_benc.reshape(-1), grad_bdec.reshape(-1), grad_skip


def solution(mesh):
    in_specs = (
        P("seq", "tp"),
        P("seq", "tp"),
        P(None, "seq", None),
        P("seq", "tp"),
        P("seq"),
        P("seq", "tp"),
        P("tp"),
        P("seq", "tp"),
    )
    out_specs = (P("seq", "tp"), P("seq", "tp"), P("seq", "tp"), P("seq"), P("tp"), P("seq", "tp"))
    return jax.shard_map(shards, mesh=mesh, in_specs=in_specs, out_specs=out_specs, check_vma=False)
```
